32 devices in a mesh: dp: 16 (over z, x, core), tensor: 2 (over y).
Axes of the slice: x: 2, y: 2, z: 4, core: 2. Of those that a mesh axis runs over, the one named last changes fastest.
Arguments:
- tokens: bfloat16 [32768, 768], P(('dp', 'tensor')), may hold values from -6 to 6
- segment: int32 [32768], P('dp'), may hold values from 0 to 16, as said below
- weight_qkv: bfloat16 [3, 768, 768], P(None, 'dp', 'tensor'), may hold values from -0.3125 to 0.3125
- weight_out: bfloat16 [768, 768], P('tensor', 'dp'), may hold values from -0.625 to 0.625
- weight_in: bfloat16 [768, 3072], P('dp', 'tensor'), may hold values from -0.21875 to 0.21875
- weight_down: bfloat16 [3072, 768], P('tensor', 'dp'), may hold values from -0.15625 to 0.15625
- gain_one: bfloat16 [768], P('dp'), may hold values from 0.5 to 1.5
- shift_one: bfloat16 [768], P('dp'), may hold values from -3 to 3
- gain_two: bfloat16 [768], P('dp'), may hold values from 0.5 to 1.5
- shift_two: bfloat16 [768], P('dp'), may hold values from -3 to 3
- cotangent: bfloat16 [32768, 768], P(('dp', 'tensor')), may hold values from -6 to 6
Outputs:
- output: bfloat16 [32768, 768], P(('dp', 'tensor'))
- input_grad: bfloat16 [32768, 768], P(('dp', 'tensor'))
- grad_weight_qkv: float32 [3, 768, 768], P(None, 'dp', 'tensor')
- grad_weight_out: float32 [768, 768], P('tensor', 'dp')
- grad_weight_in: float32 [768, 3072], P('dp', 'tensor')
- grad_weight_down: float32 [3072, 768], P('tensor', 'dp')
- grad_gain_one: float32 [768], P('dp')
- grad_shift_one: float32 [768], P('dp')
- grad_gain_two: float32 [768], P('dp')
- grad_shift_two: float32 [768], P('dp')
The draws below stay inside these ranges and needn't reach their ends.
Inputs may be any that keep to these rules, and one draw needn't show every extreme that they name: `segment`: segment numbers start at 0 in each sequence of 512 consecutive tokens and rise by one at each document's first token; each document has 20 to 200 tokens except the last of a sequence, which may be cut shorter; every sequence holds a document of exactly 200 tokens.
All inputs are finite; a program needn't handle non-finite values.
Results may differ from the reference program's by a relative error of at most 0.02.
Values may be sent and summed in bfloat16 or wider, within the bound.
No kernel may reach another device: no remote copies, remote signals or barrier semaphores. Data moves between devices by JAX's collectives and lax.ppermute only.
A program may use at most 192 MiB of HBM per device.

```python
import math
import jax
import jax.numpy as jnp
from jax import lax

D = 768
HEADS = 12
HDIM = 64
FF = 3072
SEQ = 512
DOC_LO = 20
DOC_HI = 200
TOKENS = 32768


def draw_segment(key, part):
    key = jax.random.fold_in(key, 7)
    seq_count = TOKENS // SEQ
    slot_count = SEQ // DOC_LO + 1
    lengths = jax.random.randint(key, (seq_count, slot_count), DOC_LO, DOC_HI + 1)
    dense_row = jax.random.randint(jax.random.fold_in(key, 2), (), 0, seq_count)
    row_index = jnp.arange(seq_count)[:, None]
    lengths = jnp.where(row_index == dense_row, DOC_LO, lengths)
    chosen = jax.random.randint(jax.random.fold_in(key, 1), (seq_count, 1), 0, 2)
    slot_index = jnp.arange(slot_count)[None, :]
    lengths = jnp.where(slot_index == chosen, DOC_HI, lengths)
    bounds = jnp.cumsum(lengths, axis=1)
    position = jnp.arange(SEQ)[None, :, None]
    numbers = jnp.sum((bounds[:, None, :] <= position).astype(jnp.int32), axis=2)
    return numbers.reshape(TOKENS).astype(jnp.int32)


def with_spikes(values, own_key, source, target, shards_of, factor):
    owner, partner = [(jnp.arange(values.shape[axis_at]) // (values.shape[axis_at] // shards_of)).reshape([-1 if axis == axis_at else 1 for axis in range(values.ndim)]) for axis_at in (source, target)]
    chosen = jax.random.permutation(own_key, shards_of)[partner]
    strong = (owner == chosen) | (owner == (partner + shards_of // 2) % shards_of)
    return jnp.where(strong, factor * values, values)


def block_levels(own_key, extent, pieces, least, high):
    def one(dim, parts):
        steps = jax.random.uniform(jax.random.fold_in(jax.random.fold_in(own_key, 6), dim), (parts,), jnp.float32, least / len(pieces), high / len(pieces))
        return jnp.repeat(jnp.exp(steps), extent[dim] // parts).reshape((-1,) + (1,) * (len(extent) - dim - 1))

    loudness = one(*pieces[0])
    for cut in pieces[1:]:
        loudness = loudness * one(*cut)
    return loudness


def gaussian(stream_key, shape, scale, reach, pieces=(), held_as=jnp.bfloat16):
    values = jax.random.normal(stream_key, shape, jnp.float32) * scale
    if len(pieces) > 0:
        values = block_levels(stream_key, shape, pieces, -0.22, 0.18) * values
    return jnp.clip(values, min=-reach, max=reach).astype(held_as)


def bell_draw_with(stream_key, extent, deviation, bound, split, heavy, kind=jnp.bfloat16):
    values = deviation * jax.random.normal(stream_key, extent, jnp.float32)
    if split:
        values = values * block_levels(stream_key, extent, split, -0.22, 0.18)
    return jnp.clip(with_spikes(values, jax.random.fold_in(stream_key, 3), *heavy), -bound, bound).astype(kind)


def setup_inputs(seed: int = 0) -> dict:
    keys = jax.random.split(jax.random.key(seed), 12)
    return {
        "tokens": bell_draw_with(keys[0], (TOKENS, D), 1.0, 6.0, ((0, 32),), (0, 1, 32, 2.75)),
        "segment": draw_segment(jax.random.fold_in(keys[11], 71), 0),
        "weight_qkv": gaussian(keys[2], (3, D, D), (D // 2) ** -0.5, 0.3125, ((1, 16), (2, 2))),
        "weight_out": gaussian(keys[3], (D, D), (D // 8) ** -0.5, 0.625, ((0, 2), (1, 16))),
        "weight_in": gaussian(keys[4], (D, FF), D ** -0.5, 0.21875, ((0, 16), (1, 2))),
        "weight_down": gaussian(keys[5], (FF, D), (FF // 2) ** -0.5, 0.15625, ((0, 2), (1, 16))),
        "gain_one": jnp.clip(1.0 + 0.1 * jax.random.normal(keys[6], (D,), jnp.float32), 0.5, 1.5).astype(jnp.bfloat16),
        "shift_one": gaussian(keys[7], (D,), 0.5, 3.0, ((0, 16),)),
        "gain_two": jnp.clip(1.0 + 0.1 * jax.random.normal(keys[8], (D,), jnp.float32), 0.5, 1.5).astype(jnp.bfloat16),
        "shift_two": gaussian(keys[9], (D,), 0.5, 3.0, ((0, 16),)),
        "cotangent": bell_draw_with(keys[10], (TOKENS, D), 1.0, 6.0, ((0, 32),), (0, 1, 32, 2.75)),
    }


highest = lax.Precision.HIGHEST
epsilon = 1e-05

@jax.custom_vjp
def low(v):
    return lax.optimization_barrier(v.astype(jnp.bfloat16)).astype(jnp.float32)

@jax.custom_vjp
def low_back(v):
    return v

def low_keep(v):
    return (low(v), None)

def low_pass(kept, grad):
    return (grad,)

def back_keep(v):
    return (v, None)

def back_low(kept, grad):
    return (low(grad),)
low.defvjp(low_keep, low_pass)
low_back.defvjp(back_keep, back_low)

def rounded_both(value):
    return low_back(low(value))

def layer_norm(value, gain, shift):
    centered = value - lax.optimization_barrier(jnp.mean(value, axis=-1, keepdims=True))
    variance = lax.optimization_barrier(jnp.mean(centered * centered, axis=-1, keepdims=True))
    return centered * lax.rsqrt(variance + epsilon) * gain + shift

def attend_one(block):
    queries, key_rows, value_rows, numbers = block
    scaling = HDIM ** (-0.5)
    scores = jnp.einsum('qhd,khd->hqk', queries, key_rows, precision=highest) * scaling
    same_doc = numbers[:, None] == numbers[None, :]
    scores = low_back(jnp.where(same_doc[None, :, :], scores, -1e+30))
    largest = lax.optimization_barrier(jnp.max(scores, axis=-1, keepdims=True))
    weights = jnp.exp(scores - largest)
    attention = weights / lax.optimization_barrier(jnp.sum(weights, axis=-1, keepdims=True))
    mixed = jnp.einsum('hqk,khd->qhd', low(attention), value_rows, precision=highest)
    return rounded_both(mixed)

def layer(token_rows, weight_qkv, weight_out, weight_in, weight_down, gain_one, shift_one, gain_two, shift_two, numbers):
    row_count = token_rows.shape[0]
    seq_count = row_count // SEQ
    projected = rounded_both(jnp.einsum('td,jde->jte', token_rows, weight_qkv, precision=highest))
    projected = projected.reshape(3, seq_count, SEQ, HEADS, HDIM)
    attended = lax.map(jax.checkpoint(attend_one), (projected[0], projected[1], projected[2], numbers.reshape(seq_count, SEQ)))
    attended = attended.reshape(row_count, D)
    branch = low_back(jnp.dot(attended, weight_out, precision=highest))
    first = layer_norm(token_rows + branch, gain_one, shift_one)
    inner = low_back(jnp.dot(low(first), weight_in, precision=highest))
    hidden = low(jax.nn.gelu(inner, approximate=False))
    second = low_back(jnp.dot(hidden, weight_down, precision=highest))
    return layer_norm(first + second, gain_two, shift_two)

def reference(tokens, segment, weight_qkv, weight_out, weight_in, weight_down, gain_one, shift_one, gain_two, shift_two, cotangent):
    params = tuple((weight.astype(jnp.float32) for weight in (weight_qkv, weight_out, weight_in, weight_down, gain_one, shift_one, gain_two, shift_two)))
    group_rows = math.gcd(TOKENS // SEQ, 8) * SEQ
    group_count = TOKENS // group_rows
    rows_all = tokens.astype(jnp.float32).reshape(group_count, group_rows, D)
    numbers_all = segment.reshape(group_count, group_rows)
    grads_all = cotangent.astype(jnp.float32).reshape(group_count, group_rows, D)

    def one_group(totals, items):
        token_rows, numbers, grad_output = items

        def forward(rows_in, *weights):
            return layer(rows_in, *weights, numbers)
        result, pull_back = jax.vjp(forward, token_rows, *params)
        pulled = pull_back(grad_output)
        totals = tuple((running + piece for running, piece in zip(totals, pulled[1:])))
        return (totals, (result.astype(jnp.bfloat16), pulled[0].astype(jnp.bfloat16)))
    starting = tuple((jnp.zeros(weight.shape, jnp.float32) for weight in params))
    totals, (outputs, input_grads) = lax.scan(one_group, starting, (rows_all, numbers_all, grads_all))
    return (outputs.reshape(TOKENS, D), input_grads.reshape(TOKENS, D), totals[0], totals[1], totals[2], totals[3], totals[4], totals[5], totals[6], totals[7])
```

```python
import jax
import jax.numpy as jnp
from jax import lax
from jax.sharding import PartitionSpec as P

HDIM = 64
SEQ = 512
epsilon = 1e-05
ALL = ("tensor", "dp")


def layer_norm(value, gain, shift):
    centered = value - jnp.mean(value, axis=-1, keepdims=True)
    inverse = lax.rsqrt(jnp.mean(centered * centered, axis=-1, keepdims=True) + epsilon)
    scaled = centered * inverse
    return (scaled * gain + shift, scaled, inverse)


def norm_back(grad_output, scaled, inverse, gain):
    grad_scaled = grad_output * gain
    centered_grad = grad_scaled - jnp.mean(grad_scaled, axis=-1, keepdims=True)
    return inverse * (
        centered_grad - scaled * jnp.mean(grad_scaled * scaled, axis=-1, keepdims=True)
    )


def norm_stats(grad_output, scaled):
    return jnp.stack([jnp.sum(grad_output * scaled, axis=0), jnp.sum(grad_output, axis=0)])


def dot_nn(left, right):
    return lax.dot_general(left, right, (((1,), (0,)), ((), ())), preferred_element_type=jnp.float32)


def dot_tn(left, right):
    return lax.dot_general(left, right, (((0,), (0,)), ((), ())), preferred_element_type=jnp.float32)


def dot_nt(left, right):
    return lax.dot_general(left, right, (((1,), (1,)), ((), ())), preferred_element_type=jnp.float32)


def gather(piece):
    full = lax.all_gather(piece, ALL, axis=0, tiled=True)
    return full.reshape(2, full.shape[0] // 2, full.shape[1])


def scatter(full):
    full = full.astype(jnp.bfloat16).reshape(-1, full.shape[-1])
    return lax.psum_scatter(full, ALL, scatter_dimension=0, tiled=True).astype(jnp.float32)


def masked_scores(queries, key_rows, same_doc):
    scores = jnp.einsum("bqhd,bkhd->bhqk", queries, key_rows, preferred_element_type=jnp.float32)
    return jnp.where(same_doc[:, None], scores * HDIM ** (-0.5), -1e30)


def shards(
    tokens,
    segment,
    weight_qkv,
    weight_out,
    weight_in,
    weight_down,
    gain_one,
    shift_one,
    gain_two,
    shift_two,
    cotangent,
):
    rows, width = tokens.shape
    seqs = rows // SEQ
    own = weight_qkv.shape[1]
    qkv = gather(jnp.transpose(weight_qkv, (1, 0, 2)).reshape(own, -1))
    out = gather(weight_out.T)
    win = gather(weight_in)
    down = gather(weight_down.T)
    norms = jnp.stack([gain_one, shift_one, gain_two, shift_two])
    norms = lax.all_gather(norms, "dp", axis=1, tiled=True).astype(jnp.float32)
    gain_first, shift_first, gain_second, shift_second = [norms[i] for i in range(4)]

    numbers = lax.dynamic_slice_in_dim(segment, lax.axis_index("tensor") * rows, rows)
    numbers = numbers.reshape(seqs, SEQ)
    same_doc = numbers[:, :, None] == numbers[:, None, :]

    sides = range(2)
    parts = []
    for t in sides:
        prod = dot_nn(tokens, qkv[t]).astype(jnp.bfloat16)
        third = prod.shape[1] // 3
        parts.append([prod[:, j * third : (j + 1) * third].reshape(seqs, SEQ, -1, HDIM) for j in range(3)])

    attended, kept = [], []
    for t in sides:
        queries, key_rows, value_rows = parts[t]
        scores = masked_scores(queries, key_rows, same_doc)
        largest = jnp.max(scores, axis=-1, keepdims=True)
        weights = jnp.exp(scores - largest)
        row_sums = jnp.sum(weights, axis=-1, keepdims=True)
        attention = weights / row_sums
        mixed = jnp.einsum(
            "bhqk,bkhd->bqhd", attention.astype(jnp.bfloat16), value_rows, preferred_element_type=jnp.float32
        )
        attended.append(mixed.astype(jnp.bfloat16).reshape(rows, -1))
        kept.append(largest + jnp.log(row_sums))

    branch = dot_nt(attended[0], out[0]) + dot_nt(attended[1], out[1])
    first, scaled_one, inverse_one = layer_norm(
        tokens.astype(jnp.float32) + branch, gain_first, shift_first
    )
    first_low = first.astype(jnp.bfloat16)
    inner = [dot_nn(first_low, win[t]) for t in sides]
    hidden = [jax.nn.gelu(inner[t], approximate=False).astype(jnp.bfloat16) for t in sides]
    second = dot_nt(hidden[0], down[0]) + dot_nt(hidden[1], down[1])
    final, scaled_two, inverse_two = layer_norm(first + second, gain_second, shift_second)
    output = final.astype(jnp.bfloat16)

    grad_final = cotangent.astype(jnp.float32)
    stats_two = norm_stats(grad_final, scaled_two)
    grad_resid_two = norm_back(grad_final, scaled_two, inverse_two, gain_second)
    grad_second = grad_resid_two.astype(jnp.bfloat16)
    sum_down = scatter(jnp.stack([dot_tn(grad_second, hidden[t]) for t in sides]))
    grad_inner = []
    for t in sides:
        pull = jax.vjp(lambda value: jax.nn.gelu(value, approximate=False), inner[t])[1]
        grad_inner.append(pull(dot_nn(grad_second, down[t]))[0].astype(jnp.bfloat16))
    sum_in = scatter(jnp.stack([dot_tn(first_low, grad_inner[t]) for t in sides]))
    grad_first = grad_resid_two + dot_nt(grad_inner[0], win[0]) + dot_nt(grad_inner[1], win[1])
    stats_one = norm_stats(grad_first, scaled_one)
    grad_resid_one = norm_back(grad_first, scaled_one, inverse_one, gain_first)
    grad_branch = grad_resid_one.astype(jnp.bfloat16)
    sum_out = scatter(jnp.stack([dot_tn(grad_branch, attended[t]) for t in sides]))
    back = grad_resid_one
    grad_qkv = []
    for t in sides:
        grad_mixed = dot_nn(grad_branch, out[t]).astype(jnp.bfloat16).reshape(seqs, SEQ, -1, HDIM)
        queries, key_rows, value_rows = parts[t]
        attention = jnp.exp(masked_scores(queries, key_rows, same_doc) - kept[t])
        grad_attention = jnp.einsum("bqhd,bkhd->bhqk", grad_mixed, value_rows, preferred_element_type=jnp.float32)
        centre = jnp.sum(attention * grad_attention, axis=-1, keepdims=True)
        grad_scores = (attention * (grad_attention - centre)).astype(jnp.bfloat16)
        scaling = HDIM ** (-0.5)
        grad_queries = scaling * jnp.einsum("bhqk,bkhd->bqhd", grad_scores, key_rows, preferred_element_type=jnp.float32)
        grad_keys = scaling * jnp.einsum("bhqk,bqhd->bkhd", grad_scores, queries, preferred_element_type=jnp.float32)
        grad_values = jnp.einsum(
            "bhqk,bqhd->bkhd", attention.astype(jnp.bfloat16), grad_mixed, preferred_element_type=jnp.float32
        )
        grad_parts = jnp.concatenate(
            [g.astype(jnp.bfloat16).reshape(rows, -1) for g in (grad_queries, grad_keys, grad_values)], axis=1
        )
        grad_qkv.append(dot_tn(tokens, grad_parts))
        back = back + dot_nt(grad_parts, qkv[t])
    sum_qkv = scatter(jnp.stack(grad_qkv))
    input_grad = back.astype(jnp.bfloat16)
    stats = lax.psum(jnp.concatenate([stats_one, stats_two]), ("tensor",))
    stats = lax.psum_scatter(stats, "dp", scatter_dimension=1, tiled=True)
    return (
        output,
        input_grad,
        jnp.transpose(sum_qkv.reshape(own, 3, -1), (1, 0, 2)),
        sum_out.T,
        sum_in,
        sum_down.T,
        stats[0],
        stats[1],
        stats[2],
        stats[3],
    )


def solution(mesh):
    both = P(("dp", "tensor"), None)
    split = P("dp")
    qkv_spec = P(None, "dp", "tensor")
    row_spec = P("tensor", "dp")
    in_spec = P("dp", "tensor")
    return jax.shard_map(
        shards,
        mesh=mesh,
        in_specs=(both, split, qkv_spec, row_spec, in_spec, row_spec, split, split, split, split, both),
        out_specs=(both, both, qkv_spec, row_spec, in_spec, row_spec, split, split, split, split),
        check_vma=False,
    )
```

```python
import jax
import jax.numpy as jnp
from jax import lax
from jax.sharding import PartitionSpec as P

HDIM = 64
SEQ = 512
epsilon = 1e-05

AXES = ("dp", "tensor")
ZS = 4


def place(z, x, c, y):
    return ((z * 2 + x) * 2 + c) * 2 + y


def pairs(move):
    found = []
    for z in range(ZS):
        for x in range(2):
            for c in range(2):
                for y in range(2):
                    found.append((place(z, x, c, y), place(*move(z, x, c, y))))
    return found


TO_CORE = pairs(lambda z, x, c, y: (z, x, 1 - c, y))
TO_NEAR = pairs(lambda z, x, c, y: (z, x, c, 1 - y) if c else (z, 1 - x, c, y))
TO_FAR = pairs(lambda z, x, c, y: (z, 1 - x, c, y) if c else (z, x, c, 1 - y))
TO_DEPTH = [pairs(lambda z, x, c, y: ((z - k) % ZS, x, c, y)) for k in range(ZS)]


def coords():
    d = lax.axis_index("dp")
    y = lax.axis_index("tensor")
    return d // 4, (d // 2) % 2, d % 2, y


def send(value, route):
    return lax.ppermute(value, AXES, route)


def in_order(own, other, at):
    return jnp.where(at == 0, jnp.stack([own, other]), jnp.stack([other, own]))


def tuned():
    return lax.axis_size("dp") == 16 and lax.axis_size("tensor") == 2


def gather_set(left, right):
    if not tuned():
        full = lax.all_gather(jnp.concatenate([left, right], axis=1), ("tensor", "dp"), axis=0, tiled=True)
        return tuple(halves(full.reshape(lax.axis_size("tensor"), -1, full.shape[1])))
    z, x, c, y = coords()
    first = c == 0
    got = send(jnp.where(first, right, left), TO_CORE)
    mine = jnp.where(first, jnp.concatenate([left, got]), jnp.concatenate([got, right]))
    own = [mine] + [send(mine, TO_DEPTH[k]) for k in (1, 2, 3)]
    column = jnp.stack(own + own[:3])
    column = lax.dynamic_slice_in_dim(column, (ZS - z) % ZS, ZS, 0)
    near = send(column, TO_NEAR)
    plane = in_order(column, near, jnp.where(first, x, y))
    far = send(plane, TO_FAR)
    whole = in_order(plane, far, jnp.where(first, y, x))
    sibling = send(whole, TO_CORE)
    full_left = jnp.where(first, whole, sibling)
    full_right = jnp.where(first, sibling, whole)
    n, h = left.shape
    full_left = jnp.transpose(full_left, (0, 2, 1, 3, 4)).reshape(2, 16 * n, h)
    full_right = jnp.transpose(full_right, (1, 2, 0, 3, 4)).reshape(2, 16 * n, h)
    return full_left, full_right


def add(a, b):
    return a.astype(jnp.float32) + b.astype(jnp.float32)


def low(a):
    return a.astype(jnp.bfloat16)


def scatter_set(left, right):
    if not tuned():
        full = jnp.concatenate([left, right], axis=2)
        full = lax.psum_scatter(
            full.reshape(-1, full.shape[2]), ("tensor", "dp"), scatter_dimension=0, tiled=True
        )
        full = lax.optimization_barrier(full)
        return tuple(halves(full.astype(jnp.float32)))
    z, x, c, y = coords()
    first = c == 0
    _, rows, h = left.shape
    n = rows // 16
    got = send(jnp.where(first, right, left), TO_CORE)
    part = low(add(jnp.where(first, left, right), got)).reshape(2, ZS, 2, 2 * n, h)

    def over_y(i):
        return jnp.transpose(lax.dynamic_index_in_dim(part, i, 0, keepdims=False), (1, 0, 2, 3))

    def over_x(i):
        return lax.dynamic_index_in_dim(part, i, 2, keepdims=False)

    got = send(jnp.where(first, over_y(1 - y), over_x(1 - x)), TO_FAR)
    part = low(add(jnp.where(first, over_y(y), over_x(x)), got))
    at = jnp.where(first, x, y)
    got = send(lax.dynamic_index_in_dim(part, 1 - at, 0, keepdims=False), TO_NEAR)
    part = low(add(lax.dynamic_index_in_dim(part, at, 0, keepdims=False), got))

    def depth(k):
        return lax.dynamic_index_in_dim(part, (z - k) % ZS, 0, keepdims=False)

    total = depth(0).astype(jnp.float32)
    for k in (1, 2, 3):
        total = total + send(depth(k), TO_DEPTH[k]).astype(jnp.float32)
    total = total.reshape(2, n, h)
    keep = lax.dynamic_index_in_dim(total, c, 0, keepdims=False)
    got = send(lax.dynamic_index_in_dim(total, 1 - c, 0, keepdims=False), TO_CORE)
    return jnp.where(first, keep, got), jnp.where(first, got, keep)


def layer_norm(value, gain, shift):
    centered = value - jnp.mean(value, axis=-1, keepdims=True)
    inverse = lax.rsqrt(jnp.mean(centered * centered, axis=-1, keepdims=True) + epsilon)
    scaled = centered * inverse
    return (scaled * gain + shift, scaled, inverse)


def norm_back(grad_output, scaled, inverse, gain):
    grad_scaled = grad_output * gain
    centered_grad = grad_scaled - jnp.mean(grad_scaled, axis=-1, keepdims=True)
    return inverse * (
        centered_grad - scaled * jnp.mean(grad_scaled * scaled, axis=-1, keepdims=True)
    )


def norm_stats(grad_output, scaled):
    return jnp.stack([jnp.sum(grad_output * scaled, axis=0), jnp.sum(grad_output, axis=0)])


def dot_nn(left, right):
    return lax.dot_general(left, right, (((1,), (0,)), ((), ())), preferred_element_type=jnp.float32)


def dot_tn(left, right):
    return lax.dot_general(left, right, (((0,), (0,)), ((), ())), preferred_element_type=jnp.float32)


def dot_nt(left, right):
    return lax.dot_general(left, right, (((1,), (1,)), ((), ())), preferred_element_type=jnp.float32)


def halves(value):
    return jnp.split(value, 2, axis=-1)


def reduce_set(value):
    return jnp.concatenate(scatter_set(*halves(value)), axis=1)


def masked_scores(queries, key_rows, same_doc):
    scores = jnp.einsum("bqhd,bkhd->bhqk", queries, key_rows, preferred_element_type=jnp.float32)
    return jnp.where(same_doc[:, None], scores * HDIM ** (-0.5), -1e30)


def shards(
    tokens,
    segment,
    weight_qkv,
    weight_out,
    weight_in,
    weight_down,
    gain_one,
    shift_one,
    gain_two,
    shift_two,
    cotangent,
):
    rows, width = tokens.shape
    seqs = rows // SEQ
    own = weight_qkv.shape[1]
    norms = jnp.stack([gain_one, shift_one, gain_two, shift_two], axis=1)
    norms = jnp.pad(norms, ((0, 0), (0, 124)))
    set_one = jnp.concatenate([jnp.transpose(weight_qkv, (1, 0, 2)).reshape(own, -1), norms], axis=1)
    set_two = jnp.concatenate(
        [weight_out.T, weight_in, jnp.zeros((own, 128), jnp.bfloat16)], axis=1
    )
    set_one = jnp.concatenate(gather_set(*halves(set_one)), axis=2)
    set_two = jnp.concatenate(gather_set(*halves(set_two)), axis=2)
    down = jnp.concatenate(gather_set(*halves(weight_down.T)), axis=2)
    span = 3 * weight_qkv.shape[2]
    qkv = set_one[:, :, :span]
    wide = weight_out.shape[0]
    out = set_two[:, :, :wide]
    win = set_two[:, :, wide : wide + weight_in.shape[1]]
    norms = set_one[0, :, span : span + 4].T.astype(jnp.float32)
    gain_first, shift_first, gain_second, shift_second = [norms[i] for i in range(4)]

    numbers = lax.dynamic_slice_in_dim(segment, lax.axis_index("tensor") * rows, rows)
    numbers = numbers.reshape(seqs, SEQ)
    same_doc = numbers[:, :, None] == numbers[:, None, :]

    sides = range(2)
    parts = []
    for t in sides:
        prod = dot_nn(tokens, qkv[t]).astype(jnp.bfloat16)
        third = prod.shape[1] // 3
        parts.append([prod[:, j * third : (j + 1) * third].reshape(seqs, SEQ, -1, HDIM) for j in range(3)])

    attended, kept = [], []
    for t in sides:
        queries, key_rows, value_rows = parts[t]
        scores = masked_scores(queries, key_rows, same_doc)
        largest = jnp.max(scores, axis=-1, keepdims=True)
        weights = jnp.exp(scores - largest)
        row_sums = jnp.sum(weights, axis=-1, keepdims=True)
        attention = weights / row_sums
        mixed = jnp.einsum(
            "bhqk,bkhd->bqhd", attention.astype(jnp.bfloat16), value_rows, preferred_element_type=jnp.float32
        )
        attended.append(mixed.astype(jnp.bfloat16).reshape(rows, -1))
        kept.append(largest + jnp.log(row_sums))

    branch = dot_nt(attended[0], out[0]) + dot_nt(attended[1], out[1])
    first, scaled_one, inverse_one = layer_norm(
        tokens.astype(jnp.float32) + branch, gain_first, shift_first
    )
    first_low = first.astype(jnp.bfloat16)
    inner = [dot_nn(first_low, win[t]) for t in sides]
    hidden = [jax.nn.gelu(inner[t], approximate=False).astype(jnp.bfloat16) for t in sides]
    second = dot_nt(hidden[0], down[0]) + dot_nt(hidden[1], down[1])
    final, scaled_two, inverse_two = layer_norm(first + second, gain_second, shift_second)
    output = final.astype(jnp.bfloat16)

    grad_final = cotangent.astype(jnp.float32)
    stats_two = norm_stats(grad_final, scaled_two)
    grad_resid_two = norm_back(grad_final, scaled_two, inverse_two, gain_second)
    grad_second = grad_resid_two.astype(jnp.bfloat16)
    sum_down = reduce_set(jnp.stack([low(dot_tn(grad_second, hidden[t])) for t in sides]))
    grad_inner = []
    for t in sides:
        pull = jax.vjp(lambda value: jax.nn.gelu(value, approximate=False), inner[t])[1]
        grad_inner.append(pull(dot_nn(grad_second, down[t]))[0].astype(jnp.bfloat16))
    grad_in = [low(dot_tn(first_low, grad_inner[t])) for t in sides]
    grad_first = grad_resid_two + dot_nt(grad_inner[0], win[0]) + dot_nt(grad_inner[1], win[1])
    stats_one = norm_stats(grad_first, scaled_one)
    grad_resid_one = norm_back(grad_first, scaled_one, inverse_one, gain_first)
    grad_branch = grad_resid_one.astype(jnp.bfloat16)
    grad_out = [low(dot_tn(grad_branch, attended[t])) for t in sides]
    stats = low(jnp.concatenate([stats_one, stats_two]).T)
    stats = jnp.pad(stats, ((0, 0), (0, 124)))
    sum_two = reduce_set(
        jnp.stack([jnp.concatenate([grad_in[t], grad_out[t], stats], axis=1) for t in sides])
    )
    back = grad_resid_one
    grad_qkv = []
    for t in sides:
        grad_mixed = dot_nn(grad_branch, out[t]).astype(jnp.bfloat16).reshape(seqs, SEQ, -1, HDIM)
        queries, key_rows, value_rows = parts[t]
        attention = jnp.exp(masked_scores(queries, key_rows, same_doc) - kept[t])
        grad_attention = jnp.einsum("bqhd,bkhd->bhqk", grad_mixed, value_rows, preferred_element_type=jnp.float32)
        centre = jnp.sum(attention * grad_attention, axis=-1, keepdims=True)
        grad_scores = (attention * (grad_attention - centre)).astype(jnp.bfloat16)
        scaling = HDIM ** (-0.5)
        grad_queries = scaling * jnp.einsum("bhqk,bkhd->bqhd", grad_scores, key_rows, preferred_element_type=jnp.float32)
        grad_keys = scaling * jnp.einsum("bhqk,bqhd->bkhd", grad_scores, queries, preferred_element_type=jnp.float32)
        grad_values = jnp.einsum(
            "bhqk,bqhd->bkhd", attention.astype(jnp.bfloat16), grad_mixed, preferred_element_type=jnp.float32
        )
        grad_parts = jnp.concatenate(
            [g.astype(jnp.bfloat16).reshape(rows, -1) for g in (grad_queries, grad_keys, grad_values)], axis=1
        )
        grad_qkv.append(low(dot_tn(tokens, grad_parts)))
        back = back + dot_nt(grad_parts, qkv[t])
    sum_qkv = reduce_set(jnp.pad(jnp.stack(grad_qkv), ((0, 0), (0, 0), (0, 128))))[:, :span]
    input_grad = back.astype(jnp.bfloat16)
    hidden_span = weight_in.shape[1]
    stats = sum_two[:, hidden_span + wide : hidden_span + wide + 4].T
    return (
        output,
        input_grad,
        jnp.transpose(sum_qkv.reshape(own, 3, -1), (1, 0, 2)),
        sum_two[:, hidden_span : hidden_span + wide].T,
        sum_two[:, :hidden_span],
        sum_down.T,
        stats[0],
        stats[1],
        stats[2],
        stats[3],
    )


def solution(mesh):
    both = P(("dp", "tensor"), None)
    split = P("dp")
    qkv_spec = P(None, "dp", "tensor")
    row_spec = P("tensor", "dp")
    in_spec = P("dp", "tensor")
    return jax.shard_map(
        shards,
        mesh=mesh,
        in_specs=(both, split, qkv_spec, row_spec, in_spec, row_spec, split, split, split, split, both),
        out_specs=(both, both, qkv_spec, row_spec, in_spec, row_spec, split, split, split, split),
        check_vma=False,
    )
```

```python
import jax
import jax.numpy as jnp
from jax import lax
from jax.experimental import pallas as pl
from jax.experimental.pallas import tpu as pltpu
from jax.sharding import PartitionSpec as P

HDIM = 64
SEQ = 512
LANES = 128
VMEM = 56 * 1024 * 1024
epsilon = 1e-05

AXES = ("dp", "tensor")
ZS = 4


def place(z, x, c, y):
    return ((z * 2 + x) * 2 + c) * 2 + y


def pairs(move):
    found = []
    for z in range(ZS):
        for x in range(2):
            for c in range(2):
                for y in range(2):
                    found.append((place(z, x, c, y), place(*move(z, x, c, y))))
    return found


TO_CORE = pairs(lambda z, x, c, y: (z, x, 1 - c, y))
TO_NEAR = pairs(lambda z, x, c, y: (z, x, c, 1 - y) if c else (z, 1 - x, c, y))
TO_FAR = pairs(lambda z, x, c, y: (z, 1 - x, c, y) if c else (z, x, c, 1 - y))
TO_DEPTH = [pairs(lambda z, x, c, y: ((z - k) % ZS, x, c, y)) for k in range(ZS)]


def coords():
    d = lax.axis_index("dp")
    y = lax.axis_index("tensor")
    return d // 4, (d // 2) % 2, d % 2, y


def send(value, route):
    return lax.ppermute(value, AXES, route)


def in_order(own, other, at):
    return jnp.where(at == 0, jnp.stack([own, other]), jnp.stack([other, own]))


def tuned():
    return lax.axis_size("dp") == 16 and lax.axis_size("tensor") == 2


def tie(*values):
    return lax.optimization_barrier(values)


def gather_steps(left, right):
    if not tuned():
        for _ in range(4):
            left = yield left
        full = lax.all_gather(jnp.concatenate([left, right], axis=1), ("tensor", "dp"), axis=0, tiled=True)
        full = full.reshape(lax.axis_size("tensor"), -1, full.shape[1])
        yield tuple(jnp.split(full, 2, axis=2))
        return
    z, x, c, y = coords()
    first = c == 0
    got = send(jnp.where(first, right, left), TO_CORE)
    mine = jnp.where(first, jnp.concatenate([left, got]), jnp.concatenate([got, right]))
    mine = yield mine
    own = [mine] + [send(mine, TO_DEPTH[k]) for k in (1, 2, 3)]
    column = jnp.stack(own + own[:3])
    column = lax.dynamic_slice_in_dim(column, (ZS - z) % ZS, ZS, 0)
    column = yield column
    near = send(column, TO_NEAR)
    plane = in_order(column, near, jnp.where(first, x, y))
    plane = yield plane
    far = send(plane, TO_FAR)
    whole = in_order(plane, far, jnp.where(first, y, x))
    whole = yield whole
    sibling = send(whole, TO_CORE)
    full_left = jnp.where(first, whole, sibling)
    full_right = jnp.where(first, sibling, whole)
    n, h = left.shape
    full_left = jnp.transpose(full_left, (0, 2, 1, 3, 4)).reshape(2, 16 * n, h)
    full_right = jnp.transpose(full_right, (1, 2, 0, 3, 4)).reshape(2, 16 * n, h)
    yield full_left, full_right


def add(a, b):
    return a.astype(jnp.float32) + b.astype(jnp.float32)


def scatter_steps(left, right):
    if not tuned():
        for _ in range(4):
            left = yield left
        full = jnp.concatenate([left, right], axis=2)
        full = lax.psum_scatter(
            full.reshape(-1, full.shape[2]), ("tensor", "dp"), scatter_dimension=0, tiled=True
        )
        full = lax.optimization_barrier(full).astype(jnp.float32)
        yield tuple(jnp.split(full, 2, axis=1))
        return
    z, x, c, y = coords()
    first = c == 0
    _, rows, h = left.shape
    n = rows // 16
    got = send(jnp.where(first, right, left), TO_CORE)
    part = low(add(jnp.where(first, left, right), got)).reshape(2, ZS, 2, 2 * n, h)
    part = yield part

    def over_y(i):
        return jnp.transpose(lax.dynamic_index_in_dim(part, i, 0, keepdims=False), (1, 0, 2, 3))

    def over_x(i):
        return lax.dynamic_index_in_dim(part, i, 2, keepdims=False)

    got = send(jnp.where(first, over_y(1 - y), over_x(1 - x)), TO_FAR)
    part = low(add(jnp.where(first, over_y(y), over_x(x)), got))
    part = yield part
    at = jnp.where(first, x, y)
    got = send(lax.dynamic_index_in_dim(part, 1 - at, 0, keepdims=False), TO_NEAR)
    part = low(add(lax.dynamic_index_in_dim(part, at, 0, keepdims=False), got))
    part = yield part

    def depth(k):
        return lax.dynamic_index_in_dim(part, (z - k) % ZS, 0, keepdims=False)

    total = depth(0).astype(jnp.float32)
    for k in (1, 2, 3):
        total = total + send(depth(k), TO_DEPTH[k]).astype(jnp.float32)
    total = total.reshape(2, n, h)
    total = yield total
    keep = lax.dynamic_index_in_dim(total, c, 0, keepdims=False)
    got = send(lax.dynamic_index_in_dim(total, 1 - c, 0, keepdims=False), TO_CORE)
    yield jnp.where(first, keep, got), jnp.where(first, got, keep)


def dot_nn(left, right):
    return lax.dot_general(left, right, (((1,), (0,)), ((), ())), preferred_element_type=jnp.float32)


def dot_tn(left, right):
    return lax.dot_general(left, right, (((0,), (0,)), ((), ())), preferred_element_type=jnp.float32)


def dot_nt(left, right):
    return lax.dot_general(left, right, (((1,), (1,)), ((), ())), preferred_element_type=jnp.float32)


def low(value):
    return value.astype(jnp.bfloat16)


def flip(value):
    return jnp.swapaxes(value, 0, 1)


def pair_cols(left, right, pairs, at):
    start = at * LANES
    width = left.shape[-1]
    if start < width:
        return left[:, start : start + LANES]
    return right[:, start - width : start - width + LANES]


def attend_kernel(x_ref, a_ref, b_ref, row_ref, col_ref, pa_ref, pb_ref, e_ref, att_ref, flat_ref, inv_ref, bias_ref):
    pairs = att_ref.shape[-1] // LANES
    x = x_ref[...]
    pa_ref[0] = low(dot_nn(x, a_ref[0]))
    pb_ref[0] = low(dot_nn(x, b_ref[0]))
    bias_ref[...] = jnp.where(col_ref[0] == row_ref[0], 0.0, -1e30)
    lane = lax.broadcasted_iota(jnp.int32, (SEQ, LANES), 1)
    chunk = SEQ // 2
    left, right = pa_ref[0], pb_ref[0]
    for p in range(pairs):
        queries = pair_cols(left, right, pairs, p)
        key_rows = pair_cols(left, right, pairs, pairs + p)
        values_flat = flip(pair_cols(left, right, pairs, 2 * pairs + p))
        for half in range(2):
            h = 2 * p + half
            own = (lane < HDIM) if half == 0 else (lane >= HDIM)
            chosen = low(jnp.where(own, queries.astype(jnp.float32) * HDIM**-0.5, 0.0))
            value_half = values_flat[half * HDIM : (half + 1) * HDIM]
            for n in range(2):
                cut = slice(n * chunk, (n + 1) * chunk)
                scores = dot_nt(key_rows, chosen[cut]) + bias_ref[:, cut]
                largest = jnp.max(scores, axis=0, keepdims=True)
                weights = jnp.exp(scores - largest)
                inverse = 1.0 / jnp.sum(weights, axis=0, keepdims=True)
                weights = low(weights)
                e_ref[0, 0, h, :, cut] = weights
                inv_ref[0, 0, h : h + 1, cut] = inverse
                flat_ref[0, 0, h * HDIM : (h + 1) * HDIM, cut] = low(dot_nn(value_half, weights) * inverse)
        att_ref[0, :, p * LANES : (p + 1) * LANES] = flip(flat_ref[0, 0, p * LANES : (p + 1) * LANES, :])


def attend(tokens, left, right, numbers, t):
    rows, width = tokens.shape
    seqs = rows // SEQ
    cols = left.shape[2]
    wide = (2 * cols - LANES) // 3
    heads = wide // HDIM
    used = cols - LANES
    bf = jnp.bfloat16
    return pl.pallas_call(
        attend_kernel,
        grid=(seqs,),
        in_specs=[
            pl.BlockSpec((SEQ, width), lambda s: (s, 0)),
            pl.BlockSpec((1, width, cols), lambda s: (t, 0, 0)),
            pl.BlockSpec((1, width, used), lambda s: (t, 0, 0)),
            pl.BlockSpec((1, 1, SEQ), lambda s: (s, 0, 0)),
            pl.BlockSpec((1, SEQ, 1), lambda s: (s, 0, 0)),
        ],
        out_specs=[
            pl.BlockSpec((1, SEQ, cols), lambda s: (0, s, 0)),
            pl.BlockSpec((1, SEQ, used), lambda s: (0, s, 0)),
            pl.BlockSpec((1, 1, heads, SEQ, SEQ), lambda s: (0, s, 0, 0, 0)),
            pl.BlockSpec((1, SEQ, wide), lambda s: (0, s, 0)),
            pl.BlockSpec((1, 1, wide, SEQ), lambda s: (0, s, 0, 0)),
            pl.BlockSpec((1, 1, heads, SEQ), lambda s: (0, s, 0, 0)),
        ],
        out_shape=[
            jax.ShapeDtypeStruct((1, rows, cols), bf),
            jax.ShapeDtypeStruct((1, rows, used), bf),
            jax.ShapeDtypeStruct((1, seqs, heads, SEQ, SEQ), bf),
            jax.ShapeDtypeStruct((1, rows, wide), bf),
            jax.ShapeDtypeStruct((1, seqs, wide, SEQ), bf),
            jax.ShapeDtypeStruct((1, seqs, heads, SEQ), jnp.float32),
        ],
        scratch_shapes=[pltpu.VMEM((SEQ, SEQ), jnp.float32)],
        compiler_params=pltpu.CompilerParams(vmem_limit_bytes=VMEM),
        cost_estimate=pl.CostEstimate(flops=8_000_000_000, bytes_accessed=15_000_000, transcendentals=3_100_000),
        name="attend",
    )(tokens, left, right, numbers.reshape(seqs, 1, SEQ), numbers.reshape(seqs, SEQ, 1))


def attend_back_kernel(g_ref, w_ref, pa_ref, pb_ref, e_ref, flat_ref, inv_ref, da_ref, db_ref, gt_ref):
    wide = flat_ref.shape[2]
    pairs = wide // LANES
    gt_ref[...] = flip(low(dot_nn(g_ref[...], w_ref[...])))
    left, right = pa_ref[0], pb_ref[0]
    lane = lax.broadcasted_iota(jnp.int32, (SEQ, LANES), 1)
    cols = da_ref.shape[2]

    def put(at, value):
        start = at * LANES
        if start < cols:
            da_ref[0, :, start : start + LANES] = value
        else:
            db_ref[0, :, start - cols : start - cols + LANES] = value

    blank = jnp.zeros((HDIM, SEQ), jnp.bfloat16)
    for p in range(pairs):
        queries = pair_cols(left, right, pairs, p)
        key_rows = pair_cols(left, right, pairs, pairs + p)
        value_rows = pair_cols(left, right, pairs, 2 * pairs + p)
        keys_flat = flip(key_rows)
        scaled = []
        for half in range(2):
            h = 2 * p + half
            grads = gt_ref[h * HDIM : (h + 1) * HDIM, :].astype(jnp.float32)
            scaled.append(low(grads * inv_ref[0, 0, h : h + 1, :]))
        grads = flip(jnp.concatenate(scaled, axis=0))
        dq, dk, dv = [], [], []
        for half in range(2):
            h = 2 * p + half
            mine = scaled[half]
            flat = flat_ref[0, 0, h * HDIM : (h + 1) * HDIM, :].astype(jnp.float32)
            centre = jnp.sum(mine.astype(jnp.float32) * flat, axis=0, keepdims=True)
            stacked = [mine, blank] if half == 0 else [blank, mine]
            grad_weights = dot_nn(value_rows, jnp.concatenate(stacked, axis=0))
            weights = e_ref[0, 0, h]
            grad_scores = low(weights.astype(jnp.float32) * (grad_weights - centre))
            dv.append(dot_nn(weights, grads))
            dk.append(dot_nn(grad_scores, queries))
            dq.append(dot_nn(keys_flat[half * HDIM : (half + 1) * HDIM], grad_scores))
        put(p, flip(low(jnp.concatenate(dq, axis=0) * HDIM**-0.5)))
        put(pairs + p, low(jnp.where(lane < HDIM, dk[0], dk[1]) * HDIM**-0.5))
        put(2 * pairs + p, low(jnp.where(lane < HDIM, dv[0], dv[1])))
    db_ref[0, :, cols - LANES :] = jnp.zeros((SEQ, LANES), jnp.bfloat16)


def attend_back(grad_branch, weight_out, kept, t):
    pa, pb, e, att, flat, inv = kept
    rows, width = grad_branch.shape
    seqs = rows // SEQ
    cols, used = pa.shape[2], pb.shape[2]
    heads, wide = e.shape[2], att.shape[2]
    bf = jnp.bfloat16
    return pl.pallas_call(
        attend_back_kernel,
        grid=(seqs,),
        in_specs=[
            pl.BlockSpec((SEQ, width), lambda s: (s, 0)),
            pl.BlockSpec((width, wide), lambda s: (0, t)),
            pl.BlockSpec((1, SEQ, cols), lambda s: (0, s, 0)),
            pl.BlockSpec((1, SEQ, used), lambda s: (0, s, 0)),
            pl.BlockSpec((1, 1, heads, SEQ, SEQ), lambda s: (0, s, 0, 0, 0)),
            pl.BlockSpec((1, 1, wide, SEQ), lambda s: (0, s, 0, 0)),
            pl.BlockSpec((1, 1, heads, SEQ), lambda s: (0, s, 0, 0)),
        ],
        out_specs=[
            pl.BlockSpec((1, SEQ, cols), lambda s: (0, s, 0)),
            pl.BlockSpec((1, SEQ, cols), lambda s: (0, s, 0)),
        ],
        out_shape=[jax.ShapeDtypeStruct((1, rows, cols), bf)] * 2,
        scratch_shapes=[pltpu.VMEM((wide, SEQ), bf)],
        compiler_params=pltpu.CompilerParams(vmem_limit_bytes=VMEM),
        cost_estimate=pl.CostEstimate(flops=8_000_000_000, bytes_accessed=15_000_000, transcendentals=0),
        name="attend_back",
    )(grad_branch, weight_out, pa, pb, e, flat, inv)


def gelu_parts(v):
    size = jnp.abs(v)
    base = 1.0 + (0.3275911 * 0.5**0.5) * size
    near = pl.reciprocal(base, approx=True)
    t = near * (2.0 - base * near)
    bell = jnp.exp(-0.5 * (v * v))
    tail = t * (0.127414796 + t * (-0.142248368 + t * (0.710706871 + t * (-0.7265760135 + t * 0.5307027145)))) * bell
    below = jnp.where(v >= 0.0, 1.0 - tail, tail)
    return v * below, below + 0.3989422804014327 * (v * bell)


def widen_kernel(x_ref, w_ref, hid_ref, slope_ref):
    x = x_ref[...]
    for start in range(0, w_ref.shape[1], 256):
        cut = slice(start, start + 256)
        value, slope = gelu_parts(dot_nn(x, w_ref[:, cut]))
        hid_ref[:, cut] = low(value)
        slope_ref[:, cut] = low(slope)


def widen(first_low, weight_in):
    rows, width = first_low.shape
    span = weight_in.shape[1]
    block, part = 256, span // 2
    bf = jnp.bfloat16
    return pl.pallas_call(
        widen_kernel,
        grid=(2, rows // block),
        in_specs=[
            pl.BlockSpec((block, width), lambda t, r: (r, 0)),
            pl.BlockSpec((width, part), lambda t, r: (0, t)),
        ],
        out_specs=[pl.BlockSpec((block, part), lambda t, r: (r, t))] * 2,
        out_shape=[jax.ShapeDtypeStruct((rows, span), bf)] * 2,
        compiler_params=pltpu.CompilerParams(vmem_limit_bytes=VMEM),
        cost_estimate=pl.CostEstimate(flops=10_000_000_000, bytes_accessed=20_000_000, transcendentals=3_100_000),
        name="widen",
    )(first_low, weight_in)


def layer_norm(value, gain, shift):
    centered = value - jnp.mean(value, axis=-1, keepdims=True)
    inverse = lax.rsqrt(jnp.mean(centered * centered, axis=-1, keepdims=True) + epsilon)
    scaled = centered * inverse
    return (scaled * gain + shift, scaled, inverse)


def norm_back(grad_output, scaled, inverse, gain):
    grad_scaled = grad_output * gain
    centered_grad = grad_scaled - jnp.mean(grad_scaled, axis=-1, keepdims=True)
    return inverse * (
        centered_grad - scaled * jnp.mean(grad_scaled * scaled, axis=-1, keepdims=True)
    )


def norm_stats(grad_output, scaled):
    return jnp.stack([jnp.sum(grad_output * scaled, axis=0), jnp.sum(grad_output, axis=0)])


def halves(value):
    return jnp.split(value, 2, axis=-1)


def shards(
    tokens,
    segment,
    weight_qkv,
    weight_out,
    weight_in,
    weight_down,
    gain_one,
    shift_one,
    gain_two,
    shift_two,
    cotangent,
):
    rows, width = tokens.shape
    own = weight_qkv.shape[1]
    wide = weight_out.shape[0]
    span = weight_in.shape[1]
    sides = range(2)
    bf = jnp.bfloat16

    norms = jnp.stack([gain_one, shift_one, gain_two, shift_two], axis=1)
    norms = jnp.pad(norms, ((0, 0), (0, LANES - 4)))
    set_one = jnp.concatenate([jnp.transpose(weight_qkv, (1, 0, 2)).reshape(own, -1), norms], axis=1)
    set_two = jnp.concatenate([weight_out.T, weight_in, jnp.zeros((own, LANES), bf)], axis=1)
    get_one = gather_steps(*halves(set_one))
    get_two = gather_steps(*halves(set_two))
    get_three = gather_steps(*halves(weight_down.T))
    one = next(get_one)
    two = next(get_two)
    three = next(get_three)
    one = get_one.send(one)
    one, two = tie(one, two)
    two = get_two.send(two)
    one = get_one.send(one)
    one = get_one.send(one)
    one, two, three = tie(one, two, three)
    three = get_three.send(three)
    left, right = get_one.send(one)
    norms = right[0, :, right.shape[2] - LANES :][:, :4].T.astype(jnp.float32)
    gain_first, shift_first, gain_second, shift_second = [norms[i] for i in range(4)]

    numbers = lax.dynamic_slice_in_dim(segment, lax.axis_index("tensor") * rows, rows)
    numbers = numbers.reshape(rows // SEQ, SEQ)
    kept = [attend(tokens, left, right, numbers, 0)]
    two = get_two.send(two)
    two, left = tie(two, left)
    kept.append(attend(tokens, left, right, numbers, 1))
    attended = [kept[t][3][0] for t in sides]
    two = get_two.send(two)
    two, three = tie(two, three)
    three = get_three.send(three)
    two_left, two_right = get_two.send(two)
    out = jnp.concatenate([two_left[t][:, :wide] for t in sides], axis=1)
    split = two_left.shape[2] - wide
    win = jnp.concatenate(
        [piece for t in sides for piece in (two_left[t][:, wide:], two_right[t][:, : span - split])], axis=1
    )

    branch = dot_nt(attended[0], out[:, :wide]) + dot_nt(attended[1], out[:, wide:])
    first, scaled_one, inverse_one = layer_norm(
        tokens.astype(jnp.float32) + branch, gain_first, shift_first
    )
    first_low = low(first)
    three, first_low = tie(three, first_low)
    hidden, slope = widen(first_low, win)
    three = get_three.send(three)
    three_left, three_right = get_three.send(three)
    down = jnp.concatenate([piece for t in sides for piece in (three_left[t], three_right[t])], axis=1)
    second = dot_nt(hidden, down)
    final, scaled_two, inverse_two = layer_norm(first + second, gain_second, shift_second)
    output = low(final)

    grad_final = cotangent.astype(jnp.float32)
    stats_two = norm_stats(grad_final, scaled_two)
    grad_resid_two = norm_back(grad_final, scaled_two, inverse_two, gain_second)
    grad_second = low(grad_resid_two)
    grad_down = low(dot_tn(grad_second, hidden)).reshape(width, 2, 2, -1)
    put_down = scatter_steps(*[jnp.transpose(grad_down[:, :, i], (1, 0, 2)) for i in sides])
    three = next(put_down)
    grad_inner = low(dot_nn(grad_second, down) * slope.astype(jnp.float32))
    three, grad_inner = tie(three, grad_inner)
    three = put_down.send(three)
    grad_in = low(dot_tn(first_low, grad_inner))
    three, grad_inner = tie(three, grad_inner)
    three = put_down.send(three)
    grad_first = grad_resid_two + dot_nt(grad_inner, win)
    stats_one = norm_stats(grad_first, scaled_one)
    grad_resid_one = norm_back(grad_first, scaled_one, inverse_one, gain_first)
    grad_branch = low(grad_resid_one)
    three, grad_branch = tie(three, grad_branch)
    three = put_down.send(three)
    grad_out = [low(dot_tn(grad_branch, attended[t])) for t in sides]
    stats = low(jnp.concatenate([stats_one, stats_two]).T)
    stats = jnp.pad(stats, ((0, 0), (0, LANES - 4)))
    put_two = scatter_steps(
        jnp.stack([jnp.concatenate([grad_out[t], grad_in[:, t * span : t * span + split]], axis=1) for t in sides]),
        jnp.stack([jnp.concatenate([grad_in[:, t * span + split : (t + 1) * span], stats], axis=1) for t in sides]),
    )
    two = next(put_two)
    grad_parts = [attend_back(grad_branch, out, kept[0], 0)]
    two, grad_branch = tie(two, grad_branch)
    two = put_two.send(two)
    grad_parts.append(attend_back(grad_branch, out, kept[1], 1))
    put_one = scatter_steps(
        *[jnp.stack([low(dot_tn(tokens, grad_parts[t][i][0])) for t in sides]) for i in sides]
    )
    one = next(put_one)
    two = put_two.send(two)
    one, two = tie(one, two)
    one = put_one.send(one)
    two = put_two.send(two)
    back = grad_resid_one
    for t in sides:
        back = back + dot_nt(grad_parts[t][0][0], left[t]) + dot_nt(grad_parts[t][1][0], right[t])
    input_grad = low(back)
    one = put_one.send(one)
    one = put_one.send(one)
    sum_one = jnp.concatenate(put_one.send(one), axis=1)[:, : 3 * wide]
    sum_two = jnp.concatenate(put_two.send(two), axis=1)
    sum_down = jnp.concatenate(put_down.send(three), axis=1)
    stats = sum_two[:, wide + span : wide + span + 4].T
    return (
        output,
        input_grad,
        jnp.transpose(sum_one.reshape(own, 3, -1), (1, 0, 2)),
        sum_two[:, :wide].T,
        sum_two[:, wide : wide + span],
        sum_down.T,
        stats[0],
        stats[1],
        stats[2],
        stats[3],
    )


def solution(mesh):
    both = P(("dp", "tensor"), None)
    split = P("dp")
    qkv_spec = P(None, "dp", "tensor")
    row_spec = P("tensor", "dp")
    in_spec = P("dp", "tensor")
    return jax.shard_map(
        shards,
        mesh=mesh,
        in_specs=(both, split, qkv_spec, row_spec, in_spec, row_spec, split, split, split, split, both),
        out_specs=(both, both, qkv_spec, row_spec, in_spec, row_spec, split, split, split, split),
        check_vma=False,
    )
```

```python
import functools

import jax
import jax.numpy as jnp
from jax import lax
from jax.experimental import pallas as pl
from jax.experimental.pallas import tpu as pltpu
from jax.sharding import PartitionSpec as P

HDIM = 64
SEQ = 512
LANES = 128
BLOCK = 256
CHUNK = 256
VMEM = 56 * 1024 * 1024
epsilon = 1e-05


def low(value):
    return value.astype(jnp.bfloat16)


AXES = ("dp", "tensor")
ZS = 4


def place(z, x, c, y):
    return ((z * 2 + x) * 2 + c) * 2 + y


def pairs(move):
    found = []
    for z in range(ZS):
        for x in range(2):
            for c in range(2):
                for y in range(2):
                    found.append((place(z, x, c, y), place(*move(z, x, c, y))))
    return found


TO_CORE = pairs(lambda z, x, c, y: (z, x, 1 - c, y))
TO_NEAR = pairs(lambda z, x, c, y: (z, x, c, 1 - y) if c else (z, 1 - x, c, y))
TO_FAR = pairs(lambda z, x, c, y: (z, 1 - x, c, y) if c else (z, x, c, 1 - y))
TO_DEPTH = [pairs(lambda z, x, c, y: ((z - k) % ZS, x, c, y)) for k in range(ZS)]


def coords():
    d = lax.axis_index("dp")
    y = lax.axis_index("tensor")
    return d // 4, (d // 2) % 2, d % 2, y


def send(value, route):
    return lax.ppermute(value, AXES, route)


def in_order(own, other, at):
    return jnp.where(at == 0, jnp.stack([own, other]), jnp.stack([other, own]))


def tuned():
    return lax.axis_size("dp") == 16 and lax.axis_size("tensor") == 2


def after(value, *others):
    return lax.optimization_barrier((value, others))[0]


class Flow:
    def __init__(self, steps):
        self.steps = steps
        self.value = next(steps)

    def go(self, count=1):
        for _ in range(count):
            self.value = self.steps.send(self.value)
        return self.value

    def after(self, *others):
        self.value = after(self.value, *others)


def gather_steps(left, right):
    if not tuned():
        for _ in range(10):
            left = yield left
        full = lax.all_gather(jnp.concatenate([left, right], axis=1), ("tensor", "dp"), axis=0, tiled=True)
        full = full.reshape(2, ZS, 2, -1, full.shape[1])
        left, right = jnp.split(full, 2, axis=4)
        left = jnp.transpose(left, (0, 2, 1, 3, 4))
        right = jnp.transpose(right, (2, 0, 1, 3, 4))
        yield left, right, jnp.zeros((1,), jnp.int32)
        return
    z, x, c, y = coords()
    first = c == 0
    own = yield jnp.where(first, right, left)
    got = yield send(own, TO_CORE)
    mine = jnp.where(first, jnp.concatenate([left, got]), jnp.concatenate([got, right]))
    mine = yield mine
    got = yield [send(mine, TO_DEPTH[k]) for k in (1, 2, 3)]
    column = jnp.stack([mine, *got, mine, *got[:2]])
    column = yield lax.dynamic_slice_in_dim(column, (ZS - z) % ZS, ZS, 0)
    near = yield send(column, TO_NEAR)
    plane = yield in_order(column, near, jnp.where(first, x, y))
    far = yield send(plane, TO_FAR)
    whole = yield in_order(plane, far, jnp.where(first, y, x))
    sibling = yield send(whole, TO_CORE)
    yield whole, sibling, c.astype(jnp.int32).reshape(1)


def add(a, b):
    return a.astype(jnp.float32) + b.astype(jnp.float32)


def pick(value, at):
    return lax.dynamic_index_in_dim(value, at, 0, keepdims=False)


def scatter_steps(part):
    if not tuned():
        left = yield part(jnp.zeros((1,), jnp.int32))
        for _ in range(9):
            left = yield left
        right = part(jnp.ones((1,), jnp.int32))
        left = jnp.transpose(left, (0, 2, 1, 3, 4))
        right = jnp.transpose(right, (1, 2, 0, 3, 4))
        full = jnp.concatenate([left, right], axis=4)
        full = lax.psum_scatter(
            full.reshape(-1, full.shape[4]), ("tensor", "dp"), scatter_dimension=0, tiled=True
        )
        full = lax.optimization_barrier(full).astype(jnp.float32)
        yield tuple(jnp.split(full, 2, axis=1))
        return
    z, x, c, y = coords()
    first = c == 0
    side = c.astype(jnp.int32).reshape(1)
    other = yield part(1 - side)
    got = yield send(other, TO_CORE)
    total = low(add(part(side), got))
    at = jnp.where(first, y, x)
    away = yield pick(total, 1 - at)
    got = yield send(away, TO_FAR)
    total = low(add(pick(total, at), got))
    at = jnp.where(first, x, y)
    away = yield pick(total, 1 - at)
    got = yield send(away, TO_NEAR)
    total = low(add(pick(total, at), got))
    away = yield [pick(total, (z - k) % ZS) for k in (1, 2, 3)]
    got = yield [send(piece, TO_DEPTH[k + 1]) for k, piece in enumerate(away)]
    total = pick(total, z).astype(jnp.float32)
    for piece in got:
        total = total + piece.astype(jnp.float32)
    total = total.reshape(2, -1, total.shape[1])
    away = yield pick(total, 1 - c)
    got = yield send(away, TO_CORE)
    keep = pick(total, c)
    yield jnp.where(first, keep, got), jnp.where(first, got, keep)


def dot_nn(left, right):
    return lax.dot_general(left, right, (((1,), (0,)), ((), ())), preferred_element_type=jnp.float32)


def dot_nt(left, right):
    return lax.dot_general(left, right, (((1,), (1,)), ((), ())), preferred_element_type=jnp.float32)


def flip(value):
    return jnp.swapaxes(value, 0, 1)


def load_set(side_ref, mine_ref, other_ref, left, right, sems, only=None):
    count = mine_ref.shape[3]

    def start(left_ref, right_ref):
        for y in range(2) if only is None else (only,):
            at = y if only is None else 0
            for x in range(2):
                for z in range(ZS):
                    cut = pl.ds((z * 2 + x) * count, count)
                    pltpu.make_async_copy(left_ref.at[y, x, z], left.at[at, cut], sems.at[0]).start()
                    pltpu.make_async_copy(right_ref.at[x, y, z], right.at[at, cut], sems.at[1]).start()

    @pl.when(side_ref[0] == 0)
    def _():
        start(mine_ref, other_ref)

    @pl.when(side_ref[0] != 0)
    def _():
        start(other_ref, mine_ref)


def wait_set(left, right, sems):
    pltpu.make_async_copy(left, left, sems.at[0]).wait()
    pltpu.make_async_copy(right, right, sems.at[1]).wait()


def set_scratch(weights, count=2):
    width, cols = 8 * weights[0].shape[3], weights[0].shape[4]
    buffer = pltpu.VMEM((count, width, cols), jnp.bfloat16)
    return [buffer, buffer, pltpu.SemaphoreType.DMA((2,))]


def set_specs():
    return [
        pl.BlockSpec(memory_space=pltpu.SMEM),
        pl.BlockSpec(memory_space=pl.ANY),
        pl.BlockSpec(memory_space=pl.ANY),
    ]


def set_args(weights):
    return weights[2], weights[0], weights[1]


def params():
    return pltpu.CompilerParams(vmem_limit_bytes=VMEM)


def pair_cols(left, right, at):
    start = at * LANES
    width = left.shape[-1]
    if start < width:
        return left[:, start : start + LANES]
    return right[:, start - width : start - width + LANES]


def attend_kernel(
    t, side_ref, mine_ref, other_ref, x_ref, row_ref, col_ref,
    pa_ref, pb_ref, e_ref, att_ref, flat_ref, inv_ref, bias_ref, a_ref, b_ref, sems,
):
    pairs = flat_ref.shape[2] // LANES

    @pl.when(pl.program_id(0) == 0)
    def _():
        load_set(side_ref, mine_ref, other_ref, a_ref, b_ref, sems, t)
        wait_set(a_ref, b_ref, sems)

    x = x_ref[...]
    pa_ref[0] = low(dot_nn(x, a_ref[0]))
    pb_ref[0] = low(dot_nn(x, b_ref[0, :, : pb_ref.shape[2]]))
    bias_ref[...] = jnp.where(col_ref[0] == row_ref[0], 0.0, -1e30)
    lane = lax.broadcasted_iota(jnp.int32, (SEQ, LANES), 1)
    chunk = SEQ // 2
    left, right = pa_ref[0], pb_ref[0]
    for p in range(pairs):
        queries = pair_cols(left, right, p)
        key_rows = pair_cols(left, right, pairs + p)
        values_flat = flip(pair_cols(left, right, 2 * pairs + p))
        for half in range(2):
            h = 2 * p + half
            own = (lane < HDIM) if half == 0 else (lane >= HDIM)
            chosen = low(jnp.where(own, queries.astype(jnp.float32) * HDIM**-0.5, 0.0))
            value_half = values_flat[half * HDIM : (half + 1) * HDIM]
            for n in range(2):
                cut = slice(n * chunk, (n + 1) * chunk)
                scores = dot_nt(key_rows, chosen[cut]) + bias_ref[:, cut]
                largest = jnp.max(scores, axis=0, keepdims=True)
                weights = jnp.exp(scores - largest)
                inverse = 1.0 / jnp.sum(weights, axis=0, keepdims=True)
                weights = low(weights)
                e_ref[0, h, :, cut] = weights
                inv_ref[0, h : h + 1, cut] = inverse
                flat_ref[0, 0, h * HDIM : (h + 1) * HDIM, cut] = low(dot_nn(value_half, weights) * inverse)
        att_ref[:, p * LANES : (p + 1) * LANES] = flip(flat_ref[0, 0, p * LANES : (p + 1) * LANES, :])
    att_ref[:, pairs * LANES :] = jnp.zeros((SEQ, LANES), jnp.bfloat16)


def attend(tokens, weights, numbers, t):
    rows, width = tokens.shape
    seqs = rows // SEQ
    cols = weights[0].shape[4]
    wide = (2 * cols - LANES) // 3
    heads = wide // HDIM
    used = cols - LANES
    bf = jnp.bfloat16
    return pl.pallas_call(
        functools.partial(attend_kernel, t),
        grid=(seqs,),
        in_specs=set_specs() + [
            pl.BlockSpec((SEQ, width), lambda s: (s, 0)),
            pl.BlockSpec((1, 1, SEQ), lambda s: (s, 0, 0)),
            pl.BlockSpec((1, SEQ, 1), lambda s: (s, 0, 0)),
        ],
        out_specs=[
            pl.BlockSpec((1, SEQ, cols), lambda s: (0, s, 0)),
            pl.BlockSpec((1, SEQ, used), lambda s: (0, s, 0)),
            pl.BlockSpec((1, heads, SEQ, SEQ), lambda s: (s, 0, 0, 0)),
            pl.BlockSpec((SEQ, wide + LANES), lambda s: (s, 0)),
            pl.BlockSpec((1, 1, wide, SEQ), lambda s: (0, s, 0, 0)),
            pl.BlockSpec((1, heads, SEQ), lambda s: (s, 0, 0)),
        ],
        out_shape=[
            jax.ShapeDtypeStruct((1, rows, cols), bf),
            jax.ShapeDtypeStruct((1, rows, used), bf),
            jax.ShapeDtypeStruct((seqs, heads, SEQ, SEQ), bf),
            jax.ShapeDtypeStruct((rows, wide + LANES), bf),
            jax.ShapeDtypeStruct((1, seqs, wide, SEQ), bf),
            jax.ShapeDtypeStruct((seqs, heads, SEQ), jnp.float32),
        ],
        scratch_shapes=[pltpu.VMEM((SEQ, SEQ), jnp.float32)] + set_scratch(weights, 1),
        compiler_params=params(),
        cost_estimate=pl.CostEstimate(flops=8_000_000_000, bytes_accessed=15_000_000, transcendentals=3_100_000),
        name="attend",
    )(*set_args(weights), tokens, numbers.reshape(seqs, 1, SEQ), numbers.reshape(seqs, SEQ, 1))


def attend_back_kernel(
    t, side_ref, mine_ref, other_ref, g_ref, pa_ref, pb_ref, e_ref, flat_ref, inv_ref, d_ref, w_ref, gt_ref, sem,
):
    wide = flat_ref.shape[2]
    pairs = wide // LANES
    count = mine_ref.shape[3]

    @pl.when(pl.program_id(0) == 0)
    def _():
        def start(left_ref):
            for x in range(2):
                for z in range(ZS):
                    pltpu.make_async_copy(
                        left_ref.at[t, x, z], w_ref.at[pl.ds((z * 2 + x) * count, count)], sem
                    ).start()

        @pl.when(side_ref[0] == 0)
        def _():
            start(mine_ref)

        @pl.when(side_ref[0] != 0)
        def _():
            start(other_ref)

        pltpu.make_async_copy(w_ref, w_ref, sem).wait()

    gt_ref[...] = flip(low(dot_nn(g_ref[...], w_ref[:, :wide])))
    left, right = pa_ref[0], pb_ref[0]
    lane = lax.broadcasted_iota(jnp.int32, (SEQ, LANES), 1)
    cols = d_ref.shape[2]

    def put(at, value):
        start = at * LANES
        side = start // cols
        d_ref[side, :, start - side * cols : start - side * cols + LANES] = value

    blank = jnp.zeros((HDIM, SEQ), jnp.bfloat16)
    for p in range(pairs):
        queries = pair_cols(left, right, p)
        key_rows = pair_cols(left, right, pairs + p)
        value_rows = pair_cols(left, right, 2 * pairs + p)
        keys_flat = flip(key_rows)
        scaled = []
        for half in range(2):
            h = 2 * p + half
            grads = gt_ref[h * HDIM : (h + 1) * HDIM, :].astype(jnp.float32)
            scaled.append(low(grads * inv_ref[0, h : h + 1, :]))
        grads = flip(jnp.concatenate(scaled, axis=0))
        dq, dk, dv = [], [], []
        for half in range(2):
            h = 2 * p + half
            mine = scaled[half]
            flat = flat_ref[0, 0, h * HDIM : (h + 1) * HDIM, :].astype(jnp.float32)
            centre = jnp.sum(mine.astype(jnp.float32) * flat, axis=0, keepdims=True)
            stacked = [mine, blank] if half == 0 else [blank, mine]
            grad_weights = dot_nn(value_rows, jnp.concatenate(stacked, axis=0))
            weights = e_ref[0, h]
            grad_scores = low(weights.astype(jnp.float32) * (grad_weights - centre))
            dv.append(dot_nn(weights, grads))
            dk.append(dot_nn(grad_scores, queries))
            dq.append(dot_nn(keys_flat[half * HDIM : (half + 1) * HDIM], grad_scores))
        put(p, flip(low(jnp.concatenate(dq, axis=0) * HDIM**-0.5)))
        put(pairs + p, low(jnp.where(lane < HDIM, dk[0], dk[1]) * HDIM**-0.5))
        put(2 * pairs + p, low(jnp.where(lane < HDIM, dv[0], dv[1])))
    d_ref[1, :, cols - LANES :] = jnp.zeros((SEQ, LANES), jnp.bfloat16)


def attend_back(grad_branch, weights, kept, t):
    pa, pb, e, _, flat, inv = kept
    rows, width = grad_branch.shape
    seqs = rows // SEQ
    cols, used = pa.shape[2], pb.shape[2]
    heads, wide = e.shape[1], flat.shape[2]
    bf = jnp.bfloat16
    return pl.pallas_call(
        functools.partial(attend_back_kernel, t),
        grid=(seqs,),
        in_specs=set_specs() + [
            pl.BlockSpec((SEQ, width), lambda s: (s, 0)),
            pl.BlockSpec((1, SEQ, cols), lambda s: (0, s, 0)),
            pl.BlockSpec((1, SEQ, used), lambda s: (0, s, 0)),
            pl.BlockSpec((1, heads, SEQ, SEQ), lambda s: (s, 0, 0, 0)),
            pl.BlockSpec((1, 1, wide, SEQ), lambda s: (0, s, 0, 0)),
            pl.BlockSpec((1, heads, SEQ), lambda s: (s, 0, 0)),
        ],
        out_specs=pl.BlockSpec((2, SEQ, cols), lambda s: (0, s, 0)),
        out_shape=jax.ShapeDtypeStruct((2, rows, cols), bf),
        scratch_shapes=[
            pltpu.VMEM((width, weights[0].shape[4]), bf),
            pltpu.VMEM((wide, SEQ), bf),
            pltpu.SemaphoreType.DMA,
        ],
        compiler_params=params(),
        cost_estimate=pl.CostEstimate(flops=8_000_000_000, bytes_accessed=15_000_000, transcendentals=0),
        name="attend_back",
    )(*set_args(weights), grad_branch, pa, pb, e, flat, inv)


def gelu_parts(v):
    size = jnp.abs(v)
    base = 1.0 + (0.3275911 * 0.5**0.5) * size
    near = pl.reciprocal(base, approx=True)
    t = near * (2.0 - base * near)
    bell = jnp.exp(-0.5 * (v * v))
    tail = t * (0.127414796 + t * (-0.142248368 + t * (0.710706871 + t * (-0.7265760135 + t * 0.5307027145)))) * bell
    below = jnp.where(v >= 0.0, 1.0 - tail, tail)
    return v * below, below + 0.3989422804014327 * (v * bell)


def row_norm(value):
    centered = value - jnp.mean(value, axis=-1, keepdims=True)
    inverse = lax.rsqrt(jnp.mean(centered * centered, axis=-1, keepdims=True) + epsilon)
    return centered * inverse, inverse


def row_norm_back(grad_scaled, scaled, inverse):
    centered = grad_scaled - jnp.mean(grad_scaled, axis=-1, keepdims=True)
    return inverse * (centered - scaled * jnp.mean(grad_scaled * scaled, axis=-1, keepdims=True))


def pieces(left, right, skip):
    at = 0
    for t in range(2):
        for ref, start, end in ((left, skip, left.shape[2]), (right, 0, right.shape[2] - (LANES if skip else 0))):
            while start < end:
                size = min(CHUNK, end - start)
                yield ref.at[t, :, pl.ds(start, size)], slice(at, at + size)
                start, at = start + size, at + size


def widen_kernel(
    side_ref, mine_ref, other_ref, x_ref, u_ref, v_ref, n_ref,
    sum_ref, low_ref, hid_ref, slope_ref, left, right, sems,
):
    wide = u_ref.shape[1] - LANES

    @pl.when(pl.program_id(0) == 0)
    def _():
        load_set(side_ref, mine_ref, other_ref, left, right, sems)
        wait_set(left, right, sems)

    branch = dot_nt(u_ref[:, :wide], left[0, :, :wide]) + dot_nt(v_ref[:, :wide], left[1, :, :wide])
    total = x_ref[...].astype(jnp.float32) + branch
    sum_ref[...] = total
    scaled, _ = row_norm(total)
    x = low(scaled * n_ref[0:1, :] + n_ref[1:2, :])
    low_ref[...] = flip(x)
    for ref, cut in pieces(left, right, wide):
        value, slope = gelu_parts(dot_nn(x, ref[...]))
        hid_ref[:, cut] = low(value)
        slope_ref[:, cut] = low(slope)


def widen(tokens, attended, weights, norms, span):
    rows, width = tokens.shape
    bf = jnp.bfloat16
    by_row = lambda n: pl.BlockSpec((BLOCK, n), lambda r: (r, 0))
    full = lambda a: pl.BlockSpec(a.shape, lambda r: (0, 0))
    side = by_row(attended[0].shape[1])
    return pl.pallas_call(
        widen_kernel,
        grid=(rows // BLOCK,),
        in_specs=set_specs() + [by_row(width), side, side, full(norms)],
        out_specs=[by_row(width), pl.BlockSpec((width, BLOCK), lambda r: (0, r)), by_row(span), by_row(span)],
        out_shape=[
            jax.ShapeDtypeStruct((rows, width), jnp.float32),
            jax.ShapeDtypeStruct((width, rows), bf),
            jax.ShapeDtypeStruct((rows, span), bf),
            jax.ShapeDtypeStruct((rows, span), bf),
        ],
        scratch_shapes=set_scratch(weights),
        compiler_params=params(),
        cost_estimate=pl.CostEstimate(flops=12_000_000_000, bytes_accessed=25_000_000, transcendentals=3_100_000),
        name="widen",
    )(*set_args(weights), tokens, *attended, norms)


def middle_kernel(
    side_ref, mine_ref, other_ref, side_two_ref, mine_two_ref, other_two_ref,
    sum_ref, hid_ref, slope_ref, n_ref, cot_ref,
    out_ref, gs_ref, gi_ref, res_ref, gb_ref, gbt_ref, stat_ref,
    left, right, sems, win_left, win_right, win_sems,
):
    @pl.when(pl.program_id(0) == 0)
    def _():
        load_set(side_ref, mine_ref, other_ref, left, right, sems)
        load_set(side_two_ref, mine_two_ref, other_two_ref, win_left, win_right, win_sems)
        wait_set(left, right, sems)

    gain_one, shift_one = n_ref[0:1, :], n_ref[1:2, :]
    gain_two, shift_two = n_ref[2:3, :], n_ref[3:4, :]
    scaled_one, inverse_one = row_norm(sum_ref[...])
    value = scaled_one * gain_one + shift_one
    half = left.shape[2]
    for t in range(2):
        for i, ref in enumerate((left, right)):
            start = (2 * t + i) * half
            value = value + dot_nt(hid_ref[:, start : start + half], ref[t])
    scaled_two, inverse_two = row_norm(value)
    out_ref[...] = low(scaled_two * gain_two + shift_two)
    cotangent = cot_ref[...].astype(jnp.float32)
    grad_two = row_norm_back(cotangent * gain_two, scaled_two, inverse_two)
    grad_second = low(grad_two)
    gs_ref[...] = flip(grad_second)
    for ref, cut in pieces(left, right, 0):
        gi_ref[:, cut] = low(dot_nn(grad_second, ref[...]) * slope_ref[:, cut].astype(jnp.float32))

    @pl.when(pl.program_id(0) == 0)
    def _():
        wait_set(win_left, win_right, win_sems)
        stat_ref[...] = jnp.zeros_like(stat_ref)

    grad_first = grad_two
    skip = 2 * win_left.shape[2] - LANES - gi_ref.shape[1] // 2
    at = 0
    for t in range(2):
        for ref, start, end in ((win_left, skip, win_left.shape[2]), (win_right, 0, win_right.shape[2] - LANES)):
            grad_first = grad_first + dot_nt(gi_ref[:, at : at + end - start], ref[t, :, start:end])
            at += end - start
    grad_one = row_norm_back(grad_first * gain_one, scaled_one, inverse_one)
    res_ref[...] = grad_one
    gb_ref[...] = low(grad_one)
    gbt_ref[...] = flip(low(grad_one))
    for row, value in enumerate((grad_first * scaled_one, grad_first, cotangent * scaled_two, cotangent)):
        stat_ref[row : row + 1, :] += jnp.sum(value, axis=0, keepdims=True)


def middle(total, hidden, slope, weights_down, weights_in, norms, cotangent):
    rows, width = total.shape
    span = hidden.shape[1]
    bf = jnp.bfloat16
    by_row = lambda n: pl.BlockSpec((BLOCK, n), lambda r: (r, 0))
    by_col = pl.BlockSpec((width, BLOCK), lambda r: (0, r))
    full = lambda a: pl.BlockSpec(a.shape, lambda r: (0, 0))
    return pl.pallas_call(
        middle_kernel,
        grid=(rows // BLOCK,),
        in_specs=set_specs() * 2 + [by_row(width), by_row(span), by_row(span), full(norms), by_row(width)],
        out_specs=[by_row(width), by_col, by_row(span), by_row(width), by_row(width), by_col, full(norms)],
        out_shape=[
            jax.ShapeDtypeStruct((rows, width), bf),
            jax.ShapeDtypeStruct((width, rows), bf),
            jax.ShapeDtypeStruct((rows, span), bf),
            jax.ShapeDtypeStruct((rows, width), jnp.float32),
            jax.ShapeDtypeStruct((rows, width), bf),
            jax.ShapeDtypeStruct((width, rows), bf),
            jax.ShapeDtypeStruct(norms.shape, jnp.float32),
        ],
        scratch_shapes=set_scratch(weights_down) + set_scratch(weights_in),
        compiler_params=params(),
        cost_estimate=pl.CostEstimate(flops=22_000_000_000, bytes_accessed=40_000_000, transcendentals=0),
        name="middle",
    )(*set_args(weights_down), *set_args(weights_in), total, hidden, slope, norms, cotangent)


def put_rows(out_ref, side, t, value, cut):
    count = out_ref.shape[3]
    for x in range(2):
        a = jnp.where(side == 0, t, x)
        b = jnp.where(side == 0, x, t)
        for z in range(ZS):
            start = (z * 2 + x) * count
            out_ref[a, b, z, :, cut] = value[start : start + count]


def weigh_kernel(side_ref, a_ref, b_ref, out_ref):
    side, t = side_ref[0], pl.program_id(0)
    put_rows(out_ref, side, t, low(dot_nn(a_ref[...], b_ref[...])), slice(None))


def weigh_more_kernel(side_ref, a_ref, b_ref, c_ref, u_ref, v_ref, out_ref):
    side, t = side_ref[0], pl.program_id(0)
    cols = b_ref.shape[1]
    put_rows(out_ref, side, t, low(dot_nn(a_ref[...], b_ref[...])), slice(0, cols))
    chosen = jnp.where(t == 0, u_ref[...], v_ref[...])
    put_rows(out_ref, side, t, low(dot_nn(c_ref[...], chosen)), slice(cols, out_ref.shape[4]))


def weigh_last_kernel(side_ref, a_ref, u_ref, v_ref, s_ref, out_ref):
    side, t = side_ref[0], pl.program_id(0)
    chosen = jnp.where(t == 0, u_ref[0], v_ref[0])
    value = low(dot_nn(a_ref[...], chosen))
    edge = out_ref.shape[4] - LANES
    put_rows(out_ref, side, t, value[:, :edge], slice(0, edge))
    put_rows(out_ref, side, t, jnp.where(side == 0, value[:, edge:], s_ref[...]), slice(edge, edge + LANES))


def weigh_call(kernel, specs, cols, flops, side, *args):
    width = args[0].shape[0]
    shape = (2, 2, ZS, width // (2 * ZS), cols)
    return pl.pallas_call(
        kernel,
        grid_spec=pltpu.PrefetchScalarGridSpec(
            num_scalar_prefetch=1,
            grid=(2,),
            in_specs=specs,
            out_specs=pl.BlockSpec(shape, lambda t, side: (0, 0, 0, 0, 0)),
        ),
        out_shape=jax.ShapeDtypeStruct(shape, jnp.bfloat16),
        compiler_params=params(),
        cost_estimate=pl.CostEstimate(flops=flops, bytes_accessed=8_000_000, transcendentals=0),
        name="weigh",
    )(side, *args)


def whole_spec(value):
    return pl.BlockSpec(value.shape, lambda t, side: (0,) * value.ndim)


def weigh(flat, value, side):
    cols = value.shape[1] // 4
    specs = [whole_spec(flat), pl.BlockSpec((value.shape[0], cols), lambda t, side: (0, 2 * t + side[0]))]
    return weigh_call(weigh_kernel, specs, cols, 2_500_000_000, side, flat, value)


def weigh_more(flat, value, flat_two, attended, side):
    cols = value.shape[1] // 4
    more = attended[0].shape[1] // 2
    extra = pl.BlockSpec((value.shape[0], more), lambda t, side: (0, side[0]))
    specs = [
        whole_spec(flat),
        pl.BlockSpec((value.shape[0], cols), lambda t, side: (0, 2 * t + side[0])),
        whole_spec(flat_two), extra, extra,
    ]
    return weigh_call(
        weigh_more_kernel, specs, cols + more, 3_500_000_000, side, flat, value, flat_two, *attended
    )


def weigh_last(flat, parts, stats, side):
    _, rows, cols = parts[0].shape
    spec = pl.BlockSpec((1, rows, cols), lambda t, side: (side[0], 0, 0))
    specs = [whole_spec(flat), spec, spec, whole_spec(stats)]
    return weigh_call(weigh_last_kernel, specs, cols, 2_500_000_000, side, flat, *parts, stats)


def input_kernel(side_ref, mine_ref, other_ref, res_ref, u_ref, v_ref, out_ref, left, right, sems):
    @pl.when(pl.program_id(0) == 0)
    def _():
        load_set(side_ref, mine_ref, other_ref, left, right, sems)
        wait_set(left, right, sems)

    total = res_ref[...]
    for t, ref in enumerate((u_ref, v_ref)):
        total = total + dot_nt(ref[0], left[t]) + dot_nt(ref[1], right[t])
    out_ref[...] = low(total)


def input_back(resid, parts, weights):
    rows, width = resid.shape
    cols = parts[0].shape[2]
    by_row = pl.BlockSpec((BLOCK, width), lambda r: (r, 0))
    side = pl.BlockSpec((2, BLOCK, cols), lambda r: (0, r, 0))
    return pl.pallas_call(
        input_kernel,
        grid=(rows // BLOCK,),
        in_specs=set_specs() + [by_row, side, side],
        out_specs=by_row,
        out_shape=jax.ShapeDtypeStruct((rows, width), jnp.bfloat16),
        scratch_shapes=set_scratch(weights),
        compiler_params=params(),
        cost_estimate=pl.CostEstimate(flops=4_000_000_000, bytes_accessed=14_000_000, transcendentals=0),
        name="input_back",
    )(*set_args(weights), resid, *parts)


def halves(value):
    return jnp.split(value, 2, axis=-1)


def shards(
    tokens,
    segment,
    weight_qkv,
    weight_out,
    weight_in,
    weight_down,
    gain_one,
    shift_one,
    gain_two,
    shift_two,
    cotangent,
):
    rows, width = tokens.shape
    own = weight_qkv.shape[1]
    wide = weight_out.shape[0]
    half_span = weight_in.shape[1]
    bf = jnp.bfloat16

    norms = jnp.stack([gain_one, shift_one, gain_two, shift_two], axis=1)
    norms = jnp.pad(norms, ((0, 0), (0, LANES - 4)))
    set_one = jnp.concatenate([jnp.transpose(weight_qkv, (1, 0, 2)).reshape(own, -1), norms], axis=1)
    set_two = jnp.concatenate([weight_out.T, weight_in, jnp.zeros((own, LANES), bf)], axis=1)
    one = Flow(gather_steps(*halves(set_one)))
    two = Flow(gather_steps(*halves(set_two)))
    three = Flow(gather_steps(*halves(weight_down.T)))
    one.go(2)
    two.go(2)
    three.go(2)
    one.go()
    column = one.go()
    one.go()
    two.after(column)
    two.go()
    one.go()
    one.go()
    three.after(two.go())
    three.go()
    whole = one.go()
    one.go()
    two.after(whole)
    wait_two = two.value
    two.go()
    wait_three = three.go()
    three.after(whole)
    three.go()
    weights_one = one.go()
    first_mine, first_other, first_side = weights_one
    norms = jnp.where(first_side[0] == 0, first_other, first_mine)[:, 0, :, :, first_mine.shape[4] - LANES :]
    norms = jnp.transpose(norms, (1, 0, 2, 3)).reshape(width, LANES)[:, :8].T.astype(jnp.float32)

    numbers = lax.dynamic_slice_in_dim(segment, lax.axis_index("tensor") * rows, rows)
    numbers = numbers.reshape(rows // SEQ, SEQ)
    kept = [attend(after(tokens, wait_two, wait_three), weights_one, numbers, 0)]
    two.after(kept[0])
    plane = two.go()
    two.go()
    three.after(kept[0])
    kept.append(attend(after(tokens, plane, kept[0][3]), weights_one, numbers, 1))
    two.after(kept[1])
    whole = two.go()
    two.go()
    three.go()
    three.after(whole)
    three.go()
    weights_two = two.go()
    attended = [kept[t][3] for t in range(2)]
    total, low_flat, hidden, slope = widen(tokens, attended, weights_two, norms, 2 * half_span)
    three.after(hidden)
    three.go(2)
    weights_three = three.go()
    output, second_flat, grad_inner, grad_resid_one, grad_branch, branch_flat, stats = middle(
        total, hidden, slope, weights_three, weights_two, norms, cotangent
    )

    put_three = Flow(scatter_steps(lambda side: weigh(second_flat, hidden, side)))
    ready = put_three.value
    put_three.go()
    low_flat = after(low_flat, ready)
    put_two = Flow(scatter_steps(lambda side: weigh_more(low_flat, grad_inner, branch_flat, attended, side)))
    put_two.go()
    put_three.go()
    put_three.go()
    ready = put_two.go()
    put_two.go()
    parts = [attend_back(after(grad_branch, ready), weights_two, kept[0], 0)]
    put_three.after(parts[0])
    ready = put_three.go()
    put_three.go()
    parts.append(attend_back(after(grad_branch, ready), weights_two, kept[1], 1))
    put_two.after(parts[1])
    put_three.after(parts[1])
    ready = put_two.go()
    put_two.go()
    put_three.go()
    put_three.go()
    tokens_flat = after(tokens.T, ready)
    stats = jnp.pad(low(stats.T), ((0, 0), (0, LANES - stats.shape[0])))
    put_one = Flow(scatter_steps(lambda side: weigh_last(tokens_flat, parts, stats, side)))
    put_one.go()
    ready = put_one.go()
    put_one.go()
    put_two.after(ready)
    put_two.go()
    put_two.go()
    input_grad = input_back(after(grad_resid_one, ready), parts, weights_one)
    put_three.after(ready)
    put_three.go(2)
    put_one.after(input_grad)
    put_one.go()
    put_one.go()
    put_one.go()
    put_one.go()
    put_two.go(2)
    put_one.go(2)
    sum_one = jnp.concatenate(put_one.go(), axis=1)
    two_left, two_right = put_two.go()
    sum_three = jnp.concatenate(put_three.go(), axis=1)
    half = half_span // 2
    stats = sum_one[:, 3 * wide : 3 * wide + 4].T
    sum_out = jnp.concatenate([two_left[:, half:], two_right[:, half:]], axis=1)[:, :wide]
    return (
        output,
        input_grad,
        jnp.transpose(sum_one[:, : 3 * wide].reshape(own, 3, -1), (1, 0, 2)),
        sum_out.T,
        jnp.concatenate([two_left[:, :half], two_right[:, :half]], axis=1),
        sum_three.T,
        stats[0],
        stats[1],
        stats[2],
        stats[3],
    )


def solution(mesh):
    both = P(("dp", "tensor"), None)
    split = P("dp")
    qkv_spec = P(None, "dp", "tensor")
    row_spec = P("tensor", "dp")
    in_spec = P("dp", "tensor")
    return jax.shard_map(
        shards,
        mesh=mesh,
        in_specs=(both, split, qkv_spec, row_spec, in_spec, row_spec, split, split, split, split, both),
        out_specs=(both, both, qkv_spec, row_spec, in_spec, row_spec, split, split, split, split),
        check_vma=False,
    )
```

```python
import functools

import jax
import jax.numpy as jnp
from jax import lax
from jax.experimental import pallas as pl
from jax.experimental.pallas import tpu as pltpu
from jax.sharding import PartitionSpec as P

HDIM = 64
SEQ = 512
LANES = 128
BLOCK = 256
CHUNK = 256
VMEM = 56 * 1024 * 1024
epsilon = 1e-05
SMALL = pl.CostEstimate(flops=100_000_000, bytes_accessed=100_000, transcendentals=0)


def low(value):
    return value.astype(jnp.bfloat16)


AXES = ("dp", "tensor")
ZS = 4


def place(z, x, c, y):
    return ((z * 2 + x) * 2 + c) * 2 + y


def pairs(move):
    found = []
    for z in range(ZS):
        for x in range(2):
            for c in range(2):
                for y in range(2):
                    found.append((place(z, x, c, y), place(*move(z, x, c, y))))
    return found


TO_CORE = pairs(lambda z, x, c, y: (z, x, 1 - c, y))
TO_NEAR = pairs(lambda z, x, c, y: (z, x, c, 1 - y) if c else (z, 1 - x, c, y))
TO_FAR = pairs(lambda z, x, c, y: (z, 1 - x, c, y) if c else (z, x, c, 1 - y))
TO_DEPTH = [pairs(lambda z, x, c, y: ((z - k) % ZS, x, c, y)) for k in range(ZS)]


def coords():
    d = lax.axis_index("dp")
    y = lax.axis_index("tensor")
    return d // 4, (d // 2) % 2, d % 2, y


def send(value, route):
    return lax.ppermute(value, AXES, route)


def in_order(own, other, at):
    return jnp.where(at == 0, jnp.stack([own, other]), jnp.stack([other, own]))


def tuned():
    return lax.axis_size("dp") == 16 and lax.axis_size("tensor") == 2


def sync(*values):
    found = lax.optimization_barrier([value.value if isinstance(value, Flow) else value for value in values])
    for value, new in zip(values, found):
        if isinstance(value, Flow):
            value.value = new
    found = [new for value, new in zip(values, found) if not isinstance(value, Flow)]
    return found[0] if len(found) == 1 else found


def hold(pieces, *values):
    if not isinstance(pieces, list):
        return pieces
    return [*pieces[:-1], sync(pieces[-1], *values)]


class Flow:
    def __init__(self, steps):
        self.steps = steps
        self.value = next(steps)

    def go(self, count=1):
        for _ in range(count):
            self.value = self.steps.send(self.value)
        return self.value


def gather_steps(left, right):
    if not tuned():
        for _ in range(10):
            left = yield left
        full = lax.all_gather(jnp.concatenate([left, right], axis=1), ("tensor", "dp"), axis=0, tiled=True)
        full = full.reshape(2, ZS, 2, -1, full.shape[1])
        left, right = jnp.split(full, 2, axis=4)
        left = jnp.transpose(left, (0, 2, 1, 3, 4))
        right = jnp.transpose(right, (2, 0, 1, 3, 4))
        yield left, right, jnp.zeros((1,), jnp.int32)
        return
    z, x, c, y = coords()
    first = c == 0
    own = yield jnp.where(first, right, left)
    got = yield send(own, TO_CORE)
    mine = jnp.where(first, jnp.concatenate([left, got]), jnp.concatenate([got, right]))
    mine = yield mine
    got = yield [send(mine, TO_DEPTH[k]) for k in (1, 2, 3)]
    column = jnp.stack([mine, *got, mine, *got[:2]])
    column = yield lax.dynamic_slice_in_dim(column, (ZS - z) % ZS, ZS, 0)
    near = yield send(column, TO_NEAR)
    plane = yield in_order(column, near, jnp.where(first, x, y))
    far = yield send(plane, TO_FAR)
    whole = yield in_order(plane, far, jnp.where(first, y, x))
    sibling = yield send(whole, TO_CORE)
    yield whole, sibling, c.astype(jnp.int32).reshape(1)


def add(a, b):
    return a.astype(jnp.float32) + b.astype(jnp.float32)


def pick(value, at):
    return lax.dynamic_index_in_dim(value, at, 0, keepdims=False)


def scatter_steps(part):
    if not tuned():
        left = yield part(jnp.array([0, 0], jnp.int32), None)
        for _ in range(9):
            left = yield left
        right = part(jnp.array([1, 0], jnp.int32), None)
        left = jnp.transpose(left, (0, 2, 1, 3, 4))
        right = jnp.transpose(right, (1, 2, 0, 3, 4))
        full = jnp.concatenate([left, right], axis=4)
        full = lax.psum_scatter(
            full.reshape(-1, full.shape[4]), ("tensor", "dp"), scatter_dimension=0, tiled=True
        )
        full = lax.optimization_barrier(full).astype(jnp.float32)
        yield tuple(jnp.split(full, 2, axis=1))
        return
    z, x, c, y = coords()
    first = c == 0
    at = jnp.where(first, y, x)
    other = yield part(jnp.stack([1 - c, at]).astype(jnp.int32), None)
    got = yield send(other, TO_CORE)
    stay, away = part(jnp.stack([c, at]).astype(jnp.int32), got)
    away = yield away
    got = yield send(away, TO_FAR)
    total = low(add(stay, got))
    at = jnp.where(first, x, y)
    away = yield pick(total, 1 - at)
    got = yield send(away, TO_NEAR)
    total = low(add(pick(total, at), got))
    away = yield [pick(total, (z - k) % ZS) for k in (1, 2, 3)]
    got = yield [send(piece, TO_DEPTH[k + 1]) for k, piece in enumerate(away)]
    total = pick(total, z).astype(jnp.float32)
    for piece in got:
        total = total + piece.astype(jnp.float32)
    total = total.reshape(2, -1, total.shape[1])
    away = yield pick(total, 1 - c)
    got = yield send(away, TO_CORE)
    keep = pick(total, c)
    yield jnp.where(first, keep, got), jnp.where(first, got, keep)


def dot_nn(left, right):
    return lax.dot_general(left, right, (((1,), (0,)), ((), ())), preferred_element_type=jnp.float32)


def dot_nt(left, right):
    return lax.dot_general(left, right, (((1,), (1,)), ((), ())), preferred_element_type=jnp.float32)


def flip(value):
    return jnp.swapaxes(value, 0, 1)


def load_set(side_ref, mine_ref, other_ref, left, right, sems, only=None):
    count = mine_ref.shape[3]

    def start(left_ref, right_ref):
        for y in range(2) if only is None else (only,):
            at = y if only is None else 0
            for x in range(2):
                for z in range(ZS):
                    cut = pl.ds((z * 2 + x) * count, count)
                    pltpu.make_async_copy(left_ref.at[y, x, z], left.at[at, cut], sems.at[0]).start()
                    pltpu.make_async_copy(right_ref.at[x, y, z], right.at[at, cut], sems.at[1]).start()

    @pl.when(side_ref[0] == 0)
    def _():
        start(mine_ref, other_ref)

    @pl.when(side_ref[0] != 0)
    def _():
        start(other_ref, mine_ref)


def wait_set(left, right, sems):
    pltpu.make_async_copy(left, left, sems.at[0]).wait()
    pltpu.make_async_copy(right, right, sems.at[1]).wait()


def set_scratch(weights, count=2):
    width, cols = 8 * weights[0].shape[3], weights[0].shape[4]
    buffer = pltpu.VMEM((count, width, cols), jnp.bfloat16)
    return [buffer, buffer, pltpu.SemaphoreType.DMA((2,))]


def set_specs():
    return [
        pl.BlockSpec(memory_space=pltpu.SMEM),
        pl.BlockSpec(memory_space=pl.ANY),
        pl.BlockSpec(memory_space=pl.ANY),
    ]


def set_args(weights):
    return weights[2], weights[0], weights[1]


def params():
    return pltpu.CompilerParams(vmem_limit_bytes=VMEM)


def pair_cols(left, right, at):
    start = at * LANES
    width = left.shape[-1]
    if start < width:
        return left[:, start : start + LANES]
    return right[:, start - width : start - width + LANES]


def by_head(value):
    lane = lax.broadcasted_iota(jnp.int32, value.shape, 1)
    blank = jnp.zeros_like(value)
    return jnp.concatenate([jnp.where(lane < HDIM, value, blank), jnp.where(lane < HDIM, blank, value)], axis=0)


def own_heads(value):
    return jnp.concatenate([value[:HDIM, :SEQ], value[HDIM:, SEQ:]], axis=0)


def attend_kernel(t, carried, side_ref, mine_ref, other_ref, x_ref, row_ref, col_ref, *refs):
    pa_ref, pb_ref, e_ref, att_ref, flat_ref, inv_ref, bias_ref, a_ref, b_ref, sems = refs[carried:]
    pairs = flat_ref.shape[2] // LANES
    load_set(side_ref, mine_ref, other_ref, a_ref, b_ref, sems, t)
    wait_set(a_ref, b_ref, sems)

    x = x_ref[...]
    pa_ref[0] = low(dot_nn(x, a_ref[0]))
    pb_ref[0] = low(dot_nn(x, b_ref[0, :, : pb_ref.shape[2]]))
    bias = jnp.where(col_ref[0, :, :1] == row_ref[0], 0.0, -1e30)
    bias_ref[:, :SEQ] = bias
    bias_ref[:, SEQ:] = bias
    left, right = pa_ref[0], pb_ref[0]
    for p in range(pairs):
        queries = by_head(low(pair_cols(left, right, p).astype(jnp.float32) * HDIM**-0.5))
        key_rows = pair_cols(left, right, pairs + p)
        values_flat = flip(pair_cols(left, right, 2 * pairs + p))
        scores = dot_nt(key_rows, queries) + bias_ref[...]
        weights = jnp.exp(scores - jnp.max(scores, axis=0, keepdims=True))
        inverse = 1.0 / jnp.sum(weights, axis=0, keepdims=True)
        weights = low(weights)
        e_ref[0, p] = weights
        inv_ref[0, p : p + 1, :] = inverse
        flat = low(own_heads(dot_nn(values_flat, weights) * inverse))
        flat_ref[0, 0, p * LANES : (p + 1) * LANES, :] = flat
        att_ref[:, p * LANES : (p + 1) * LANES] = flip(flat)
    att_ref[:, pairs * LANES :] = jnp.zeros((SEQ, LANES), jnp.bfloat16)


def attend(tokens, weights, numbers, t, s, carry=()):
    rows, width = tokens.shape
    seqs = rows // SEQ
    cols = weights[0].shape[4]
    wide = (2 * cols - LANES) // 3
    pairs = wide // LANES
    used = cols - LANES
    bf = jnp.bfloat16
    at = lambda *index: (lambda i: index)
    return pl.pallas_call(
        functools.partial(attend_kernel, t, len(carry)),
        grid=(1,),
        in_specs=set_specs() + [
            pl.BlockSpec((SEQ, width), at(s, 0)),
            pl.BlockSpec((1, 1, SEQ), at(s, 0, 0)),
            pl.BlockSpec((1, SEQ, LANES), at(s, 0, 0)),
        ] + [pl.BlockSpec(memory_space=pl.ANY)] * len(carry),
        out_specs=[
            pl.BlockSpec((1, SEQ, cols), at(0, s, 0)),
            pl.BlockSpec((1, SEQ, used), at(0, s, 0)),
            pl.BlockSpec((1, pairs, SEQ, 2 * SEQ), at(s, 0, 0, 0)),
            pl.BlockSpec((SEQ, wide + LANES), at(s, 0)),
            pl.BlockSpec((1, 1, wide, SEQ), at(0, s, 0, 0)),
            pl.BlockSpec((1, pairs, 2 * SEQ), at(s, 0, 0)),
        ],
        out_shape=[
            jax.ShapeDtypeStruct((1, rows, cols), bf),
            jax.ShapeDtypeStruct((1, rows, used), bf),
            jax.ShapeDtypeStruct((seqs, pairs, SEQ, 2 * SEQ), bf),
            jax.ShapeDtypeStruct((rows, wide + LANES), bf),
            jax.ShapeDtypeStruct((1, seqs, wide, SEQ), bf),
            jax.ShapeDtypeStruct((seqs, pairs, 2 * SEQ), jnp.float32),
        ],
        input_output_aliases={6 + i: i for i in range(len(carry))},
        scratch_shapes=[pltpu.VMEM((SEQ, 2 * SEQ), jnp.float32)] + set_scratch(weights, 1),
        compiler_params=params(),
        cost_estimate=SMALL,
        name="attend",
    )(*set_args(weights), tokens, *numbers, *carry)


def attend_back_kernel(
    t, side_ref, mine_ref, other_ref, g_ref, pa_ref, pb_ref, e_ref, flat_ref, inv_ref, d_ref, w_ref, gt_ref, sem,
):
    wide = flat_ref.shape[2]
    pairs = wide // LANES
    count = mine_ref.shape[3]

    @pl.when(pl.program_id(0) == 0)
    def _():
        def start(left_ref):
            for x in range(2):
                for z in range(ZS):
                    pltpu.make_async_copy(
                        left_ref.at[t, x, z], w_ref.at[pl.ds((z * 2 + x) * count, count)], sem
                    ).start()

        @pl.when(side_ref[0] == 0)
        def _():
            start(mine_ref)

        @pl.when(side_ref[0] != 0)
        def _():
            start(other_ref)

        pltpu.make_async_copy(w_ref, w_ref, sem).wait()

    gt_ref[...] = flip(low(dot_nn(g_ref[...], w_ref[:, :wide])))
    left, right = pa_ref[0], pb_ref[0]
    cols = d_ref.shape[2]

    def put(at, value):
        start = at * LANES
        side = start // cols
        d_ref[side, :, start - side * cols : start - side * cols + LANES] = value

    blank = jnp.zeros((HDIM, SEQ), jnp.bfloat16)
    for p in range(pairs):
        queries = by_head(pair_cols(left, right, p))
        keys_flat = flip(pair_cols(left, right, pairs + p))
        value_rows = pair_cols(left, right, 2 * pairs + p)
        flat = flat_ref[0, 0, p * LANES : (p + 1) * LANES, :].astype(jnp.float32)
        scaled, centre = [], []
        for half in range(2):
            rows = slice(half * HDIM, (half + 1) * HDIM)
            grads = gt_ref[p * LANES + half * HDIM : p * LANES + (half + 1) * HDIM, :].astype(jnp.float32)
            scaled.append(low(grads * inv_ref[0, p : p + 1, half * SEQ : (half + 1) * SEQ]))
            centre.append(jnp.sum(scaled[half].astype(jnp.float32) * flat[rows], axis=0, keepdims=True))
        grads = jnp.concatenate(
            [jnp.concatenate([scaled[0], blank], axis=0), jnp.concatenate([blank, scaled[1]], axis=0)], axis=1
        )
        weights = e_ref[0, p]
        grad_weights = dot_nn(value_rows, grads) - jnp.concatenate(centre, axis=1)
        grad_scores = low(weights.astype(jnp.float32) * grad_weights)
        put(p, flip(low(own_heads(dot_nn(keys_flat, grad_scores)) * HDIM**-0.5)))
        put(pairs + p, low(dot_nn(grad_scores, queries) * HDIM**-0.5))
        put(2 * pairs + p, low(dot_nn(weights, flip(grads))))
    d_ref[1, :, cols - LANES :] = jnp.zeros((SEQ, LANES), jnp.bfloat16)


def attend_back(grad_branch, weights, kept, t):
    pa, pb, e, _, flat, inv = kept
    rows, width = grad_branch.shape
    seqs = rows // SEQ
    cols, used = pa.shape[2], pb.shape[2]
    wide = flat.shape[2]
    bf = jnp.bfloat16
    return pl.pallas_call(
        functools.partial(attend_back_kernel, t),
        grid=(seqs,),
        in_specs=set_specs() + [
            pl.BlockSpec((SEQ, width), lambda s: (s, 0)),
            pl.BlockSpec((1, SEQ, cols), lambda s: (0, s, 0)),
            pl.BlockSpec((1, SEQ, used), lambda s: (0, s, 0)),
            pl.BlockSpec((1,) + e.shape[1:], lambda s: (s, 0, 0, 0)),
            pl.BlockSpec((1, 1, wide, SEQ), lambda s: (0, s, 0, 0)),
            pl.BlockSpec((1,) + inv.shape[1:], lambda s: (s, 0, 0)),
        ],
        out_specs=pl.BlockSpec((2, SEQ, cols), lambda s: (0, s, 0)),
        out_shape=jax.ShapeDtypeStruct((2, rows, cols), bf),
        scratch_shapes=[
            pltpu.VMEM((width, weights[0].shape[4]), bf),
            pltpu.VMEM((wide, SEQ), bf),
            pltpu.SemaphoreType.DMA,
        ],
        compiler_params=params(),
        cost_estimate=SMALL,
        name="attend_back",
    )(*set_args(weights), grad_branch, pa, pb, e, flat, inv)


def gelu_parts(v):
    below = 0.5 + 0.5 * lax.erf(v * 0.5**0.5)
    bell = jnp.exp(-0.5 * (v * v))
    return v * below, below + (0.3989422804014327 * v) * bell


def row_norm(value):
    centered = value - jnp.mean(value, axis=-1, keepdims=True)
    inverse = lax.rsqrt(jnp.mean(centered * centered, axis=-1, keepdims=True) + epsilon)
    return centered * inverse, inverse


def row_norm_back(grad_scaled, scaled, inverse):
    centered = grad_scaled - jnp.mean(grad_scaled, axis=-1, keepdims=True)
    return inverse * (centered - scaled * jnp.mean(grad_scaled * scaled, axis=-1, keepdims=True))


def pieces(left, right, skip):
    at = 0
    for t in range(2):
        for ref, start, end in ((left, skip, left.shape[2]), (right, 0, right.shape[2] - (LANES if skip else 0))):
            while start < end:
                size = min(CHUNK, end - start)
                yield ref.at[t, :, pl.ds(start, size)], slice(at, at + size)
                start, at = start + size, at + size


def widen_kernel(
    side_ref, mine_ref, other_ref, x_ref, u_ref, v_ref, n_ref,
    sum_ref, low_ref, hid_ref, slope_ref, left, right, sems,
):
    wide = u_ref.shape[1] - LANES

    @pl.when(pl.program_id(0) == 0)
    def _():
        load_set(side_ref, mine_ref, other_ref, left, right, sems)
        wait_set(left, right, sems)

    branch = dot_nt(u_ref[:, :wide], left[0, :, :wide]) + dot_nt(v_ref[:, :wide], left[1, :, :wide])
    total = x_ref[...].astype(jnp.float32) + branch
    sum_ref[...] = total
    scaled, _ = row_norm(total)
    x = low(scaled * n_ref[0:1, :] + n_ref[1:2, :])
    low_ref[...] = flip(x)
    for ref, cut in pieces(left, right, wide):
        value, slope = gelu_parts(dot_nn(x, ref[...]))
        hid_ref[:, cut] = low(value)
        slope_ref[:, cut] = low(slope)


def widen(tokens, attended, weights, norms, span):
    rows, width = tokens.shape
    bf = jnp.bfloat16
    by_row = lambda n: pl.BlockSpec((BLOCK, n), lambda r: (r, 0))
    full = lambda a: pl.BlockSpec(a.shape, lambda r: (0, 0))
    side = by_row(attended[0].shape[1])
    return pl.pallas_call(
        widen_kernel,
        grid=(rows // BLOCK,),
        in_specs=set_specs() + [by_row(width), side, side, full(norms)],
        out_specs=[by_row(width), pl.BlockSpec((width, BLOCK), lambda r: (0, r)), by_row(span), by_row(span)],
        out_shape=[
            jax.ShapeDtypeStruct((rows, width), jnp.float32),
            jax.ShapeDtypeStruct((width, rows), bf),
            jax.ShapeDtypeStruct((rows, span), bf),
            jax.ShapeDtypeStruct((rows, span), bf),
        ],
        scratch_shapes=set_scratch(weights),
        compiler_params=params(),
        cost_estimate=SMALL,
        name="widen",
    )(*set_args(weights), tokens, *attended, norms)


def middle_kernel(
    side_ref, mine_ref, other_ref, side_two_ref, mine_two_ref, other_two_ref,
    sum_ref, hid_ref, slope_ref, n_ref, cot_ref,
    out_ref, gs_ref, gi_ref, res_ref, gb_ref, gbt_ref, stat_ref,
    left, right, sems, win_left, win_right, win_sems,
):
    @pl.when(pl.program_id(0) == 0)
    def _():
        load_set(side_ref, mine_ref, other_ref, left, right, sems)
        load_set(side_two_ref, mine_two_ref, other_two_ref, win_left, win_right, win_sems)
        wait_set(left, right, sems)

    gain_one, shift_one = n_ref[0:1, :], n_ref[1:2, :]
    gain_two, shift_two = n_ref[2:3, :], n_ref[3:4, :]
    scaled_one, inverse_one = row_norm(sum_ref[...])
    value = scaled_one * gain_one + shift_one
    half = left.shape[2]
    for t in range(2):
        for i, ref in enumerate((left, right)):
            start = (2 * t + i) * half
            value = value + dot_nt(hid_ref[:, start : start + half], ref[t])
    scaled_two, inverse_two = row_norm(value)
    out_ref[...] = low(scaled_two * gain_two + shift_two)
    cotangent = cot_ref[...].astype(jnp.float32)
    grad_two = row_norm_back(cotangent * gain_two, scaled_two, inverse_two)
    grad_second = low(grad_two)
    gs_ref[...] = flip(grad_second)
    for ref, cut in pieces(left, right, 0):
        gi_ref[:, cut] = low(dot_nn(grad_second, ref[...]) * slope_ref[:, cut].astype(jnp.float32))

    @pl.when(pl.program_id(0) == 0)
    def _():
        wait_set(win_left, win_right, win_sems)
        stat_ref[...] = jnp.zeros_like(stat_ref)

    grad_first = grad_two
    skip = 2 * win_left.shape[2] - LANES - gi_ref.shape[1] // 2
    at = 0
    for t in range(2):
        for ref, start, end in ((win_left, skip, win_left.shape[2]), (win_right, 0, win_right.shape[2] - LANES)):
            grad_first = grad_first + dot_nt(gi_ref[:, at : at + end - start], ref[t, :, start:end])
            at += end - start
    grad_one = row_norm_back(grad_first * gain_one, scaled_one, inverse_one)
    res_ref[...] = grad_one
    gb_ref[...] = low(grad_one)
    gbt_ref[...] = flip(low(grad_one))
    for row, value in enumerate((grad_first * scaled_one, grad_first, cotangent * scaled_two, cotangent)):
        stat_ref[row : row + 1, :] += jnp.sum(value, axis=0, keepdims=True)


def middle(total, hidden, slope, weights_down, weights_in, norms, cotangent):
    rows, width = total.shape
    span = hidden.shape[1]
    bf = jnp.bfloat16
    by_row = lambda n: pl.BlockSpec((BLOCK, n), lambda r: (r, 0))
    by_col = pl.BlockSpec((width, BLOCK), lambda r: (0, r))
    full = lambda a: pl.BlockSpec(a.shape, lambda r: (0, 0))
    return pl.pallas_call(
        middle_kernel,
        grid=(rows // BLOCK,),
        in_specs=set_specs() * 2 + [by_row(width), by_row(span), by_row(span), full(norms), by_row(width)],
        out_specs=[by_row(width), by_col, by_row(span), by_row(width), by_row(width), by_col, full(norms)],
        out_shape=[
            jax.ShapeDtypeStruct((rows, width), bf),
            jax.ShapeDtypeStruct((width, rows), bf),
            jax.ShapeDtypeStruct((rows, span), bf),
            jax.ShapeDtypeStruct((rows, width), jnp.float32),
            jax.ShapeDtypeStruct((rows, width), bf),
            jax.ShapeDtypeStruct((width, rows), bf),
            jax.ShapeDtypeStruct(norms.shape, jnp.float32),
        ],
        scratch_shapes=set_scratch(weights_down) + set_scratch(weights_in),
        compiler_params=params(),
        cost_estimate=SMALL,
        name="middle",
    )(*set_args(weights_down), *set_args(weights_in), total, hidden, slope, norms, cotangent)


def store_rows(place_ref, t, refs, value, cut):
    count = refs[0].shape[3]
    for x in range(2):
        a = jnp.where(place_ref[0] == 0, t, x)
        b = jnp.where(place_ref[0] == 0, x, t)
        for z in range(ZS):
            start = (z * 2 + x) * count
            piece = value[start : start + count]
            if len(refs) == 1:
                refs[0][a, b, z, :, cut] = low(piece)
            else:
                got_ref, stay_ref, away_ref = refs[:3]
                piece = low(piece + got_ref[a, b, z, :, cut].astype(jnp.float32))

                @pl.when(a == place_ref[1])
                def _():
                    stay_ref[b, z, :, cut] = piece

                @pl.when(a != place_ref[1])
                def _():
                    away_ref[b, z, :, cut] = piece


def fetch(refs, first):
    if len(refs) == 1:
        return refs
    got_ref, stay_ref, away_ref, held_ref, sem = refs

    @pl.when(pl.program_id(0) == 0)
    def _():
        copy = pltpu.make_async_copy(got_ref, held_ref, sem)
        copy.start() if first else copy.wait()

    return held_ref, stay_ref, away_ref


def weigh_kernel(place_ref, a_ref, b_ref, *refs):
    fetch(refs, True)
    value = dot_nn(a_ref[...], b_ref[...])
    store_rows(place_ref, pl.program_id(0), fetch(refs, False), value, slice(None))


def weigh_more_kernel(place_ref, a_ref, b_ref, c_ref, u_ref, v_ref, *refs):
    t = pl.program_id(0)
    cols = b_ref.shape[1]
    fetch(refs, True)
    value = dot_nn(a_ref[...], b_ref[...])
    refs = fetch(refs, False)
    store_rows(place_ref, t, refs, value, slice(0, cols))
    chosen = jnp.where(t == 0, u_ref[...], v_ref[...])
    store_rows(place_ref, t, refs, dot_nn(c_ref[...], chosen), slice(cols, cols + u_ref.shape[1]))


def weigh_last_kernel(place_ref, a_ref, u_ref, v_ref, s_ref, *refs):
    t = pl.program_id(0)
    fetch(refs, True)
    chosen = jnp.where(t == 0, u_ref[0], v_ref[0])
    value = dot_nn(a_ref[...], chosen)
    refs = fetch(refs, False)
    edge = u_ref.shape[2] - LANES
    store_rows(place_ref, t, refs, value[:, :edge], slice(0, edge))
    last = jnp.where(place_ref[0] == 0, value[:, edge:], s_ref[...].astype(jnp.float32))
    store_rows(place_ref, t, refs, last, slice(edge, edge + LANES))


def weigh_call(kernel, specs, cols, place, got, *args):
    width = args[0].shape[0]
    shape = (2, 2, ZS, width // (2 * ZS), cols)
    whole = pl.BlockSpec(shape, lambda t, place: (0, 0, 0, 0, 0))
    some = pl.BlockSpec(shape[1:], lambda t, place: (0, 0, 0, 0))
    bf = jnp.bfloat16
    return pl.pallas_call(
        kernel,
        grid_spec=pltpu.PrefetchScalarGridSpec(
            num_scalar_prefetch=1,
            grid=(2,),
            in_specs=specs + ([] if got is None else [pl.BlockSpec(memory_space=pl.ANY)]),
            out_specs=whole if got is None else [some, some],
            scratch_shapes=[] if got is None else [pltpu.VMEM(shape, bf), pltpu.SemaphoreType.DMA],
        ),
        out_shape=jax.ShapeDtypeStruct(shape, bf) if got is None else [jax.ShapeDtypeStruct(shape[1:], bf)] * 2,
        compiler_params=params(),
        cost_estimate=SMALL,
        name="weigh",
    )(place, *args, *([] if got is None else [got]))


def whole_spec(value):
    return pl.BlockSpec(value.shape, lambda t, place: (0,) * value.ndim)


def weigh(flat, value, place, got):
    cols = value.shape[1] // 4
    specs = [whole_spec(flat), pl.BlockSpec((value.shape[0], cols), lambda t, place: (0, 2 * t + place[0]))]
    return weigh_call(weigh_kernel, specs, cols, place, got, flat, value)


def weigh_more(flat, value, flat_two, attended, place, got):
    cols = value.shape[1] // 4
    more = attended[0].shape[1] // 2
    extra = pl.BlockSpec((value.shape[0], more), lambda t, place: (0, place[0]))
    specs = [
        whole_spec(flat),
        pl.BlockSpec((value.shape[0], cols), lambda t, place: (0, 2 * t + place[0])),
        whole_spec(flat_two), extra, extra,
    ]
    return weigh_call(weigh_more_kernel, specs, cols + more, place, got, flat, value, flat_two, *attended)


def weigh_last(flat, parts, stats, place, got):
    _, rows, cols = parts[0].shape
    spec = pl.BlockSpec((1, rows, cols), lambda t, place: (place[0], 0, 0))
    specs = [whole_spec(flat), spec, spec, whole_spec(stats)]
    return weigh_call(weigh_last_kernel, specs, cols, place, got, flat, *parts, stats)


def input_kernel(side_ref, mine_ref, other_ref, res_ref, u_ref, v_ref, out_ref, left, right, sems):
    @pl.when(pl.program_id(0) == 0)
    def _():
        load_set(side_ref, mine_ref, other_ref, left, right, sems)
        wait_set(left, right, sems)

    total = res_ref[...]
    for t, ref in enumerate((u_ref, v_ref)):
        total = total + dot_nt(ref[0], left[t]) + dot_nt(ref[1], right[t])
    out_ref[...] = low(total)


def input_back(resid, parts, weights):
    rows, width = resid.shape
    cols = parts[0].shape[2]
    by_row = pl.BlockSpec((BLOCK, width), lambda r: (r, 0))
    side = pl.BlockSpec((2, BLOCK, cols), lambda r: (0, r, 0))
    return pl.pallas_call(
        input_kernel,
        grid=(rows // BLOCK,),
        in_specs=set_specs() + [by_row, side, side],
        out_specs=by_row,
        out_shape=jax.ShapeDtypeStruct((rows, width), jnp.bfloat16),
        scratch_shapes=set_scratch(weights),
        compiler_params=params(),
        cost_estimate=SMALL,
        name="input_back",
    )(*set_args(weights), resid, *parts)


def halves(value):
    return jnp.split(value, 2, axis=-1)


def shards(
    tokens,
    segment,
    weight_qkv,
    weight_out,
    weight_in,
    weight_down,
    gain_one,
    shift_one,
    gain_two,
    shift_two,
    cotangent,
):
    rows, width = tokens.shape
    own = weight_qkv.shape[1]
    wide = weight_out.shape[0]
    half_span = weight_in.shape[1]
    bf = jnp.bfloat16

    norms = jnp.stack([gain_one, shift_one, gain_two, shift_two], axis=1)
    norms = jnp.pad(norms, ((0, 0), (0, LANES - 4)))
    set_one = jnp.concatenate([jnp.transpose(weight_qkv, (1, 0, 2)).reshape(own, -1), norms], axis=1)
    one = Flow(gather_steps(*halves(set_one)))
    one.go(2)
    weight_out, weight_in, weight_down, tokens, segment = sync(
        one, weight_out, weight_in, weight_down, tokens, segment
    )
    one.go()
    set_two = jnp.concatenate([weight_out.T, weight_in, jnp.zeros((own, LANES), bf)], axis=1)
    two = Flow(gather_steps(*halves(set_two)))
    three = Flow(gather_steps(*halves(weight_down.T)))
    two.go(2)
    three.go(2)
    numbers = lax.dynamic_slice_in_dim(segment, lax.axis_index("tensor") * rows, rows)
    numbers = numbers.reshape(-1, 1, SEQ), jnp.broadcast_to(numbers[:, None], (rows, LANES)).reshape(-1, SEQ, LANES)
    tokens, tokens_flat, numbers = sync(one, two, three, tokens, tokens.T, numbers)
    one.go()
    sync(one, two)
    one.go()
    two.go()
    two.value = hold(two.value, one)
    one.go()
    one.go()
    sync(one, two)
    one.go()
    two.go()
    sync(one, two, three)
    one.go()
    two.go()
    tokens = sync(one, tokens)
    weights_one = one.go()
    kept = [attend(tokens, weights_one, numbers, 0, 0), None]
    tokens, kept[0] = sync(two, three, tokens, kept[0])
    two.go()
    tokens = sync(two, tokens)
    two.go()
    three.go()
    kept[0] = attend(tokens, weights_one, numbers, 0, 1, kept[0])
    tokens, kept[0] = sync(tokens, kept[0])
    kept[1] = attend(tokens, weights_one, numbers, 1, 0)
    tokens, kept[1] = sync(two, three, tokens, kept[1])
    two.go()
    three.go()
    tokens, kept[1] = sync(two, three, tokens, kept[1])
    two.go()
    three.go()
    first_mine, first_other, first_side = weights_one
    norms = jnp.where(first_side[0] == 0, first_other, first_mine)[:, 0, :, :, first_mine.shape[4] - LANES :]
    norms = jnp.transpose(norms, (1, 0, 2, 3)).reshape(width, LANES)[:, :8].T.astype(jnp.float32)
    kept[1] = attend(tokens, weights_one, numbers, 1, 1, kept[1])
    tokens, kept[1], norms = sync(two, three, tokens, kept[1], norms)
    three.go()
    tokens = sync(three, tokens)
    three.go()
    weights_two = two.go()
    attended = [kept[t][3] for t in range(2)]
    total, low_flat, hidden, slope = widen(tokens, attended, weights_two, norms, 2 * half_span)
    total, hidden = sync(three, total, hidden)
    three.go(2)
    weights_three = three.go()
    output, second_flat, grad_inner, grad_resid_one, grad_branch, branch_flat, stats = middle(
        total, hidden, slope, weights_three, weights_two, norms, cotangent
    )

    def part_two(place, got):
        return weigh_more(low_flat, grad_inner, branch_flat, attended, place, got)

    three = Flow(scatter_steps(lambda place, got: weigh(second_flat, hidden, place, got)))
    low_flat = sync(three, low_flat)
    three.go()
    two = Flow(scatter_steps(part_two))
    sync(two, three)
    two.go()
    three.go()
    low_flat = sync(two, three, low_flat)
    three.go()
    two.go()
    grad_branch = sync(two, grad_branch)
    two.go()
    parts = [attend_back(grad_branch, weights_two, kept[0], 0)]
    parts[0] = sync(three, parts[0])
    three.go()
    grad_branch, kept[1] = sync(three, grad_branch, kept[1])
    three.go()
    parts.append(attend_back(grad_branch, weights_two, kept[1], 1))
    parts = sync(two, three, parts)
    two.go()
    three.go()
    parts, tokens_flat = sync(two, three, parts, tokens_flat)
    two.go()
    three.go()
    stats = jnp.pad(low(stats.T), ((0, 0), (0, LANES - stats.shape[0])))
    one = Flow(scatter_steps(lambda place, got: weigh_last(tokens_flat, parts, stats, place, got)))
    sync(one, two, three)
    one.go()
    two.go()
    tokens_flat = sync(one, two, tokens_flat)
    two.go()
    one.go()
    two.value = hold(two.value, one)
    grad_resid_one = sync(one, grad_resid_one)
    one.go()
    three.go(2)
    input_grad = input_back(grad_resid_one, parts, weights_one)
    input_grad = sync(one, two, three, input_grad)
    one.go()
    two.go()
    sync(one, two)
    one.go()
    two.go()
    sync(one, two)
    one.go()
    one.go()
    one.go(2)
    sum_one = jnp.concatenate(one.go(), axis=1)
    two_left, two_right = two.go()
    sum_three = jnp.concatenate(three.go(), axis=1)
    half = half_span // 2
    stats = sum_one[:, 3 * wide : 3 * wide + 4].T
    sum_out = jnp.concatenate([two_left[:, half:], two_right[:, half:]], axis=1)[:, :wide]
    return (
        output,
        input_grad,
        jnp.transpose(sum_one[:, : 3 * wide].reshape(own, 3, -1), (1, 0, 2)),
        sum_out.T,
        jnp.concatenate([two_left[:, :half], two_right[:, :half]], axis=1),
        sum_three.T,
        stats[0],
        stats[1],
        stats[2],
        stats[3],
    )


def solution(mesh):
    both = P(("dp", "tensor"), None)
    split = P("dp")
    qkv_spec = P(None, "dp", "tensor")
    row_spec = P("tensor", "dp")
    in_spec = P("dp", "tensor")
    return jax.shard_map(
        shards,
        mesh=mesh,
        in_specs=(both, split, qkv_spec, row_spec, in_spec, row_spec, split, split, split, split, both),
        out_specs=(both, both, qkv_spec, row_spec, in_spec, row_spec, split, split, split, split),
        check_vma=False,
    )
```

```python
import functools

import jax
import jax.numpy as jnp
from jax import lax
from jax.experimental import pallas as pl
from jax.experimental.pallas import tpu as pltpu
from jax.sharding import PartitionSpec as P

HDIM = 64
SEQ = 512
LANES = 128
EDGE = 256
BLOCK = 256
CHUNK = 256
VMEM = 56 * 1024 * 1024
epsilon = 1e-05
SMALL = pl.CostEstimate(flops=100_000_000, bytes_accessed=100_000, transcendentals=0)


def low(value):
    return value.astype(jnp.bfloat16)


AXES = ("dp", "tensor")
ZS = 4


def place(z, x, c, y):
    return ((z * 2 + x) * 2 + c) * 2 + y


def pairs(move):
    found = []
    for z in range(ZS):
        for x in range(2):
            for c in range(2):
                for y in range(2):
                    found.append((place(z, x, c, y), place(*move(z, x, c, y))))
    return found


TO_CORE = pairs(lambda z, x, c, y: (z, x, 1 - c, y))
TO_NEAR = pairs(lambda z, x, c, y: (z, x, c, 1 - y) if c else (z, 1 - x, c, y))
TO_FAR = pairs(lambda z, x, c, y: (z, 1 - x, c, y) if c else (z, x, c, 1 - y))
TO_DEPTH = [pairs(lambda z, x, c, y: ((z - k) % ZS, x, c, y)) for k in range(ZS)]


def coords():
    d = lax.axis_index("dp")
    y = lax.axis_index("tensor")
    return d // 4, (d // 2) % 2, d % 2, y


def send(value, route):
    return lax.ppermute(value, AXES, route)


def in_order(own, other, at):
    return jnp.where(at == 0, jnp.stack([own, other]), jnp.stack([other, own]))


def tuned():
    return lax.axis_size("dp") == 16 and lax.axis_size("tensor") == 2


def sync(*values):
    found = lax.optimization_barrier([value.value if isinstance(value, Flow) else value for value in values])
    for value, new in zip(values, found):
        if isinstance(value, Flow):
            value.value = new
    found = [new for value, new in zip(values, found) if not isinstance(value, Flow)]
    return found[0] if len(found) == 1 else found


def hold(pieces, *values):
    if not isinstance(pieces, list):
        return pieces
    return [*pieces[:-1], sync(pieces[-1], *values)]


class Flow:
    def __init__(self, steps):
        self.steps = steps
        self.value = next(steps)

    def go(self, count=1):
        for _ in range(count):
            self.value = self.steps.send(self.value)
        return self.value


def gather_steps(left, right):
    if not tuned():
        for _ in range(10):
            left = yield left
        full = lax.all_gather(jnp.concatenate([left, right], axis=1), ("tensor", "dp"), axis=0, tiled=True)
        full = full.reshape(2, ZS, 2, -1, full.shape[1])
        left, right = jnp.split(full, 2, axis=4)
        left = jnp.transpose(left, (0, 2, 1, 3, 4))
        right = jnp.transpose(right, (2, 0, 1, 3, 4))
        yield left, right, jnp.zeros((1,), jnp.int32)
        return
    z, x, c, y = coords()
    first = c == 0
    own = yield jnp.where(first, right, left)
    got = yield send(own, TO_CORE)
    mine = jnp.where(first, jnp.concatenate([left, got]), jnp.concatenate([got, right]))
    mine = yield mine
    got = yield [send(mine, TO_DEPTH[k]) for k in (1, 2, 3)]
    column = jnp.stack([mine, *got, mine, *got[:2]])
    column = yield lax.dynamic_slice_in_dim(column, (ZS - z) % ZS, ZS, 0)
    near = yield send(column, TO_NEAR)
    plane = yield in_order(column, near, jnp.where(first, x, y))
    far = yield send(plane, TO_FAR)
    whole = yield in_order(plane, far, jnp.where(first, y, x))
    sibling = yield send(whole, TO_CORE)
    yield whole, sibling, c.astype(jnp.int32).reshape(1)


def add(a, b):
    return a.astype(jnp.float32) + b.astype(jnp.float32)


def pick(value, at):
    return lax.dynamic_index_in_dim(value, at, 0, keepdims=False)


def core_side():
    return coords()[2].astype(jnp.int32) if tuned() else jnp.int32(0)


def place_of(own):
    _, x, _, y = coords()
    side = core_side() if own else 1 - core_side()
    at = jnp.where(side == 0, y, x) if tuned() else 0 * y
    return jnp.stack([side, at.astype(jnp.int32)])


def exchange(value):
    return send(value, TO_CORE) if tuned() else jnp.zeros_like(value)


def scatter_steps(part):
    if not tuned():
        left, right = [jnp.stack(part(own)) for own in (True, False)]
        left = yield left
        for _ in range(7):
            left = yield left
        left = jnp.transpose(left, (0, 2, 1, 3, 4))
        right = jnp.transpose(right, (1, 2, 0, 3, 4))
        full = jnp.concatenate([left, right], axis=4)
        full = lax.psum_scatter(
            full.reshape(-1, full.shape[4]), ("tensor", "dp"), scatter_dimension=0, tiled=True
        )
        full = lax.optimization_barrier(full).astype(jnp.float32)
        yield tuple(jnp.split(full, 2, axis=1))
        return
    z, x, c, y = coords()
    first = c == 0
    stay, away = part(True)
    away = yield away
    got = yield send(away, TO_FAR)
    total = low(add(stay, got))
    at = jnp.where(first, x, y)
    away = yield pick(total, 1 - at)
    got = yield send(away, TO_NEAR)
    total = low(add(pick(total, at), got))
    away = yield [pick(total, (z - k) % ZS) for k in (1, 2, 3)]
    got = yield [send(piece, TO_DEPTH[k + 1]) for k, piece in enumerate(away)]
    total = pick(total, z).astype(jnp.float32)
    for piece in got:
        total = total + piece.astype(jnp.float32)
    total = total.reshape(2, -1, total.shape[1])
    away = yield pick(total, 1 - c)
    got = yield send(away, TO_CORE)
    keep = pick(total, c)
    yield jnp.where(first, keep, got), jnp.where(first, got, keep)


def dot_nn(left, right):
    return lax.dot_general(left, right, (((1,), (0,)), ((), ())), preferred_element_type=jnp.float32)


def dot_nt(left, right):
    return lax.dot_general(left, right, (((1,), (1,)), ((), ())), preferred_element_type=jnp.float32)


def flip(value):
    return jnp.swapaxes(value, 0, 1)


def load_set(side_ref, mine_ref, other_ref, left, right, sems, only=None):
    count = mine_ref.shape[3]

    def start(left_ref, right_ref):
        for y in range(2) if only is None else (only,):
            at = y if only is None else 0
            for x in range(2):
                for z in range(ZS):
                    cut = pl.ds((z * 2 + x) * count, count)
                    pltpu.make_async_copy(left_ref.at[y, x, z], left.at[at, cut], sems.at[0]).start()
                    pltpu.make_async_copy(right_ref.at[x, y, z], right.at[at, cut], sems.at[1]).start()

    @pl.when(side_ref[0] == 0)
    def _():
        start(mine_ref, other_ref)

    @pl.when(side_ref[0] != 0)
    def _():
        start(other_ref, mine_ref)


def load_halves(side_ref, mine_ref, other_ref, mine, other, sems):
    count = mine_ref.shape[3]

    def start(flipped):
        for y in range(2):
            for x in range(2):
                for z in range(ZS):
                    cut = pl.ds((z * 2 + x) * count, count)
                    for source, target, sem, turned in (
                        (mine_ref, mine, sems.at[0], flipped), (other_ref, other, sems.at[1], not flipped),
                    ):
                        block = source.at[x, y, z] if turned else source.at[y, x, z]
                        pltpu.make_async_copy(block, target.at[y, cut], sem).start()

    @pl.when(side_ref[0] == 0)
    def _():
        start(False)

    @pl.when(side_ref[0] != 0)
    def _():
        start(True)


def wait_set(left, right, sems):
    pltpu.make_async_copy(left, left, sems.at[0]).wait()
    pltpu.make_async_copy(right, right, sems.at[1]).wait()


def set_scratch(weights, count=2):
    width, cols = 8 * weights[0].shape[3], weights[0].shape[4]
    buffer = pltpu.VMEM((count, width, cols), jnp.bfloat16)
    return [buffer, buffer, pltpu.SemaphoreType.DMA((2,))]


def set_specs():
    return [
        pl.BlockSpec(memory_space=pltpu.SMEM),
        pl.BlockSpec(memory_space=pl.ANY),
        pl.BlockSpec(memory_space=pl.ANY),
    ]


def set_args(weights):
    return weights[2], weights[0], weights[1]


def params():
    return pltpu.CompilerParams(vmem_limit_bytes=VMEM)


def pair_cols(left, right, at):
    start = at * LANES
    width = left.shape[-1]
    if start < width:
        return left[:, start : start + LANES]
    return right[:, start - width : start - width + LANES]


def by_head(value):
    lane = lax.broadcasted_iota(jnp.int32, value.shape, 1)
    blank = jnp.zeros_like(value)
    return jnp.concatenate([jnp.where(lane < HDIM, value, blank), jnp.where(lane < HDIM, blank, value)], axis=0)


def own_heads(value):
    return jnp.concatenate([value[:HDIM, :SEQ], value[HDIM:, SEQ:]], axis=0)


def attend_kernel(t, carried, side_ref, mine_ref, other_ref, x_ref, row_ref, col_ref, *refs):
    pa_ref, pb_ref, e_ref, att_ref, flat_ref, inv_ref, bias_ref, a_ref, b_ref, sems = refs[carried:]
    pairs = flat_ref.shape[2] // LANES
    load_set(side_ref, mine_ref, other_ref, a_ref, b_ref, sems, t)
    wait_set(a_ref, b_ref, sems)

    x = x_ref[...]
    pa_ref[0] = low(dot_nn(x, a_ref[0]))
    pb_ref[0] = low(dot_nn(x, b_ref[0, :, : pb_ref.shape[2]]))
    bias = jnp.where(col_ref[0, :, :1] == row_ref[0], 0.0, -1e30)
    bias_ref[:, :SEQ] = bias
    bias_ref[:, SEQ:] = bias
    left, right = pa_ref[0], pb_ref[0]
    for p in range(pairs):
        queries = by_head(low(pair_cols(left, right, p).astype(jnp.float32) * HDIM**-0.5))
        key_rows = pair_cols(left, right, pairs + p)
        values_flat = flip(pair_cols(left, right, 2 * pairs + p))
        scores = dot_nt(key_rows, queries) + bias_ref[...]
        weights = jnp.exp(scores - jnp.max(scores, axis=0, keepdims=True))
        inverse = 1.0 / jnp.sum(weights, axis=0, keepdims=True)
        weights = low(weights)
        e_ref[0, p] = weights
        inv_ref[0, p : p + 1, :] = inverse
        flat = low(own_heads(dot_nn(values_flat, weights) * inverse))
        flat_ref[0, 0, p * LANES : (p + 1) * LANES, :] = flat
        at = p * LANES
        att_ref[at // EDGE, :, at % EDGE : at % EDGE + LANES] = flip(flat)
    at = pairs * LANES
    att_ref[at // EDGE, :, at % EDGE :] = jnp.zeros((SEQ, LANES), jnp.bfloat16)


def attend(tokens, weights, numbers, t, s, carry=()):
    rows, width = tokens.shape
    seqs = rows // SEQ
    cols = weights[0].shape[4]
    wide = (2 * cols - LANES) // 3
    pairs = wide // LANES
    used = cols - LANES
    bf = jnp.bfloat16
    at = lambda *index: (lambda i: index)
    return pl.pallas_call(
        functools.partial(attend_kernel, t, len(carry)),
        grid=(1,),
        in_specs=set_specs() + [
            pl.BlockSpec((SEQ, width), at(s, 0)),
            pl.BlockSpec((1, 1, SEQ), at(s, 0, 0)),
            pl.BlockSpec((1, SEQ, LANES), at(s, 0, 0)),
        ] + [pl.BlockSpec(memory_space=pl.ANY)] * len(carry),
        out_specs=[
            pl.BlockSpec((1, SEQ, cols), at(0, s, 0)),
            pl.BlockSpec((1, SEQ, used), at(0, s, 0)),
            pl.BlockSpec((1, pairs, SEQ, 2 * SEQ), at(s, 0, 0, 0)),
            pl.BlockSpec((2, SEQ, EDGE), at(0, s, 0)),
            pl.BlockSpec((1, 1, wide, SEQ), at(0, s, 0, 0)),
            pl.BlockSpec((1, pairs, 2 * SEQ), at(s, 0, 0)),
        ],
        out_shape=[
            jax.ShapeDtypeStruct((1, rows, cols), bf),
            jax.ShapeDtypeStruct((1, rows, used), bf),
            jax.ShapeDtypeStruct((seqs, pairs, SEQ, 2 * SEQ), bf),
            jax.ShapeDtypeStruct((2, rows, EDGE), bf),
            jax.ShapeDtypeStruct((1, seqs, wide, SEQ), bf),
            jax.ShapeDtypeStruct((seqs, pairs, 2 * SEQ), jnp.float32),
        ],
        input_output_aliases={6 + i: i for i in range(len(carry))},
        scratch_shapes=[pltpu.VMEM((SEQ, 2 * SEQ), jnp.float32)] + set_scratch(weights, 1),
        compiler_params=params(),
        cost_estimate=SMALL,
        name="attend",
    )(*set_args(weights), tokens, *numbers, *carry)


def attend_back_kernel(
    t, side_ref, mine_ref, other_ref, g_ref, pa_ref, pb_ref, e_ref, flat_ref, inv_ref,
    dm_ref, do_ref, w_ref, gt_ref, sem,
):
    wide = flat_ref.shape[2]
    pairs = wide // LANES
    count = mine_ref.shape[3]

    @pl.when(pl.program_id(0) == 0)
    def _():
        def start(left_ref, right_ref):
            cols = pl.ds(0, EDGE)
            for x in range(2):
                for z in range(ZS):
                    cut = pl.ds((z * 2 + x) * count, count)
                    pltpu.make_async_copy(left_ref.at[t, x, z, :, cols], w_ref.at[0, cut], sem).start()
                    pltpu.make_async_copy(right_ref.at[x, t, z, :, cols], w_ref.at[1, cut], sem).start()

        @pl.when(side_ref[0] == 0)
        def _():
            start(mine_ref, other_ref)

        @pl.when(side_ref[0] != 0)
        def _():
            start(other_ref, mine_ref)

        pltpu.make_async_copy(w_ref, w_ref, sem).wait()

    for side in range(2):
        size = min(EDGE, wide - side * EDGE)
        gt_ref[side * EDGE : side * EDGE + size] = flip(low(dot_nn(g_ref[...], w_ref[side, :, :size])))
    left, right = pa_ref[0], pb_ref[0]
    found = {}
    blank = jnp.zeros((HDIM, SEQ), jnp.bfloat16)
    for p in range(pairs):
        queries = by_head(pair_cols(left, right, p))
        keys_flat = flip(pair_cols(left, right, pairs + p))
        value_rows = pair_cols(left, right, 2 * pairs + p)
        flat = flat_ref[0, 0, p * LANES : (p + 1) * LANES, :].astype(jnp.float32)
        scaled, centre = [], []
        for half in range(2):
            rows = slice(half * HDIM, (half + 1) * HDIM)
            grads = gt_ref[p * LANES + half * HDIM : p * LANES + (half + 1) * HDIM, :].astype(jnp.float32)
            scaled.append(low(grads * inv_ref[0, p : p + 1, half * SEQ : (half + 1) * SEQ]))
            centre.append(jnp.sum(scaled[half].astype(jnp.float32) * flat[rows], axis=0, keepdims=True))
        grads = jnp.concatenate(
            [jnp.concatenate([scaled[0], blank], axis=0), jnp.concatenate([blank, scaled[1]], axis=0)], axis=1
        )
        weights = e_ref[0, p]
        grad_weights = dot_nn(value_rows, grads) - jnp.concatenate(centre, axis=1)
        grad_scores = low(weights.astype(jnp.float32) * grad_weights)
        found[p] = flip(low(own_heads(dot_nn(keys_flat, grad_scores)) * HDIM**-0.5))
        found[pairs + p] = low(dot_nn(grad_scores, queries) * HDIM**-0.5)
        found[2 * pairs + p] = low(dot_nn(weights, flip(grads)))
    found[3 * pairs] = jnp.zeros((SEQ, LANES), jnp.bfloat16)
    count = (3 * pairs + 1) // 2
    for at in range(count):
        cut = slice(at * LANES, (at + 1) * LANES)
        dm_ref[:, cut] = jnp.where(side_ref[0] == 0, found[at], found[at + count])
        do_ref[:, cut] = jnp.where(side_ref[0] == 0, found[at + count], found[at])


def attend_back(grad_branch, weights, kept, t):
    pa, pb, e, _, flat, inv = kept
    rows, width = grad_branch.shape
    seqs = rows // SEQ
    cols, used = pa.shape[2], pb.shape[2]
    wide = flat.shape[2]
    bf = jnp.bfloat16
    return pl.pallas_call(
        functools.partial(attend_back_kernel, t),
        grid=(seqs,),
        in_specs=set_specs() + [
            pl.BlockSpec((SEQ, width), lambda s: (s, 0)),
            pl.BlockSpec((1, SEQ, cols), lambda s: (0, s, 0)),
            pl.BlockSpec((1, SEQ, used), lambda s: (0, s, 0)),
            pl.BlockSpec((1,) + e.shape[1:], lambda s: (s, 0, 0, 0)),
            pl.BlockSpec((1, 1, wide, SEQ), lambda s: (0, s, 0, 0)),
            pl.BlockSpec((1,) + inv.shape[1:], lambda s: (s, 0, 0)),
        ],
        out_specs=[pl.BlockSpec((SEQ, cols), lambda s: (s, 0))] * 2,
        out_shape=[jax.ShapeDtypeStruct((rows, cols), bf)] * 2,
        scratch_shapes=[
            pltpu.VMEM((2, width, EDGE), bf),
            pltpu.VMEM((wide, SEQ), bf),
            pltpu.SemaphoreType.DMA,
        ],
        compiler_params=params(),
        cost_estimate=SMALL,
        name="attend_back",
    )(*set_args(weights), grad_branch, pa, pb, e, flat, inv)


def gelu_parts(v):
    below = 0.5 + 0.5 * lax.erf(v * 0.5**0.5)
    bell = jnp.exp(-0.5 * (v * v))
    return v * below, below + (0.3989422804014327 * v) * bell


def row_norm(value):
    centered = value - jnp.mean(value, axis=-1, keepdims=True)
    inverse = lax.rsqrt(jnp.mean(centered * centered, axis=-1, keepdims=True) + epsilon)
    return centered * inverse, inverse


def row_norm_back(grad_scaled, scaled, inverse):
    centered = grad_scaled - jnp.mean(grad_scaled, axis=-1, keepdims=True)
    return inverse * (centered - scaled * jnp.mean(grad_scaled * scaled, axis=-1, keepdims=True))


def widen_kernel(
    side_ref, mine_ref, other_ref, x_ref, u_ref, v_ref, n_ref,
    sum_ref, low_ref, hm_ref, ho_ref, sm_ref, so_ref, mine, other, sems,
):
    @pl.when(pl.program_id(0) == 0)
    def _():
        load_halves(side_ref, mine_ref, other_ref, mine, other, sems)
        wait_set(mine, other, sems)

    total = x_ref[...].astype(jnp.float32)
    for t, ref in enumerate((u_ref, v_ref)):
        near = jnp.where(side_ref[0] == 0, ref[0], ref[1])
        away = jnp.where(side_ref[0] == 0, ref[1], ref[0])
        total = total + dot_nt(near, mine[t, :, :EDGE]) + dot_nt(away, other[t, :, :EDGE])
    sum_ref[...] = total
    scaled, _ = row_norm(total)
    x = low(scaled * n_ref[0:1, :] + n_ref[1:2, :])
    low_ref[...] = flip(x)
    half = mine.shape[2] - EDGE
    for t in range(2):
        for ref, hid_ref, slope_ref in ((mine, hm_ref, sm_ref), (other, ho_ref, so_ref)):
            for start in range(0, half, CHUNK):
                cut = slice(t * half + start, t * half + start + CHUNK)
                value, slope = gelu_parts(dot_nn(x, ref[t, :, EDGE + start : EDGE + start + CHUNK]))
                hid_ref[:, cut] = low(value)
                slope_ref[:, cut] = low(slope)


def widen(tokens, attended, weights, norms):
    rows, width = tokens.shape
    span = 2 * (weights[0].shape[4] - EDGE)
    bf = jnp.bfloat16
    by_row = lambda n: pl.BlockSpec((BLOCK, n), lambda r: (r, 0))
    full = lambda a: pl.BlockSpec(a.shape, lambda r: (0, 0))
    side = pl.BlockSpec((2, BLOCK, EDGE), lambda r: (0, r, 0))
    return pl.pallas_call(
        widen_kernel,
        grid=(rows // BLOCK,),
        in_specs=set_specs() + [by_row(width), side, side, full(norms)],
        out_specs=[by_row(width), pl.BlockSpec((width, BLOCK), lambda r: (0, r))] + [by_row(span)] * 4,
        out_shape=[
            jax.ShapeDtypeStruct((rows, width), jnp.float32),
            jax.ShapeDtypeStruct((width, rows), bf),
        ] + [jax.ShapeDtypeStruct((rows, span), bf)] * 4,
        scratch_shapes=set_scratch(weights),
        compiler_params=params(),
        cost_estimate=SMALL,
        name="widen",
    )(*set_args(weights), tokens, *attended, norms)


def middle_kernel(
    side_ref, mine_ref, other_ref, side_two_ref, mine_two_ref, other_two_ref,
    sum_ref, hm_ref, ho_ref, sm_ref, so_ref, n_ref, cot_ref,
    out_ref, gs_ref, gm_ref, go_ref, res_ref, gb_ref, gbt_ref, stat_ref,
    mine, other, sems, win_mine, win_other, win_sems,
):
    @pl.when(pl.program_id(0) == 0)
    def _():
        load_halves(side_ref, mine_ref, other_ref, mine, other, sems)
        load_halves(side_two_ref, mine_two_ref, other_two_ref, win_mine, win_other, win_sems)
        wait_set(mine, other, sems)

    gain_one, shift_one = n_ref[0:1, :], n_ref[1:2, :]
    gain_two, shift_two = n_ref[2:3, :], n_ref[3:4, :]
    scaled_one, inverse_one = row_norm(sum_ref[...])
    value = scaled_one * gain_one + shift_one
    half = mine.shape[2]
    for t in range(2):
        for ref, hid_ref in ((mine, hm_ref), (other, ho_ref)):
            value = value + dot_nt(hid_ref[:, t * half : (t + 1) * half], ref[t])
    scaled_two, inverse_two = row_norm(value)
    out_ref[...] = low(scaled_two * gain_two + shift_two)
    cotangent = cot_ref[...].astype(jnp.float32)
    grad_two = row_norm_back(cotangent * gain_two, scaled_two, inverse_two)
    grad_second = low(grad_two)
    gs_ref[...] = flip(grad_second)
    for t in range(2):
        for ref, slope_ref, gi_ref in ((mine, sm_ref, gm_ref), (other, so_ref, go_ref)):
            for start in range(0, half, CHUNK):
                cut = slice(t * half + start, t * half + start + CHUNK)
                grad_hidden = dot_nn(grad_second, ref[t, :, start : start + CHUNK])
                gi_ref[:, cut] = low(grad_hidden * slope_ref[:, cut].astype(jnp.float32))

    @pl.when(pl.program_id(0) == 0)
    def _():
        wait_set(win_mine, win_other, win_sems)
        stat_ref[...] = jnp.zeros_like(stat_ref)

    grad_first = grad_two
    for t in range(2):
        for ref, gi_ref in ((win_mine, gm_ref), (win_other, go_ref)):
            grad_first = grad_first + dot_nt(gi_ref[:, t * half : (t + 1) * half], ref[t, :, EDGE:])
    grad_one = row_norm_back(grad_first * gain_one, scaled_one, inverse_one)
    res_ref[...] = grad_one
    gb_ref[...] = low(grad_one)
    gbt_ref[...] = flip(low(grad_one))
    for row, value in enumerate((grad_first * scaled_one, grad_first, cotangent * scaled_two, cotangent)):
        stat_ref[row : row + 1, :] += jnp.sum(value, axis=0, keepdims=True)


def middle(total, hidden, slope, weights_down, weights_in, norms, cotangent):
    rows, width = total.shape
    span = hidden[0].shape[1]
    bf = jnp.bfloat16
    by_row = lambda n: pl.BlockSpec((BLOCK, n), lambda r: (r, 0))
    by_col = pl.BlockSpec((width, BLOCK), lambda r: (0, r))
    full = lambda a: pl.BlockSpec(a.shape, lambda r: (0, 0))
    return pl.pallas_call(
        middle_kernel,
        grid=(rows // BLOCK,),
        in_specs=set_specs() * 2 + [by_row(width)] + [by_row(span)] * 4 + [full(norms), by_row(width)],
        out_specs=[
            by_row(width), by_col, by_row(span), by_row(span), by_row(width), by_row(width), by_col, full(norms),
        ],
        out_shape=[
            jax.ShapeDtypeStruct((rows, width), bf),
            jax.ShapeDtypeStruct((width, rows), bf),
            jax.ShapeDtypeStruct((rows, span), bf),
            jax.ShapeDtypeStruct((rows, span), bf),
            jax.ShapeDtypeStruct((rows, width), jnp.float32),
            jax.ShapeDtypeStruct((rows, width), bf),
            jax.ShapeDtypeStruct((width, rows), bf),
            jax.ShapeDtypeStruct(norms.shape, jnp.float32),
        ],
        scratch_shapes=set_scratch(weights_down) + set_scratch(weights_in),
        compiler_params=params(),
        cost_estimate=SMALL,
        name="middle",
    )(*set_args(weights_down), *set_args(weights_in), total, *hidden, *slope, norms, cotangent)


def store_rows(place_ref, t, refs, value, cut):
    stay_ref, away_ref = refs
    count = stay_ref.shape[2]
    for x in range(2):
        a = jnp.where(place_ref[0] == 0, t, x)
        b = jnp.where(place_ref[0] == 0, x, t)
        for z in range(ZS):
            start = (z * 2 + x) * count
            piece = low(value[start : start + count])

            @pl.when(a == place_ref[1])
            def _():
                stay_ref[b, z, :, cut] = piece

            @pl.when(a != place_ref[1])
            def _():
                away_ref[b, z, :, cut] = piece


def weigh_kernel(jobs, place_ref, stats_ref, *refs):
    refs = list(refs)
    sources = [refs.pop(0) for _ in range(6 * len(jobs))]
    outs = refs.pop(0), refs.pop(0)
    *buffers, sems = refs
    copies = []
    for j, (views, start, size) in enumerate(jobs):
        flat_buf, value_buf = buffers[2 * j], buffers[2 * j + 1]
        rows = flat_buf.shape[1] // 2
        low_part, high_part = pl.ds(0, rows), pl.ds(rows, rows)
        targets = [
            flat_buf.at[:, low_part], flat_buf.at[:, high_part],
            value_buf.at[0, low_part], value_buf.at[0, high_part],
            value_buf.at[1, low_part], value_buf.at[1, high_part],
        ]
        copies.append([
            pltpu.make_async_copy(view(source, place_ref), target, sems.at[6 * j + i])
            for i, (view, source, target) in enumerate(zip(views, sources[6 * j : 6 * j + 6], targets))
        ])
    for group in copies:
        for copy in group:
            copy.start()
    for j, (_, start, size) in enumerate(jobs):
        flat_buf, value_buf = buffers[2 * j], buffers[2 * j + 1]
        for t in range(2):
            for copy in copies[j][2 + 2 * t : 4 + 2 * t] + (copies[j][:2] if t == 0 else []):
                copy.wait()
            value = dot_nn(flat_buf[...], value_buf[t])
            if stats_ref.shape[0] == value.shape[0]:
                edge = size - LANES
                store_rows(place_ref, t, outs, value[:, :edge], slice(start, start + edge))
                value = jnp.where(place_ref[0] == 0, value[:, edge:], stats_ref[...])
                store_rows(place_ref, t, outs, value, slice(start + edge, start + size))
            else:
                store_rows(place_ref, t, outs, value, slice(start, start + size))


def weigh_call(place, stats, *jobs):
    width, rows = jobs[0][0][0].shape
    cols = sum(job[2] for job in jobs)
    shape = (2, ZS, width // (2 * ZS), cols)
    bf = jnp.bfloat16
    arrays, plan, scratch, start = [], [], [], 0
    for values, views, size in jobs:
        arrays += values
        plan.append((views, start, size))
        scratch += [pltpu.VMEM((width, 2 * rows), bf), pltpu.VMEM((2, 2 * rows, size), bf)]
        start += size
    return pl.pallas_call(
        functools.partial(weigh_kernel, plan),
        in_specs=[pl.BlockSpec(memory_space=pltpu.SMEM), pl.BlockSpec(memory_space=pltpu.VMEM)]
        + [pl.BlockSpec(memory_space=pl.ANY)] * len(arrays),
        out_specs=[pl.BlockSpec(memory_space=pltpu.VMEM)] * 2,
        out_shape=[jax.ShapeDtypeStruct(shape, bf)] * 2,
        scratch_shapes=scratch + [pltpu.SemaphoreType.DMA((len(arrays),))],
        compiler_params=params(),
        cost_estimate=SMALL,
        name="weigh",
    )(place, stats, *arrays)


def whole(ref, place_ref):
    return ref


def half_of(t, size):
    return lambda ref, place_ref: ref.at[:, pl.ds(t * size, size)]


def halved(flat, value, flat_got, value_got):
    size = value.shape[1] // 2
    views = [whole, whole, half_of(0, size), half_of(0, size), half_of(1, size), half_of(1, size)]
    return [flat, flat_got, value, value_got, value, value_got], views, size


def weigh(place, *args):
    return weigh_call(place, jnp.zeros((8, LANES), jnp.float32), halved(*args))


def weigh_more(place, flat, value, flat_got, value_got, flat_two, u, v, flat_two_got, u_got, v_got):
    own = lambda ref, place_ref: ref.at[place_ref[0]]
    views = [whole, whole, own, whole, own, whole]
    return weigh_call(
        place, jnp.zeros((8, LANES), jnp.float32),
        ([flat_two, flat_two_got, u, u_got, v, v_got], views, EDGE),
        halved(flat, value, flat_got, value_got),
    )


def weigh_last(place, flat, u, v, flat_got, u_got, v_got, stats):
    return weigh_call(place, stats, ([flat, flat_got, u, u_got, v, v_got], [whole] * 6, u.shape[1]))


def input_kernel(side_ref, mine_ref, other_ref, res_ref, um_ref, uo_ref, vm_ref, vo_ref, out_ref, mine, other, sems):
    @pl.when(pl.program_id(0) == 0)
    def _():
        load_halves(side_ref, mine_ref, other_ref, mine, other, sems)
        wait_set(mine, other, sems)

    total = res_ref[...]
    for t, (near, away) in enumerate(((um_ref, uo_ref), (vm_ref, vo_ref))):
        total = total + dot_nt(near[...], mine[t]) + dot_nt(away[...], other[t])
    out_ref[...] = low(total)


def input_back(resid, parts, weights):
    rows, width = resid.shape
    by_row = lambda n: pl.BlockSpec((BLOCK, n), lambda r: (r, 0))
    return pl.pallas_call(
        input_kernel,
        grid=(rows // BLOCK,),
        in_specs=set_specs() + [by_row(width)] + [by_row(parts[0][0].shape[1])] * 4,
        out_specs=by_row(width),
        out_shape=jax.ShapeDtypeStruct((rows, width), jnp.bfloat16),
        scratch_shapes=set_scratch(weights),
        compiler_params=params(),
        cost_estimate=SMALL,
        name="input_back",
    )(*set_args(weights), resid, *parts[0], *parts[1])


def halves(value):
    return jnp.split(value, 2, axis=-1)


def shards(
    tokens,
    segment,
    weight_qkv,
    weight_out,
    weight_in,
    weight_down,
    gain_one,
    shift_one,
    gain_two,
    shift_two,
    cotangent,
):
    rows, width = tokens.shape
    own = weight_qkv.shape[1]
    wide = weight_out.shape[0]
    half_span = weight_in.shape[1]
    bf = jnp.bfloat16

    norms = jnp.stack([gain_one, shift_one, gain_two, shift_two], axis=1)
    norms = jnp.pad(norms, ((0, 0), (0, LANES - 4)))
    set_one = jnp.concatenate([jnp.transpose(weight_qkv, (1, 0, 2)).reshape(own, -1), norms], axis=1)
    one = Flow(gather_steps(*halves(set_one)))
    one.go(2)
    weight_out, weight_in, weight_down, tokens, segment = sync(
        one, weight_out, weight_in, weight_down, tokens, segment
    )
    one.go()
    out_flat, half = weight_out.T, half_span // 2
    out_flat = jnp.pad(out_flat, ((0, 0), (0, 2 * EDGE - wide)))
    two = Flow(gather_steps(*[
        jnp.concatenate([o, w], axis=1) for o, w in zip(halves(out_flat), halves(weight_in))
    ]))
    three = Flow(gather_steps(*halves(weight_down.T)))
    two.go(2)
    three.go(2)
    numbers = lax.dynamic_slice_in_dim(segment, lax.axis_index("tensor") * rows, rows)
    numbers = numbers.reshape(-1, 1, SEQ), jnp.broadcast_to(numbers[:, None], (rows, LANES)).reshape(-1, SEQ, LANES)
    tokens, numbers = sync(one, two, three, tokens, numbers)
    one.go()
    sync(one, two)
    one.go()
    two.go()
    two.value = hold(two.value, one)
    one.go()
    one.go()
    tokens_flat = sync(one, two, tokens.T)
    one.go()
    two.go()
    sync(one, two, three)
    one.go()
    two.go()
    tokens = sync(one, tokens)
    weights_one = one.go()
    kept = [attend(tokens, weights_one, numbers, 0, 0), None]
    tokens, kept[0] = sync(two, three, tokens, kept[0])
    two.go()
    tokens = sync(two, tokens)
    two.go()
    three.go()
    kept[0] = attend(tokens, weights_one, numbers, 0, 1, kept[0])
    tokens, kept[0] = sync(tokens, kept[0])
    kept[1] = attend(tokens, weights_one, numbers, 1, 0)
    tokens, kept[1] = sync(two, three, tokens, kept[1])
    two.go()
    three.go()
    tokens, kept[1] = sync(two, three, tokens, kept[1])
    two.go()
    three.go()
    first_mine, first_other, first_side = weights_one
    norms = jnp.where(first_side[0] == 0, first_other, first_mine)[:, 0, :, :, first_mine.shape[4] - LANES :]
    norms = jnp.transpose(norms, (1, 0, 2, 3)).reshape(width, LANES)[:, :8].T.astype(jnp.float32)
    kept[1] = attend(tokens, weights_one, numbers, 1, 1, kept[1])
    tokens, kept[1], norms = sync(two, three, tokens, kept[1], norms)
    three.go()
    tokens = sync(three, tokens)
    three.go()
    weights_two = two.go()
    attended = [kept[t][3] for t in range(2)]
    attended_got = [exchange(lax.dynamic_index_in_dim(value, 1 - core_side(), 0, keepdims=False)) for value in attended]
    total, low_flat, *wide_out = widen(tokens, attended, weights_two, norms)
    hidden, slope = wide_out[:2], wide_out[2:]
    tokens_got = exchange(tokens_flat)
    total, low_flat, hidden, attended_got, tokens_got = sync(
        three, total, low_flat, hidden, attended_got, tokens_got
    )
    three.go(2)
    weights_three = three.go()
    weights_three, away, low_flat = sync(weights_three, hidden[1], low_flat)
    hidden_got, low_got = exchange(away), exchange(low_flat)
    output, second_flat, inner_mine, inner_other, grad_resid_one, grad_branch, branch_flat, stats = middle(
        total, hidden, slope, weights_three, weights_two, norms, cotangent
    )
    second_flat, hidden_got, low_got, inner_other, branch_flat, stats = sync(
        second_flat, hidden_got, low_got, inner_other, branch_flat, stats
    )
    second_got = exchange(second_flat)
    second_got, inner_other, branch_flat, stats = sync(second_got, inner_other, branch_flat, stats)
    inner_got, branch_got, stats_got = exchange(inner_other), exchange(branch_flat), exchange(stats)
    three = Flow(scatter_steps(lambda own: weigh(
        place_of(own), second_flat, hidden[0 if own else 1], second_got, hidden_got
    )))
    inner_mine, inner_got, branch_got, stats_got = sync(three, inner_mine, inner_got, branch_got, stats_got)
    three.go()
    two = Flow(scatter_steps(lambda own: weigh_more(
        place_of(own), low_flat, inner_mine if own else inner_other, low_got, inner_got,
        branch_flat, *attended, branch_got, *attended_got,
    )))
    grad_branch = sync(two, grad_branch)
    two.go()
    parts = [attend_back(grad_branch, weights_two, kept[0], 0)]
    parts[0] = sync(three, parts[0])
    three.go()
    grad_branch, kept[1], parts[0] = sync(three, grad_branch, kept[1], parts[0])
    three.go()
    parts_got = [exchange(parts[0][1])]
    parts.append(attend_back(grad_branch, weights_two, kept[1], 1))
    parts, parts_got = sync(two, three, parts, parts_got)
    parts_got.append(exchange(parts[1][1]))
    two.go()
    three.go()
    parts, parts_got = sync(two, three, parts, parts_got)
    two.go()
    three.go()
    stats = jnp.pad((stats + stats_got).T, ((0, 0), (0, LANES - stats.shape[0])))
    one = Flow(scatter_steps(lambda own: weigh_last(
        place_of(own), tokens_flat, *[value[0 if own else 1] for value in parts], tokens_got, *parts_got, stats
    )))
    grad_resid_one = sync(one, two, three, grad_resid_one)
    one.go()
    two.go()
    two.go()
    three.go(2)
    input_grad = input_back(grad_resid_one, parts, weights_one)
    input_grad = sync(one, two, input_grad)
    one.go()
    one.go()
    two.go(2)
    sync(one, two)
    one.go()
    one.go()
    one.go(2)
    sum_one = jnp.concatenate(one.go(), axis=1)
    two_left, two_right = two.go()
    sum_three = jnp.concatenate(three.go(), axis=1)
    stats = sum_one[:, 3 * wide : 3 * wide + 4].T
    sum_out = jnp.concatenate([two_left[:, :EDGE], two_right[:, :EDGE]], axis=1)[:, :wide]
    return (
        output,
        input_grad,
        jnp.transpose(sum_one[:, : 3 * wide].reshape(own, 3, -1), (1, 0, 2)),
        sum_out.T,
        jnp.concatenate([two_left[:, EDGE:], two_right[:, EDGE:]], axis=1),
        sum_three.T,
        stats[0],
        stats[1],
        stats[2],
        stats[3],
    )


def solution(mesh):
    both = P(("dp", "tensor"), None)
    split = P("dp")
    qkv_spec = P(None, "dp", "tensor")
    row_spec = P("tensor", "dp")
    in_spec = P("dp", "tensor")
    return jax.shard_map(
        shards,
        mesh=mesh,
        in_specs=(both, split, qkv_spec, row_spec, in_spec, row_spec, split, split, split, split, both),
        out_specs=(both, both, qkv_spec, row_spec, in_spec, row_spec, split, split, split, split),
        check_vma=False,
    )
```

```python
import functools

import jax
import jax.numpy as jnp
from jax import lax
from jax.experimental import pallas as pl
from jax.experimental.pallas import tpu as pltpu
from jax.sharding import PartitionSpec as P

HDIM = 64
SEQ = 512
LANES = 128
EDGE = 256
BLOCK = 256
CHUNK = 256
VMEM = 56 * 1024 * 1024
epsilon = 1e-05
SMALL = pl.CostEstimate(flops=100_000_000, bytes_accessed=100_000, transcendentals=0)


def low(value):
    return value.astype(jnp.bfloat16)


AXES = ("dp", "tensor")
ZS = 4


def place(z, x, c, y):
    return ((z * 2 + x) * 2 + c) * 2 + y


def pairs(move):
    found = []
    for z in range(ZS):
        for x in range(2):
            for c in range(2):
                for y in range(2):
                    found.append((place(z, x, c, y), place(*move(z, x, c, y))))
    return found


TO_CORE = pairs(lambda z, x, c, y: (z, x, 1 - c, y))
TO_NEAR = pairs(lambda z, x, c, y: (z, x, c, 1 - y) if c else (z, 1 - x, c, y))
TO_FAR = pairs(lambda z, x, c, y: (z, 1 - x, c, y) if c else (z, x, c, 1 - y))
TO_DEPTH = [pairs(lambda z, x, c, y: ((z - k) % ZS, x, c, y)) for k in range(ZS)]


def coords():
    d = lax.axis_index("dp")
    y = lax.axis_index("tensor")
    return d // 4, (d // 2) % 2, d % 2, y


def send(value, route):
    return lax.ppermute(value, AXES, route)


def in_order(own, other, at):
    return jnp.where(at == 0, jnp.stack([own, other]), jnp.stack([other, own]))


def tuned():
    return lax.axis_size("dp") == 16 and lax.axis_size("tensor") == 2


def sync(*values):
    found = lax.optimization_barrier([value.value if isinstance(value, Flow) else value for value in values])
    for value, new in zip(values, found):
        if isinstance(value, Flow):
            value.value = new
    found = [new for value, new in zip(values, found) if not isinstance(value, Flow)]
    return found[0] if len(found) == 1 else found


def hold(pieces, *values):
    if not isinstance(pieces, list):
        return pieces
    return [*pieces[:-1], sync(pieces[-1], *values)]


class Flow:
    def __init__(self, steps):
        self.steps = steps
        self.value = next(steps)

    def go(self, count=1):
        for _ in range(count):
            self.value = self.steps.send(self.value)
        return self.value


def gather_steps(left, right):
    if not tuned():
        for _ in range(10):
            left = yield left
        full = lax.all_gather(jnp.concatenate([left, right], axis=1), ("tensor", "dp"), axis=0, tiled=True)
        full = full.reshape(2, ZS, 2, -1, full.shape[1])
        left, right = jnp.split(full, 2, axis=4)
        left = jnp.transpose(left, (0, 2, 1, 3, 4))
        right = jnp.transpose(right, (2, 0, 1, 3, 4))
        yield left, right, jnp.zeros((1,), jnp.int32)
        return
    z, x, c, y = coords()
    first = c == 0
    own = yield jnp.where(first, right, left)
    got = yield send(own, TO_CORE)
    mine = jnp.where(first, jnp.concatenate([left, got]), jnp.concatenate([got, right]))
    mine = yield mine
    got = yield [send(mine, TO_DEPTH[k]) for k in (1, 2, 3)]
    column = jnp.stack([mine, *got, mine, *got[:2]])
    column = yield lax.dynamic_slice_in_dim(column, (ZS - z) % ZS, ZS, 0)
    near = yield send(column, TO_NEAR)
    plane = yield in_order(column, near, jnp.where(first, x, y))
    far = yield send(plane, TO_FAR)
    whole = yield in_order(plane, far, jnp.where(first, y, x))
    sibling = yield send(whole, TO_CORE)
    yield whole, sibling, c.astype(jnp.int32).reshape(1)


def add(a, b):
    return a.astype(jnp.float32) + b.astype(jnp.float32)


def pick(value, at):
    return lax.dynamic_index_in_dim(value, at, 0, keepdims=False)


def core_side():
    return coords()[2].astype(jnp.int32) if tuned() else jnp.int32(0)


def place_of(own):
    _, x, _, y = coords()
    side = core_side() if own else 1 - core_side()
    at = jnp.where(side == 0, y, x) if tuned() else 0 * y
    return jnp.stack([side, at.astype(jnp.int32)])


def exchange(value):
    return send(value, TO_CORE) if tuned() else jnp.zeros_like(value)


def scatter_steps(part):
    if not tuned():
        left, right = [jnp.stack(part(own)) for own in (True, False)]
        left = yield left
        for _ in range(7):
            left = yield left
        left = jnp.transpose(left, (0, 2, 1, 3, 4))
        right = jnp.transpose(right, (1, 2, 0, 3, 4))
        full = jnp.concatenate([left, right], axis=4)
        full = lax.psum_scatter(
            full.reshape(-1, full.shape[4]), ("tensor", "dp"), scatter_dimension=0, tiled=True
        )
        full = lax.optimization_barrier(full).astype(jnp.float32)
        yield tuple(jnp.split(full, 2, axis=1))
        return
    z, x, c, y = coords()
    first = c == 0
    stay, away = part(True)
    away = yield away
    got = yield send(away, TO_FAR)
    total = low(add(stay, got))
    at = jnp.where(first, x, y)
    away = yield pick(total, 1 - at)
    got = yield send(away, TO_NEAR)
    total = low(add(pick(total, at), got))
    away = yield [pick(total, (z - k) % ZS) for k in (1, 2, 3)]
    got = yield [send(piece, TO_DEPTH[k + 1]) for k, piece in enumerate(away)]
    total = pick(total, z).astype(jnp.float32)
    for piece in got:
        total = total + piece.astype(jnp.float32)
    total = total.reshape(2, -1, total.shape[1])
    away = yield pick(total, 1 - c)
    got = yield send(away, TO_CORE)
    keep = pick(total, c)
    yield jnp.where(first, keep, got), jnp.where(first, got, keep)


def dot_nn(left, right):
    return lax.dot_general(left, right, (((1,), (0,)), ((), ())), preferred_element_type=jnp.float32)


def dot_nt(left, right):
    return lax.dot_general(left, right, (((1,), (1,)), ((), ())), preferred_element_type=jnp.float32)


def flip(value):
    return jnp.swapaxes(value, 0, 1)


def load_set(side_ref, mine_ref, other_ref, left, right, sems, only=None):
    count = mine_ref.shape[3]

    def start(left_ref, right_ref):
        for y in range(2) if only is None else (only,):
            at = y if only is None else 0
            for x in range(2):
                for z in range(ZS):
                    cut = pl.ds((z * 2 + x) * count, count)
                    pltpu.make_async_copy(left_ref.at[y, x, z], left.at[at, cut], sems.at[0]).start()
                    pltpu.make_async_copy(right_ref.at[x, y, z], right.at[at, cut], sems.at[1]).start()

    @pl.when(side_ref[0] == 0)
    def _():
        start(mine_ref, other_ref)

    @pl.when(side_ref[0] != 0)
    def _():
        start(other_ref, mine_ref)


def load_halves(side_ref, mine_ref, other_ref, mine, other, sems):
    count = mine_ref.shape[3]

    def start(flipped):
        for y in range(2):
            for x in range(2):
                for z in range(ZS):
                    cut = pl.ds((z * 2 + x) * count, count)
                    for source, target, sem, turned in (
                        (mine_ref, mine, sems.at[0], flipped), (other_ref, other, sems.at[1], not flipped),
                    ):
                        block = source.at[x, y, z] if turned else source.at[y, x, z]
                        pltpu.make_async_copy(block, target.at[y, cut], sem).start()

    @pl.when(side_ref[0] == 0)
    def _():
        start(False)

    @pl.when(side_ref[0] != 0)
    def _():
        start(True)


def wait_set(left, right, sems):
    pltpu.make_async_copy(left, left, sems.at[0]).wait()
    pltpu.make_async_copy(right, right, sems.at[1]).wait()


def set_scratch(weights, count=2):
    width, cols = 8 * weights[0].shape[3], weights[0].shape[4]
    buffer = pltpu.VMEM((count, width, cols), jnp.bfloat16)
    return [buffer, buffer, pltpu.SemaphoreType.DMA((2,))]


def set_specs():
    return [
        pl.BlockSpec(memory_space=pltpu.SMEM),
        pl.BlockSpec(memory_space=pl.ANY),
        pl.BlockSpec(memory_space=pl.ANY),
    ]


def set_args(weights):
    return weights[2], weights[0], weights[1]


def params():
    return pltpu.CompilerParams(vmem_limit_bytes=VMEM)


def pair_cols(left, right, at):
    start = at * LANES
    width = left.shape[-1]
    if start < width:
        return left[:, start : start + LANES]
    return right[:, start - width : start - width + LANES]


def by_head(value):
    lane = lax.broadcasted_iota(jnp.int32, value.shape, 1)
    blank = jnp.zeros_like(value)
    return jnp.concatenate([jnp.where(lane < HDIM, value, blank), jnp.where(lane < HDIM, blank, value)], axis=0)


def own_heads(value):
    return jnp.concatenate([value[:HDIM, :SEQ], value[HDIM:, SEQ:]], axis=0)


def attend_kernel(t, carried, side_ref, mine_ref, other_ref, x_ref, row_ref, col_ref, *refs):
    pa_ref, pb_ref, e_ref, att_ref, flat_ref, inv_ref, bias_ref, a_ref, b_ref, sems = refs[carried:]
    pairs = flat_ref.shape[2] // LANES
    load_set(side_ref, mine_ref, other_ref, a_ref, b_ref, sems, t)
    wait_set(a_ref, b_ref, sems)

    x = x_ref[...]
    pa_ref[0] = low(dot_nn(x, a_ref[0]))
    pb_ref[0] = low(dot_nn(x, b_ref[0, :, : pb_ref.shape[2]]))
    bias = jnp.where(col_ref[0, :, :1] == row_ref[0], 0.0, -1e30)
    bias_ref[:, :SEQ] = bias
    bias_ref[:, SEQ:] = bias
    left, right = pa_ref[0], pb_ref[0]
    for p in range(pairs):
        queries = by_head(low(pair_cols(left, right, p).astype(jnp.float32) * HDIM**-0.5))
        key_rows = pair_cols(left, right, pairs + p)
        values_flat = flip(pair_cols(left, right, 2 * pairs + p))
        scores = dot_nt(key_rows, queries) + bias_ref[...]
        weights = jnp.exp(scores - jnp.max(scores, axis=0, keepdims=True))
        inverse = 1.0 / jnp.sum(weights, axis=0, keepdims=True)
        weights = low(weights)
        e_ref[0, p] = weights
        inv_ref[0, p : p + 1, :] = inverse
        flat = low(own_heads(dot_nn(values_flat, weights) * inverse))
        flat_ref[0, 0, p * LANES : (p + 1) * LANES, :] = flat
        at = p * LANES
        att_ref[at // EDGE, :, at % EDGE : at % EDGE + LANES] = flip(flat)
    at = pairs * LANES
    att_ref[at // EDGE, :, at % EDGE :] = jnp.zeros((SEQ, LANES), jnp.bfloat16)


def attend(tokens, weights, numbers, t, s, carry=()):
    rows, width = tokens.shape
    seqs = rows // SEQ
    cols = weights[0].shape[4]
    wide = (2 * cols - LANES) // 3
    pairs = wide // LANES
    used = cols - LANES
    bf = jnp.bfloat16
    at = lambda *index: (lambda i: index)
    return pl.pallas_call(
        functools.partial(attend_kernel, t, len(carry)),
        grid=(1,),
        in_specs=set_specs() + [
            pl.BlockSpec((SEQ, width), at(s, 0)),
            pl.BlockSpec((1, 1, SEQ), at(s, 0, 0)),
            pl.BlockSpec((1, SEQ, LANES), at(s, 0, 0)),
        ] + [pl.BlockSpec(memory_space=pl.ANY)] * len(carry),
        out_specs=[
            pl.BlockSpec((1, SEQ, cols), at(0, s, 0)),
            pl.BlockSpec((1, SEQ, used), at(0, s, 0)),
            pl.BlockSpec((1, pairs, SEQ, 2 * SEQ), at(s, 0, 0, 0)),
            pl.BlockSpec((2, SEQ, EDGE), at(0, s, 0)),
            pl.BlockSpec((1, 1, wide, SEQ), at(0, s, 0, 0)),
            pl.BlockSpec((1, pairs, 2 * SEQ), at(s, 0, 0)),
        ],
        out_shape=[
            jax.ShapeDtypeStruct((1, rows, cols), bf),
            jax.ShapeDtypeStruct((1, rows, used), bf),
            jax.ShapeDtypeStruct((seqs, pairs, SEQ, 2 * SEQ), bf),
            jax.ShapeDtypeStruct((2, rows, EDGE), bf),
            jax.ShapeDtypeStruct((1, seqs, wide, SEQ), bf),
            jax.ShapeDtypeStruct((seqs, pairs, 2 * SEQ), jnp.float32),
        ],
        input_output_aliases={6 + i: i for i in range(len(carry))},
        scratch_shapes=[pltpu.VMEM((SEQ, 2 * SEQ), jnp.float32)] + set_scratch(weights, 1),
        compiler_params=params(),
        cost_estimate=SMALL,
        name="attend",
    )(*set_args(weights), tokens, *numbers, *carry)


def attend_back_kernel(
    t, side_ref, mine_ref, other_ref, g_ref, pa_ref, pb_ref, e_ref, flat_ref, inv_ref,
    dm_ref, do_ref, w_ref, gt_ref, sem,
):
    wide = flat_ref.shape[2]
    pairs = wide // LANES
    count = mine_ref.shape[3]

    @pl.when(pl.program_id(0) == 0)
    def _():
        def start(left_ref, right_ref):
            cols = pl.ds(0, EDGE)
            for x in range(2):
                for z in range(ZS):
                    cut = pl.ds((z * 2 + x) * count, count)
                    pltpu.make_async_copy(left_ref.at[t, x, z, :, cols], w_ref.at[0, cut], sem).start()
                    pltpu.make_async_copy(right_ref.at[x, t, z, :, cols], w_ref.at[1, cut], sem).start()

        @pl.when(side_ref[0] == 0)
        def _():
            start(mine_ref, other_ref)

        @pl.when(side_ref[0] != 0)
        def _():
            start(other_ref, mine_ref)

        pltpu.make_async_copy(w_ref, w_ref, sem).wait()

    for side in range(2):
        size = min(EDGE, wide - side * EDGE)
        gt_ref[side * EDGE : side * EDGE + size] = flip(low(dot_nn(g_ref[...], w_ref[side, :, :size])))
    left, right = pa_ref[0], pb_ref[0]
    found = {}
    blank = jnp.zeros((HDIM, SEQ), jnp.bfloat16)
    for p in range(pairs):
        queries = by_head(pair_cols(left, right, p))
        keys_flat = flip(pair_cols(left, right, pairs + p))
        value_rows = pair_cols(left, right, 2 * pairs + p)
        flat = flat_ref[0, 0, p * LANES : (p + 1) * LANES, :].astype(jnp.float32)
        scaled, centre = [], []
        for half in range(2):
            rows = slice(half * HDIM, (half + 1) * HDIM)
            grads = gt_ref[p * LANES + half * HDIM : p * LANES + (half + 1) * HDIM, :].astype(jnp.float32)
            scaled.append(low(grads * inv_ref[0, p : p + 1, half * SEQ : (half + 1) * SEQ]))
            centre.append(jnp.sum(scaled[half].astype(jnp.float32) * flat[rows], axis=0, keepdims=True))
        grads = jnp.concatenate(
            [jnp.concatenate([scaled[0], blank], axis=0), jnp.concatenate([blank, scaled[1]], axis=0)], axis=1
        )
        weights = e_ref[0, p]
        grad_weights = dot_nn(value_rows, grads) - jnp.concatenate(centre, axis=1)
        grad_scores = low(weights.astype(jnp.float32) * grad_weights)
        found[p] = flip(low(own_heads(dot_nn(keys_flat, grad_scores)) * HDIM**-0.5))
        found[pairs + p] = low(dot_nn(grad_scores, queries) * HDIM**-0.5)
        found[2 * pairs + p] = low(dot_nn(weights, flip(grads)))
    found[3 * pairs] = jnp.zeros((SEQ, LANES), jnp.bfloat16)
    count = (3 * pairs + 1) // 2
    for at in range(count):
        cut = slice(at * LANES, (at + 1) * LANES)
        dm_ref[:, cut] = jnp.where(side_ref[0] == 0, found[at], found[at + count])
        do_ref[:, cut] = jnp.where(side_ref[0] == 0, found[at + count], found[at])


def attend_back(grad_branch, weights, kept, t):
    pa, pb, e, _, flat, inv = kept
    rows, width = grad_branch.shape
    seqs = rows // SEQ
    cols, used = pa.shape[2], pb.shape[2]
    wide = flat.shape[2]
    bf = jnp.bfloat16
    return pl.pallas_call(
        functools.partial(attend_back_kernel, t),
        grid=(seqs,),
        in_specs=set_specs() + [
            pl.BlockSpec((SEQ, width), lambda s: (s, 0)),
            pl.BlockSpec((1, SEQ, cols), lambda s: (0, s, 0)),
            pl.BlockSpec((1, SEQ, used), lambda s: (0, s, 0)),
            pl.BlockSpec((1,) + e.shape[1:], lambda s: (s, 0, 0, 0)),
            pl.BlockSpec((1, 1, wide, SEQ), lambda s: (0, s, 0, 0)),
            pl.BlockSpec((1,) + inv.shape[1:], lambda s: (s, 0, 0)),
        ],
        out_specs=[pl.BlockSpec((SEQ, cols), lambda s: (s, 0))] * 2,
        out_shape=[jax.ShapeDtypeStruct((rows, cols), bf)] * 2,
        scratch_shapes=[
            pltpu.VMEM((2, width, EDGE), bf),
            pltpu.VMEM((wide, SEQ), bf),
            pltpu.SemaphoreType.DMA,
        ],
        compiler_params=params(),
        cost_estimate=SMALL,
        name="attend_back",
    )(*set_args(weights), grad_branch, pa, pb, e, flat, inv)


def gelu_parts(v):
    below = 0.5 + 0.5 * lax.erf(v * 0.5**0.5)
    bell = jnp.exp(-0.5 * (v * v))
    return v * below, below + (0.3989422804014327 * v) * bell


def row_norm(value):
    centered = value - jnp.mean(value, axis=-1, keepdims=True)
    inverse = lax.rsqrt(jnp.mean(centered * centered, axis=-1, keepdims=True) + epsilon)
    return centered * inverse, inverse


def row_norm_back(grad_scaled, scaled, inverse):
    centered = grad_scaled - jnp.mean(grad_scaled, axis=-1, keepdims=True)
    return inverse * (centered - scaled * jnp.mean(grad_scaled * scaled, axis=-1, keepdims=True))


def widen_kernel(
    side_ref, mine_ref, other_ref, x_ref, u_ref, v_ref, n_ref,
    sum_ref, tok_ref, low_ref, hm_ref, ho_ref, sm_ref, so_ref, mine, other, sems,
):
    @pl.when(pl.program_id(0) == 0)
    def _():
        load_halves(side_ref, mine_ref, other_ref, mine, other, sems)
        wait_set(mine, other, sems)

    tok_ref[...] = flip(x_ref[...])
    total = x_ref[...].astype(jnp.float32)
    for t, ref in enumerate((u_ref, v_ref)):
        near = jnp.where(side_ref[0] == 0, ref[0], ref[1])
        away = jnp.where(side_ref[0] == 0, ref[1], ref[0])
        total = total + dot_nt(near, mine[t, :, :EDGE]) + dot_nt(away, other[t, :, :EDGE])
    sum_ref[...] = total
    scaled, _ = row_norm(total)
    x = low(scaled * n_ref[0:1, :] + n_ref[1:2, :])
    low_ref[...] = flip(x)
    half = mine.shape[2] - EDGE
    for t in range(2):
        for ref, hid_ref, slope_ref in ((mine, hm_ref, sm_ref), (other, ho_ref, so_ref)):
            for start in range(0, half, CHUNK):
                cut = slice(t * half + start, t * half + start + CHUNK)
                value, slope = gelu_parts(dot_nn(x, ref[t, :, EDGE + start : EDGE + start + CHUNK]))
                hid_ref[:, cut] = low(value)
                slope_ref[:, cut] = low(slope)


def widen(tokens, attended, weights, norms):
    rows, width = tokens.shape
    span = 2 * (weights[0].shape[4] - EDGE)
    bf = jnp.bfloat16
    by_row = lambda n: pl.BlockSpec((BLOCK, n), lambda r: (r, 0))
    full = lambda a: pl.BlockSpec(a.shape, lambda r: (0, 0))
    side = pl.BlockSpec((2, BLOCK, EDGE), lambda r: (0, r, 0))
    return pl.pallas_call(
        widen_kernel,
        grid=(rows // BLOCK,),
        in_specs=set_specs() + [by_row(width), side, side, full(norms)],
        out_specs=[by_row(width)] + [pl.BlockSpec((width, BLOCK), lambda r: (0, r))] * 2 + [by_row(span)] * 4,
        out_shape=[
            jax.ShapeDtypeStruct((rows, width), jnp.float32),
            jax.ShapeDtypeStruct((width, rows), bf),
            jax.ShapeDtypeStruct((width, rows), bf),
        ] + [jax.ShapeDtypeStruct((rows, span), bf)] * 4,
        scratch_shapes=set_scratch(weights),
        compiler_params=params(),
        cost_estimate=SMALL,
        name="widen",
    )(*set_args(weights), tokens, *attended, norms)


def middle_kernel(
    side_ref, mine_ref, other_ref, side_two_ref, mine_two_ref, other_two_ref,
    sum_ref, hm_ref, ho_ref, sm_ref, so_ref, n_ref, cot_ref,
    out_ref, gs_ref, gm_ref, go_ref, res_ref, gb_ref, gbt_ref, flat_ref,
    mine, other, sems, win_mine, win_other, win_sems, stat_ref,
):
    @pl.when(pl.program_id(0) == 0)
    def _():
        load_halves(side_ref, mine_ref, other_ref, mine, other, sems)
        load_halves(side_two_ref, mine_two_ref, other_two_ref, win_mine, win_other, win_sems)
        wait_set(mine, other, sems)

    gain_one, shift_one = n_ref[0:1, :], n_ref[1:2, :]
    gain_two, shift_two = n_ref[2:3, :], n_ref[3:4, :]
    scaled_one, inverse_one = row_norm(sum_ref[...])
    value = scaled_one * gain_one + shift_one
    half = mine.shape[2]
    for t in range(2):
        for ref, hid_ref in ((mine, hm_ref), (other, ho_ref)):
            value = value + dot_nt(hid_ref[:, t * half : (t + 1) * half], ref[t])
    scaled_two, inverse_two = row_norm(value)
    out_ref[...] = low(scaled_two * gain_two + shift_two)
    cotangent = cot_ref[...].astype(jnp.float32)
    grad_two = row_norm_back(cotangent * gain_two, scaled_two, inverse_two)
    grad_second = low(grad_two)
    gs_ref[...] = flip(grad_second)
    for t in range(2):
        for ref, slope_ref, gi_ref in ((mine, sm_ref, gm_ref), (other, so_ref, go_ref)):
            for start in range(0, half, CHUNK):
                cut = slice(t * half + start, t * half + start + CHUNK)
                grad_hidden = dot_nn(grad_second, ref[t, :, start : start + CHUNK])
                gi_ref[:, cut] = low(grad_hidden * slope_ref[:, cut].astype(jnp.float32))

    @pl.when(pl.program_id(0) == 0)
    def _():
        wait_set(win_mine, win_other, win_sems)
        stat_ref[...] = jnp.zeros_like(stat_ref)

    grad_first = grad_two
    for t in range(2):
        for ref, gi_ref in ((win_mine, gm_ref), (win_other, go_ref)):
            grad_first = grad_first + dot_nt(gi_ref[:, t * half : (t + 1) * half], ref[t, :, EDGE:])
    grad_one = row_norm_back(grad_first * gain_one, scaled_one, inverse_one)
    res_ref[...] = grad_one
    gb_ref[...] = low(grad_one)
    gbt_ref[...] = flip(low(grad_one))
    for row, value in enumerate((grad_first * scaled_one, grad_first, cotangent * scaled_two, cotangent)):
        stat_ref[row : row + 1, :] += jnp.sum(value, axis=0, keepdims=True)

    @pl.when(pl.program_id(0) == pl.num_programs(0) - 1)
    def _():
        flat_ref[...] = flip(stat_ref[...])


def middle(total, hidden, slope, weights_down, weights_in, norms, cotangent):
    rows, width = total.shape
    span = hidden[0].shape[1]
    bf = jnp.bfloat16
    by_row = lambda n: pl.BlockSpec((BLOCK, n), lambda r: (r, 0))
    by_col = pl.BlockSpec((width, BLOCK), lambda r: (0, r))
    full = lambda a: pl.BlockSpec(a.shape, lambda r: (0, 0))
    return pl.pallas_call(
        middle_kernel,
        grid=(rows // BLOCK,),
        in_specs=set_specs() * 2 + [by_row(width)] + [by_row(span)] * 4 + [full(norms), by_row(width)],
        out_specs=[
            by_row(width), by_col, by_row(span), by_row(span), by_row(width), by_row(width), by_col,
            pl.BlockSpec((width, LANES), lambda r: (0, 0)),
        ],
        out_shape=[
            jax.ShapeDtypeStruct((rows, width), bf),
            jax.ShapeDtypeStruct((width, rows), bf),
            jax.ShapeDtypeStruct((rows, span), bf),
            jax.ShapeDtypeStruct((rows, span), bf),
            jax.ShapeDtypeStruct((rows, width), jnp.float32),
            jax.ShapeDtypeStruct((rows, width), bf),
            jax.ShapeDtypeStruct((width, rows), bf),
            jax.ShapeDtypeStruct((width, LANES), jnp.float32),
        ],
        scratch_shapes=set_scratch(weights_down) + set_scratch(weights_in) + [pltpu.VMEM((LANES, width), jnp.float32)],
        compiler_params=params(),
        cost_estimate=SMALL,
        name="middle",
    )(*set_args(weights_down), *set_args(weights_in), total, *hidden, *slope, norms, cotangent)


def store_rows(place_ref, t, refs, value, cut):
    stay_ref, away_ref = refs
    count = stay_ref.shape[2]
    for x in range(2):
        a = jnp.where(place_ref[0] == 0, t, x)
        b = jnp.where(place_ref[0] == 0, x, t)
        for z in range(ZS):
            start = (z * 2 + x) * count
            piece = low(value[start : start + count])

            @pl.when(a == place_ref[1])
            def _():
                stay_ref[b, z, :, cut] = piece

            @pl.when(a != place_ref[1])
            def _():
                away_ref[b, z, :, cut] = piece


def weigh_kernel(jobs, place_ref, stats_ref, stats_got_ref, *refs):
    refs = list(refs)
    sources = [refs.pop(0) for _ in range(6 * len(jobs))]
    outs = refs.pop(0), refs.pop(0)
    *buffers, sems = refs
    copies = []
    for j, (views, start, size) in enumerate(jobs):
        flat_buf, value_buf = buffers[2 * j], buffers[2 * j + 1]
        rows = flat_buf.shape[1] // 2
        low_part, high_part = pl.ds(0, rows), pl.ds(rows, rows)
        targets = [
            flat_buf.at[:, low_part], flat_buf.at[:, high_part],
            value_buf.at[0, low_part], value_buf.at[0, high_part],
            value_buf.at[1, low_part], value_buf.at[1, high_part],
        ]
        copies.append([
            pltpu.make_async_copy(view(source, place_ref), target, sems.at[6 * j + i])
            for i, (view, source, target) in enumerate(zip(views, sources[6 * j : 6 * j + 6], targets))
        ])
    for group in copies:
        for copy in group:
            copy.start()
    for j, (_, start, size) in enumerate(jobs):
        flat_buf, value_buf = buffers[2 * j], buffers[2 * j + 1]
        for t in range(2):
            for copy in copies[j][2 + 2 * t : 4 + 2 * t] + (copies[j][:2] if t == 0 else []):
                copy.wait()
            value = dot_nn(flat_buf[...], value_buf[t])
            if stats_ref.shape[0] == value.shape[0]:
                edge = size - LANES
                store_rows(place_ref, t, outs, value[:, :edge], slice(start, start + edge))
                value = jnp.where(place_ref[0] == 0, value[:, edge:], stats_ref[...] + stats_got_ref[...])
                store_rows(place_ref, t, outs, value, slice(start + edge, start + size))
            else:
                store_rows(place_ref, t, outs, value, slice(start, start + size))


def weigh_call(place, stats, stats_got, *jobs):
    width, rows = jobs[0][0][0].shape
    cols = sum(job[2] for job in jobs)
    shape = (2, ZS, width // (2 * ZS), cols)
    bf = jnp.bfloat16
    arrays, plan, scratch, start = [], [], [], 0
    for values, views, size in jobs:
        arrays += values
        plan.append((views, start, size))
        scratch += [pltpu.VMEM((width, 2 * rows), bf), pltpu.VMEM((2, 2 * rows, size), bf)]
        start += size
    return pl.pallas_call(
        functools.partial(weigh_kernel, plan),
        in_specs=[pl.BlockSpec(memory_space=pltpu.SMEM)] + [pl.BlockSpec(memory_space=pltpu.VMEM)] * 2
        + [pl.BlockSpec(memory_space=pl.ANY)] * len(arrays),
        out_specs=[pl.BlockSpec(memory_space=pltpu.VMEM)] * 2,
        out_shape=[jax.ShapeDtypeStruct(shape, bf)] * 2,
        scratch_shapes=scratch + [pltpu.SemaphoreType.DMA((len(arrays),))],
        compiler_params=params(),
        cost_estimate=SMALL,
        name="weigh",
    )(place, stats, stats_got, *arrays)


def whole(ref, place_ref):
    return ref


def half_of(t, size):
    return lambda ref, place_ref: ref.at[:, pl.ds(t * size, size)]


def halved(flat, value, flat_got, value_got):
    size = value.shape[1] // 2
    views = [whole, whole, half_of(0, size), half_of(0, size), half_of(1, size), half_of(1, size)]
    return [flat, flat_got, value, value_got, value, value_got], views, size


def weigh(place, *args):
    none = jnp.zeros((8, LANES), jnp.float32)
    return weigh_call(place, none, none, halved(*args))


def weigh_more(place, flat, value, flat_got, value_got, flat_two, u, v, flat_two_got, u_got, v_got):
    own = lambda ref, place_ref: ref.at[place_ref[0]]
    views = [whole, whole, own, whole, own, whole]
    none = jnp.zeros((8, LANES), jnp.float32)
    return weigh_call(
        place, none, none,
        ([flat_two, flat_two_got, u, u_got, v, v_got], views, EDGE),
        halved(flat, value, flat_got, value_got),
    )


def weigh_last(place, flat, u, v, flat_got, u_got, v_got, stats, stats_got):
    return weigh_call(place, stats, stats_got, ([flat, flat_got, u, u_got, v, v_got], [whole] * 6, u.shape[1]))


def input_kernel(side_ref, mine_ref, other_ref, res_ref, um_ref, uo_ref, vm_ref, vo_ref, out_ref, mine, other, sems):
    @pl.when(pl.program_id(0) == 0)
    def _():
        load_halves(side_ref, mine_ref, other_ref, mine, other, sems)
        wait_set(mine, other, sems)

    total = res_ref[...]
    for t, (near, away) in enumerate(((um_ref, uo_ref), (vm_ref, vo_ref))):
        total = total + dot_nt(near[...], mine[t]) + dot_nt(away[...], other[t])
    out_ref[...] = low(total)


def input_back(resid, parts, weights):
    rows, width = resid.shape
    by_row = lambda n: pl.BlockSpec((BLOCK, n), lambda r: (r, 0))
    return pl.pallas_call(
        input_kernel,
        grid=(rows // BLOCK,),
        in_specs=set_specs() + [by_row(width)] + [by_row(parts[0][0].shape[1])] * 4,
        out_specs=by_row(width),
        out_shape=jax.ShapeDtypeStruct((rows, width), jnp.bfloat16),
        scratch_shapes=set_scratch(weights),
        compiler_params=params(),
        cost_estimate=SMALL,
        name="input_back",
    )(*set_args(weights), resid, *parts[0], *parts[1])


def halves(value):
    return jnp.split(value, 2, axis=-1)


def shards(
    tokens,
    segment,
    weight_qkv,
    weight_out,
    weight_in,
    weight_down,
    gain_one,
    shift_one,
    gain_two,
    shift_two,
    cotangent,
):
    rows, width = tokens.shape
    own = weight_qkv.shape[1]
    wide = weight_out.shape[0]
    half_span = weight_in.shape[1]
    bf = jnp.bfloat16

    norms = jnp.stack([gain_one, shift_one, gain_two, shift_two], axis=1)
    norms = jnp.pad(norms, ((0, 0), (0, LANES - 4)))
    set_one = jnp.concatenate([jnp.transpose(weight_qkv, (1, 0, 2)).reshape(own, -1), norms], axis=1)
    one = Flow(gather_steps(*halves(set_one)))
    one.go(2)
    weight_out, weight_in, weight_down, tokens, segment = sync(
        one, weight_out, weight_in, weight_down, tokens, segment
    )
    one.go()
    out_flat, half = weight_out.T, half_span // 2
    out_flat = jnp.pad(out_flat, ((0, 0), (0, 2 * EDGE - wide)))
    two = Flow(gather_steps(*[
        jnp.concatenate([o, w], axis=1) for o, w in zip(halves(out_flat), halves(weight_in))
    ]))
    three = Flow(gather_steps(*halves(weight_down.T)))
    two.go(2)
    three.go(2)
    numbers = lax.dynamic_slice_in_dim(segment, lax.axis_index("tensor") * rows, rows)
    numbers = numbers.reshape(-1, 1, SEQ), jnp.broadcast_to(numbers[:, None], (rows, LANES)).reshape(-1, SEQ, LANES)
    tokens, numbers = sync(one, two, three, tokens, numbers)
    one.go()
    sync(one, two)
    one.go()
    two.go()
    two.value = hold(two.value, one)
    one.go()
    one.go()
    sync(one, two)
    one.go()
    two.go()
    sync(one, two, three)
    one.go()
    two.go()
    tokens = sync(one, tokens)
    weights_one = one.go()
    kept = [attend(tokens, weights_one, numbers, 0, 0), None]
    tokens, kept[0] = sync(two, three, tokens, kept[0])
    two.go()
    tokens = sync(two, tokens)
    two.go()
    three.go()
    kept[0] = attend(tokens, weights_one, numbers, 0, 1, kept[0])
    tokens, kept[0] = sync(tokens, kept[0])
    kept[1] = attend(tokens, weights_one, numbers, 1, 0)
    tokens, kept[1] = sync(two, three, tokens, kept[1])
    two.go()
    three.go()
    tokens, kept[1] = sync(two, three, tokens, kept[1])
    two.go()
    three.go()
    first_mine, first_other, first_side = weights_one
    norms = jnp.where(first_side[0] == 0, first_other, first_mine)[:, 0, :, :, first_mine.shape[4] - LANES :]
    norms = jnp.transpose(norms, (1, 0, 2, 3)).reshape(width, LANES)[:, :8].T.astype(jnp.float32)
    kept[1] = attend(tokens, weights_one, numbers, 1, 1, kept[1])
    tokens, kept[1], norms = sync(two, three, tokens, kept[1], norms)
    three.go()
    tokens = sync(three, tokens)
    three.go()
    weights_two = two.go()
    attended = [kept[t][3] for t in range(2)]
    attended_got = [exchange(lax.dynamic_index_in_dim(value, 1 - core_side(), 0, keepdims=False)) for value in attended]
    total, tokens_flat, low_flat, *wide_out = widen(tokens, attended, weights_two, norms)
    hidden, slope = wide_out[:2], wide_out[2:]
    total, tokens_flat, low_flat, hidden, attended_got = sync(
        three, total, tokens_flat, low_flat, hidden, attended_got
    )
    three.go(2)
    weights_three = three.go()
    weights_three, away, low_flat, tokens_flat = sync(weights_three, hidden[1], low_flat, tokens_flat)
    hidden_got, low_got, tokens_got = exchange(away), exchange(low_flat), exchange(tokens_flat)
    output, second_flat, inner_mine, inner_other, grad_resid_one, grad_branch, branch_flat, stats = middle(
        total, hidden, slope, weights_three, weights_two, norms, cotangent
    )
    second_flat, hidden_got, low_got, tokens_got, inner_other, branch_flat, stats = sync(
        second_flat, hidden_got, low_got, tokens_got, inner_other, branch_flat, stats
    )
    second_got = exchange(second_flat)
    second_got, inner_other, branch_flat, stats = sync(second_got, inner_other, branch_flat, stats)
    inner_got, branch_got, stats_got = exchange(inner_other), exchange(branch_flat), exchange(stats)
    three = Flow(scatter_steps(lambda own: weigh(
        place_of(own), second_flat, hidden[0 if own else 1], second_got, hidden_got
    )))
    inner_mine, inner_got, branch_got, stats_got = sync(three, inner_mine, inner_got, branch_got, stats_got)
    three.go()
    two = Flow(scatter_steps(lambda own: weigh_more(
        place_of(own), low_flat, inner_mine if own else inner_other, low_got, inner_got,
        branch_flat, *attended, branch_got, *attended_got,
    )))
    grad_branch = sync(two, grad_branch)
    two.go()
    parts = [attend_back(grad_branch, weights_two, kept[0], 0)]
    parts[0] = sync(three, parts[0])
    three.go()
    grad_branch, kept[1], parts[0] = sync(three, grad_branch, kept[1], parts[0])
    three.go()
    parts_got = [exchange(parts[0][1])]
    parts.append(attend_back(grad_branch, weights_two, kept[1], 1))
    parts, parts_got = sync(two, three, parts, parts_got)
    parts_got.append(exchange(parts[1][1]))
    two.go()
    three.go()
    parts, parts_got = sync(two, three, parts, parts_got)
    two.go()
    three.go()
    one = Flow(scatter_steps(lambda own: weigh_last(
        place_of(own), tokens_flat, *[value[0 if own else 1] for value in parts], tokens_got, *parts_got, stats, stats_got
    )))
    grad_resid_one = sync(one, two, three, grad_resid_one)
    one.go()
    two.go()
    two.go()
    three.go(2)
    input_grad = input_back(grad_resid_one, parts, weights_one)
    input_grad = sync(one, two, input_grad)
    one.go()
    one.go()
    two.go(2)
    sync(one, two)
    one.go()
    one.go()
    one.go(2)
    sum_one = jnp.concatenate(one.go(), axis=1)
    two_left, two_right = two.go()
    sum_three = jnp.concatenate(three.go(), axis=1)
    stats = sum_one[:, 3 * wide : 3 * wide + 4].T
    sum_out = jnp.concatenate([two_left[:, :EDGE], two_right[:, :EDGE]], axis=1)[:, :wide]
    return (
        output,
        input_grad,
        jnp.transpose(sum_one[:, : 3 * wide].reshape(own, 3, -1), (1, 0, 2)),
        sum_out.T,
        jnp.concatenate([two_left[:, EDGE:], two_right[:, EDGE:]], axis=1),
        sum_three.T,
        stats[0],
        stats[1],
        stats[2],
        stats[3],
    )


def solution(mesh):
    both = P(("dp", "tensor"), None)
    split = P("dp")
    qkv_spec = P(None, "dp", "tensor")
    row_spec = P("tensor", "dp")
    in_spec = P("dp", "tensor")
    return jax.shard_map(
        shards,
        mesh=mesh,
        in_specs=(both, split, qkv_spec, row_spec, in_spec, row_spec, split, split, split, split, both),
        out_specs=(both, both, qkv_spec, row_spec, in_spec, row_spec, split, split, split, split),
        check_vma=False,
    )
```

```python
import functools

import jax
import jax.numpy as jnp
from jax import lax
from jax.experimental import pallas as pl
from jax.experimental.pallas import tpu as pltpu
from jax.sharding import PartitionSpec as P

HDIM = 64
SEQ = 512
LANES = 128
EDGE = 256
BLOCK = 256
CHUNK = 256
VMEM = 56 * 1024 * 1024
epsilon = 1e-05
SMALL = pl.CostEstimate(flops=100_000_000, bytes_accessed=100_000, transcendentals=0)


def low(value):
    return value.astype(jnp.bfloat16)


AXES = ("dp", "tensor")
ZS = 4


def place(z, x, c, y):
    return ((z * 2 + x) * 2 + c) * 2 + y


def pairs(move):
    found = []
    for z in range(ZS):
        for x in range(2):
            for c in range(2):
                for y in range(2):
                    found.append((place(z, x, c, y), place(*move(z, x, c, y))))
    return found


TO_CORE = pairs(lambda z, x, c, y: (z, x, 1 - c, y))
TO_NEAR = pairs(lambda z, x, c, y: (z, x, c, 1 - y) if c else (z, 1 - x, c, y))
TO_FAR = pairs(lambda z, x, c, y: (z, 1 - x, c, y) if c else (z, x, c, 1 - y))
TO_DEPTH = [pairs(lambda z, x, c, y: ((z - k) % ZS, x, c, y)) for k in range(ZS)]


def coords():
    d = lax.axis_index("dp")
    y = lax.axis_index("tensor")
    return d // 4, (d // 2) % 2, d % 2, y


def send(value, route):
    return lax.ppermute(value, AXES, route)


def in_order(own, other, at):
    return jnp.where(at == 0, jnp.stack([own, other]), jnp.stack([other, own]))


def tuned():
    return lax.axis_size("dp") == 16 and lax.axis_size("tensor") == 2


def sync(*values):
    found = lax.optimization_barrier([value.value if isinstance(value, Flow) else value for value in values])
    for value, new in zip(values, found):
        if isinstance(value, Flow):
            value.value = new
    found = [new for value, new in zip(values, found) if not isinstance(value, Flow)]
    return found[0] if len(found) == 1 else found


def hold(pieces, *values):
    if not isinstance(pieces, list):
        return pieces
    return [*pieces[:-1], sync(pieces[-1], *values)]


class Flow:
    def __init__(self, steps):
        self.steps = steps
        self.value = next(steps)

    def go(self, count=1):
        for _ in range(count):
            self.value = self.steps.send(self.value)
        return self.value


def gather_steps(left, right):
    if not tuned():
        for _ in range(10):
            left = yield left
        full = lax.all_gather(jnp.concatenate([left, right], axis=1), ("tensor", "dp"), axis=0, tiled=True)
        full = full.reshape(2, ZS, 2, -1, full.shape[1])
        left, right = jnp.split(full, 2, axis=4)
        left = jnp.transpose(left, (0, 2, 1, 3, 4))
        right = jnp.transpose(right, (2, 0, 1, 3, 4))
        yield left, right, jnp.zeros((1,), jnp.int32)
        return
    z, x, c, y = coords()
    first = c == 0
    own = yield jnp.where(first, right, left)
    got = yield send(own, TO_CORE)
    mine = jnp.where(first, jnp.concatenate([left, got]), jnp.concatenate([got, right]))
    mine = yield mine
    got = yield [send(mine, TO_DEPTH[k]) for k in (1, 2, 3)]
    column = jnp.stack([mine, *got, mine, *got[:2]])
    column = yield lax.dynamic_slice_in_dim(column, (ZS - z) % ZS, ZS, 0)
    near = yield send(column, TO_NEAR)
    plane = yield in_order(column, near, jnp.where(first, x, y))
    far = yield send(plane, TO_FAR)
    whole = yield in_order(plane, far, jnp.where(first, y, x))
    sibling = yield send(whole, TO_CORE)
    yield whole, sibling, c.astype(jnp.int32).reshape(1)


def add(a, b):
    return a.astype(jnp.float32) + b.astype(jnp.float32)


def pick(value, at):
    return lax.dynamic_index_in_dim(value, at, 0, keepdims=False)


def core_side():
    return coords()[2].astype(jnp.int32) if tuned() else jnp.int32(0)


def place_of(own):
    _, x, _, y = coords()
    side = core_side() if own else 1 - core_side()
    at = jnp.where(side == 0, y, x) if tuned() else 0 * y
    return jnp.stack([side, at.astype(jnp.int32)])


def exchange(value):
    return send(value, TO_CORE) if tuned() else jnp.zeros_like(value)


def scatter_steps(part):
    if not tuned():
        left, right = [jnp.stack(part(own)) for own in (True, False)]
        left = yield left
        for _ in range(7):
            left = yield left
        left = jnp.transpose(left, (0, 2, 1, 3, 4))
        right = jnp.transpose(right, (1, 2, 0, 3, 4))
        full = jnp.concatenate([left, right], axis=4)
        full = lax.psum_scatter(
            full.reshape(-1, full.shape[4]), ("tensor", "dp"), scatter_dimension=0, tiled=True
        )
        full = lax.optimization_barrier(full).astype(jnp.float32)
        yield tuple(jnp.split(full, 2, axis=1))
        return
    z, x, c, y = coords()
    first = c == 0
    stay, away = part(True)
    away = yield away
    got = yield send(away, TO_FAR)
    total = low(add(stay, got))
    at = jnp.where(first, x, y)
    away = yield pick(total, 1 - at)
    got = yield send(away, TO_NEAR)
    total = low(add(pick(total, at), got))
    away = yield [pick(total, (z - k) % ZS) for k in (1, 2, 3)]
    got = yield [send(piece, TO_DEPTH[k + 1]) for k, piece in enumerate(away)]
    total = pick(total, z).astype(jnp.float32)
    for piece in got:
        total = total + piece.astype(jnp.float32)
    total = total.reshape(2, -1, total.shape[1])
    away = yield pick(total, 1 - c)
    got = yield send(away, TO_CORE)
    keep = pick(total, c)
    yield jnp.where(first, keep, got), jnp.where(first, got, keep)


def dot_nn(left, right):
    return lax.dot_general(left, right, (((1,), (0,)), ((), ())), preferred_element_type=jnp.float32)


def dot_nt(left, right):
    return lax.dot_general(left, right, (((1,), (1,)), ((), ())), preferred_element_type=jnp.float32)


def flip(value):
    return jnp.swapaxes(value, 0, 1)


def load_set(side_ref, mine_ref, other_ref, left, right, sems, only=None):
    count = mine_ref.shape[3]

    def start(left_ref, right_ref):
        for y in range(2) if only is None else (only,):
            at = y if only is None else 0
            for x in range(2):
                for z in range(ZS):
                    cut = pl.ds((z * 2 + x) * count, count)
                    pltpu.make_async_copy(left_ref.at[y, x, z], left.at[at, cut], sems.at[0]).start()
                    pltpu.make_async_copy(right_ref.at[x, y, z], right.at[at, cut], sems.at[1]).start()

    @pl.when(side_ref[0] == 0)
    def _():
        start(mine_ref, other_ref)

    @pl.when(side_ref[0] != 0)
    def _():
        start(other_ref, mine_ref)


def load_halves(side_ref, mine_ref, other_ref, mine, other, sems):
    count = mine_ref.shape[3]

    def start(flipped):
        for y in range(2):
            for x in range(2):
                for z in range(ZS):
                    cut = pl.ds((z * 2 + x) * count, count)
                    for source, target, sem, turned in (
                        (mine_ref, mine, sems.at[0], flipped), (other_ref, other, sems.at[1], not flipped),
                    ):
                        block = source.at[x, y, z] if turned else source.at[y, x, z]
                        pltpu.make_async_copy(block, target.at[y, cut], sem).start()

    @pl.when(side_ref[0] == 0)
    def _():
        start(False)

    @pl.when(side_ref[0] != 0)
    def _():
        start(True)


def wait_set(left, right, sems):
    pltpu.make_async_copy(left, left, sems.at[0]).wait()
    pltpu.make_async_copy(right, right, sems.at[1]).wait()


def set_scratch(weights, count=2):
    width, cols = 8 * weights[0].shape[3], weights[0].shape[4]
    buffer = pltpu.VMEM((count, width, cols), jnp.bfloat16)
    return [buffer, buffer, pltpu.SemaphoreType.DMA((2,))]


def set_specs():
    return [
        pl.BlockSpec(memory_space=pltpu.SMEM),
        pl.BlockSpec(memory_space=pl.ANY),
        pl.BlockSpec(memory_space=pl.ANY),
    ]


def set_args(weights):
    return weights[2], weights[0], weights[1]


def params():
    return pltpu.CompilerParams(vmem_limit_bytes=VMEM)


def pair_cols(left, right, at):
    start = at * LANES
    width = left.shape[-1]
    if start < width:
        return left[:, start : start + LANES]
    return right[:, start - width : start - width + LANES]


def by_head(value):
    lane = lax.broadcasted_iota(jnp.int32, value.shape, 1)
    blank = jnp.zeros_like(value)
    return jnp.concatenate([jnp.where(lane < HDIM, value, blank), jnp.where(lane < HDIM, blank, value)], axis=0)


def own_heads(value):
    return jnp.concatenate([value[:HDIM, :SEQ], value[HDIM:, SEQ:]], axis=0)


def attend_kernel(t, carried, side_ref, mine_ref, other_ref, x_ref, row_ref, col_ref, *refs):
    pa_ref, pb_ref, e_ref, att_ref, flat_ref, inv_ref, bias_ref, a_ref, b_ref, sems = refs[carried:]
    pairs = flat_ref.shape[2] // LANES
    load_set(side_ref, mine_ref, other_ref, a_ref, b_ref, sems, t)
    wait_set(a_ref, b_ref, sems)

    x = x_ref[...]
    pa_ref[0] = low(dot_nn(x, a_ref[0]))
    pb_ref[0] = low(dot_nn(x, b_ref[0, :, : pb_ref.shape[2]]))
    bias = jnp.where(col_ref[0, :, :1] == row_ref[0], 0.0, -1e30)
    bias_ref[:, :SEQ] = bias
    bias_ref[:, SEQ:] = bias
    left, right = pa_ref[0], pb_ref[0]
    for p in range(pairs):
        queries = by_head(low(pair_cols(left, right, p).astype(jnp.float32) * HDIM**-0.5))
        key_rows = pair_cols(left, right, pairs + p)
        values_flat = flip(pair_cols(left, right, 2 * pairs + p))
        scores = dot_nt(key_rows, queries) + bias_ref[...]
        weights = jnp.exp(scores - jnp.max(scores, axis=0, keepdims=True))
        inverse = 1.0 / jnp.sum(weights, axis=0, keepdims=True)
        weights = low(weights)
        e_ref[0, p] = weights
        inv_ref[0, p : p + 1, :] = inverse
        flat = low(own_heads(dot_nn(values_flat, weights) * inverse))
        flat_ref[0, 0, p * LANES : (p + 1) * LANES, :] = flat
        at = p * LANES
        att_ref[at // EDGE, :, at % EDGE : at % EDGE + LANES] = flip(flat)
    at = pairs * LANES
    att_ref[at // EDGE, :, at % EDGE :] = jnp.zeros((SEQ, LANES), jnp.bfloat16)


def attend(tokens, weights, numbers, t, s, carry=()):
    rows, width = tokens.shape
    seqs = rows // SEQ
    cols = weights[0].shape[4]
    wide = (2 * cols - LANES) // 3
    pairs = wide // LANES
    used = cols - LANES
    bf = jnp.bfloat16
    at = lambda *index: (lambda i: index)
    return pl.pallas_call(
        functools.partial(attend_kernel, t, len(carry)),
        grid=(1,),
        in_specs=set_specs() + [
            pl.BlockSpec((SEQ, width), at(s, 0)),
            pl.BlockSpec((1, 1, SEQ), at(s, 0, 0)),
            pl.BlockSpec((1, SEQ, LANES), at(s, 0, 0)),
        ] + [pl.BlockSpec(memory_space=pl.ANY)] * len(carry),
        out_specs=[
            pl.BlockSpec((1, SEQ, cols), at(0, s, 0)),
            pl.BlockSpec((1, SEQ, used), at(0, s, 0)),
            pl.BlockSpec((1, pairs, SEQ, 2 * SEQ), at(s, 0, 0, 0)),
            pl.BlockSpec((2, SEQ, EDGE), at(0, s, 0)),
            pl.BlockSpec((1, 1, wide, SEQ), at(0, s, 0, 0)),
            pl.BlockSpec((1, pairs, 2 * SEQ), at(s, 0, 0)),
        ],
        out_shape=[
            jax.ShapeDtypeStruct((1, rows, cols), bf),
            jax.ShapeDtypeStruct((1, rows, used), bf),
            jax.ShapeDtypeStruct((seqs, pairs, SEQ, 2 * SEQ), bf),
            jax.ShapeDtypeStruct((2, rows, EDGE), bf),
            jax.ShapeDtypeStruct((1, seqs, wide, SEQ), bf),
            jax.ShapeDtypeStruct((seqs, pairs, 2 * SEQ), jnp.float32),
        ],
        input_output_aliases={6 + i: i for i in range(len(carry))},
        scratch_shapes=[pltpu.VMEM((SEQ, 2 * SEQ), jnp.float32)] + set_scratch(weights, 1),
        compiler_params=params(),
        cost_estimate=SMALL,
        name="attend",
    )(*set_args(weights), tokens, *numbers, *carry)


def attend_back_kernel(
    t, side_ref, mine_ref, other_ref, g_ref, pa_ref, pb_ref, e_ref, flat_ref, inv_ref,
    dm_ref, do_ref, w_ref, gt_ref, sem,
):
    wide = flat_ref.shape[2]
    pairs = wide // LANES
    count = mine_ref.shape[3]

    @pl.when(pl.program_id(0) == 0)
    def _():
        def start(left_ref, right_ref):
            cols = pl.ds(0, EDGE)
            for x in range(2):
                for z in range(ZS):
                    cut = pl.ds((z * 2 + x) * count, count)
                    pltpu.make_async_copy(left_ref.at[t, x, z, :, cols], w_ref.at[0, cut], sem).start()
                    pltpu.make_async_copy(right_ref.at[x, t, z, :, cols], w_ref.at[1, cut], sem).start()

        @pl.when(side_ref[0] == 0)
        def _():
            start(mine_ref, other_ref)

        @pl.when(side_ref[0] != 0)
        def _():
            start(other_ref, mine_ref)

        pltpu.make_async_copy(w_ref, w_ref, sem).wait()

    for side in range(2):
        size = min(EDGE, wide - side * EDGE)
        gt_ref[side * EDGE : side * EDGE + size] = flip(low(dot_nn(g_ref[...], w_ref[side, :, :size])))
    left, right = pa_ref[0], pb_ref[0]
    found = {}
    blank = jnp.zeros((HDIM, SEQ), jnp.bfloat16)
    for p in range(pairs):
        queries = by_head(pair_cols(left, right, p))
        keys_flat = flip(pair_cols(left, right, pairs + p))
        value_rows = pair_cols(left, right, 2 * pairs + p)
        flat = flat_ref[0, 0, p * LANES : (p + 1) * LANES, :].astype(jnp.float32)
        scaled, centre = [], []
        for half in range(2):
            rows = slice(half * HDIM, (half + 1) * HDIM)
            grads = gt_ref[p * LANES + half * HDIM : p * LANES + (half + 1) * HDIM, :].astype(jnp.float32)
            scaled.append(low(grads * inv_ref[0, p : p + 1, half * SEQ : (half + 1) * SEQ]))
            centre.append(jnp.sum(scaled[half].astype(jnp.float32) * flat[rows], axis=0, keepdims=True))
        grads = jnp.concatenate(
            [jnp.concatenate([scaled[0], blank], axis=0), jnp.concatenate([blank, scaled[1]], axis=0)], axis=1
        )
        weights = e_ref[0, p]
        grad_weights = dot_nn(value_rows, grads) - jnp.concatenate(centre, axis=1)
        grad_scores = low(weights.astype(jnp.float32) * grad_weights)
        found[p] = flip(low(own_heads(dot_nn(keys_flat, grad_scores)) * HDIM**-0.5))
        found[pairs + p] = low(dot_nn(grad_scores, queries) * HDIM**-0.5)
        found[2 * pairs + p] = low(dot_nn(weights, flip(grads)))
    found[3 * pairs] = jnp.zeros((SEQ, LANES), jnp.bfloat16)
    count = (3 * pairs + 1) // 2
    for at in range(count):
        cut = slice(at * LANES, (at + 1) * LANES)
        dm_ref[:, cut] = jnp.where(side_ref[0] == 0, found[at], found[at + count])
        do_ref[:, cut] = jnp.where(side_ref[0] == 0, found[at + count], found[at])


def attend_back(grad_branch, weights, kept, t):
    pa, pb, e, _, flat, inv = kept
    rows, width = grad_branch.shape
    seqs = rows // SEQ
    cols, used = pa.shape[2], pb.shape[2]
    wide = flat.shape[2]
    bf = jnp.bfloat16
    return pl.pallas_call(
        functools.partial(attend_back_kernel, t),
        grid=(seqs,),
        in_specs=set_specs() + [
            pl.BlockSpec((SEQ, width), lambda s: (s, 0)),
            pl.BlockSpec((1, SEQ, cols), lambda s: (0, s, 0)),
            pl.BlockSpec((1, SEQ, used), lambda s: (0, s, 0)),
            pl.BlockSpec((1,) + e.shape[1:], lambda s: (s, 0, 0, 0)),
            pl.BlockSpec((1, 1, wide, SEQ), lambda s: (0, s, 0, 0)),
            pl.BlockSpec((1,) + inv.shape[1:], lambda s: (s, 0, 0)),
        ],
        out_specs=[pl.BlockSpec((SEQ, cols), lambda s: (s, 0))] * 2,
        out_shape=[jax.ShapeDtypeStruct((rows, cols), bf)] * 2,
        scratch_shapes=[
            pltpu.VMEM((2, width, EDGE), bf),
            pltpu.VMEM((wide, SEQ), bf),
            pltpu.SemaphoreType.DMA,
        ],
        compiler_params=params(),
        cost_estimate=SMALL,
        name="attend_back",
    )(*set_args(weights), grad_branch, pa, pb, e, flat, inv)


def gelu_parts(v):
    below = 0.5 + 0.5 * lax.erf(v * 0.5**0.5)
    bell = jnp.exp(-0.5 * (v * v))
    return v * below, below + (0.3989422804014327 * v) * bell


def row_norm(value):
    centered = value - jnp.mean(value, axis=-1, keepdims=True)
    inverse = lax.rsqrt(jnp.mean(centered * centered, axis=-1, keepdims=True) + epsilon)
    return centered * inverse, inverse


def row_norm_back(grad_scaled, scaled, inverse):
    centered = grad_scaled - jnp.mean(grad_scaled, axis=-1, keepdims=True)
    return inverse * (centered - scaled * jnp.mean(grad_scaled * scaled, axis=-1, keepdims=True))


def widen_kernel(
    side_ref, mine_ref, other_ref, x_ref, u_ref, v_ref, n_ref,
    sum_ref, tok_ref, low_ref, hm_ref, ho_ref, sm_ref, so_ref, mine, other, sems,
):
    @pl.when(pl.program_id(0) == 0)
    def _():
        load_halves(side_ref, mine_ref, other_ref, mine, other, sems)
        wait_set(mine, other, sems)

    tok_ref[...] = flip(x_ref[...])
    total = x_ref[...].astype(jnp.float32)
    for t, ref in enumerate((u_ref, v_ref)):
        near = jnp.where(side_ref[0] == 0, ref[0], ref[1])
        away = jnp.where(side_ref[0] == 0, ref[1], ref[0])
        total = total + dot_nt(near, mine[t, :, :EDGE]) + dot_nt(away, other[t, :, :EDGE])
    sum_ref[...] = total
    scaled, _ = row_norm(total)
    x = low(scaled * n_ref[0:1, :] + n_ref[1:2, :])
    low_ref[...] = flip(x)
    half = mine.shape[2] - EDGE
    for t in range(2):
        for ref, hid_ref, slope_ref in ((mine, hm_ref, sm_ref), (other, ho_ref, so_ref)):
            for start in range(0, half, CHUNK):
                cut = slice(t * half + start, t * half + start + CHUNK)
                value, slope = gelu_parts(dot_nn(x, ref[t, :, EDGE + start : EDGE + start + CHUNK]))
                hid_ref[:, cut] = low(value)
                slope_ref[:, cut] = low(slope)


def widen(tokens, attended, weights, norms):
    rows, width = tokens.shape
    span = 2 * (weights[0].shape[4] - EDGE)
    bf = jnp.bfloat16
    by_row = lambda n: pl.BlockSpec((BLOCK, n), lambda r: (r, 0))
    full = lambda a: pl.BlockSpec(a.shape, lambda r: (0, 0))
    side = pl.BlockSpec((2, BLOCK, EDGE), lambda r: (0, r, 0))
    return pl.pallas_call(
        widen_kernel,
        grid=(rows // BLOCK,),
        in_specs=set_specs() + [by_row(width), side, side, full(norms)],
        out_specs=[by_row(width)] + [pl.BlockSpec((width, BLOCK), lambda r: (0, r))] * 2 + [by_row(span)] * 4,
        out_shape=[
            jax.ShapeDtypeStruct((rows, width), jnp.float32),
            jax.ShapeDtypeStruct((width, rows), bf),
            jax.ShapeDtypeStruct((width, rows), bf),
        ] + [jax.ShapeDtypeStruct((rows, span), bf)] * 4,
        scratch_shapes=set_scratch(weights),
        compiler_params=params(),
        cost_estimate=SMALL,
        name="widen",
    )(*set_args(weights), tokens, *attended, norms)


def middle_kernel(
    side_ref, mine_ref, other_ref, side_two_ref, mine_two_ref, other_two_ref,
    sum_ref, hm_ref, ho_ref, sm_ref, so_ref, n_ref, cot_ref,
    out_ref, gs_ref, gm_ref, go_ref, res_ref, gb_ref, gbt_ref, flat_ref,
    mine, other, sems, win_mine, win_other, win_sems, stat_ref,
):
    @pl.when(pl.program_id(0) == 0)
    def _():
        load_halves(side_ref, mine_ref, other_ref, mine, other, sems)
        load_halves(side_two_ref, mine_two_ref, other_two_ref, win_mine, win_other, win_sems)
        wait_set(mine, other, sems)

    gain_one, shift_one = n_ref[0:1, :], n_ref[1:2, :]
    gain_two, shift_two = n_ref[2:3, :], n_ref[3:4, :]
    scaled_one, inverse_one = row_norm(sum_ref[...])
    value = scaled_one * gain_one + shift_one
    half = mine.shape[2]
    for t in range(2):
        for ref, hid_ref in ((mine, hm_ref), (other, ho_ref)):
            value = value + dot_nt(hid_ref[:, t * half : (t + 1) * half], ref[t])
    scaled_two, inverse_two = row_norm(value)
    out_ref[...] = low(scaled_two * gain_two + shift_two)
    cotangent = cot_ref[...].astype(jnp.float32)
    grad_two = row_norm_back(cotangent * gain_two, scaled_two, inverse_two)
    grad_second = low(grad_two)
    gs_ref[...] = flip(grad_second)
    for t in range(2):
        for ref, slope_ref, gi_ref in ((mine, sm_ref, gm_ref), (other, so_ref, go_ref)):
            for start in range(0, half, CHUNK):
                cut = slice(t * half + start, t * half + start + CHUNK)
                grad_hidden = dot_nn(grad_second, ref[t, :, start : start + CHUNK])
                gi_ref[:, cut] = low(grad_hidden * slope_ref[:, cut].astype(jnp.float32))

    @pl.when(pl.program_id(0) == 0)
    def _():
        wait_set(win_mine, win_other, win_sems)
        stat_ref[...] = jnp.zeros_like(stat_ref)

    grad_first = grad_two
    for t in range(2):
        for ref, gi_ref in ((win_mine, gm_ref), (win_other, go_ref)):
            grad_first = grad_first + dot_nt(gi_ref[:, t * half : (t + 1) * half], ref[t, :, EDGE:])
    grad_one = row_norm_back(grad_first * gain_one, scaled_one, inverse_one)
    res_ref[...] = grad_one
    gb_ref[...] = low(grad_one)
    gbt_ref[...] = flip(low(grad_one))
    for row, value in enumerate((grad_first * scaled_one, grad_first, cotangent * scaled_two, cotangent)):
        stat_ref[row : row + 1, :] += jnp.sum(value, axis=0, keepdims=True)

    @pl.when(pl.program_id(0) == pl.num_programs(0) - 1)
    def _():
        flat_ref[...] = flip(stat_ref[...])


def middle(total, hidden, slope, weights_down, weights_in, norms, cotangent):
    rows, width = total.shape
    span = hidden[0].shape[1]
    bf = jnp.bfloat16
    by_row = lambda n: pl.BlockSpec((BLOCK, n), lambda r: (r, 0))
    by_col = pl.BlockSpec((width, BLOCK), lambda r: (0, r))
    full = lambda a: pl.BlockSpec(a.shape, lambda r: (0, 0))
    return pl.pallas_call(
        middle_kernel,
        grid=(rows // BLOCK,),
        in_specs=set_specs() * 2 + [by_row(width)] + [by_row(span)] * 4 + [full(norms), by_row(width)],
        out_specs=[
            by_row(width), by_col, by_row(span), by_row(span), by_row(width), by_row(width), by_col,
            pl.BlockSpec((width, LANES), lambda r: (0, 0)),
        ],
        out_shape=[
            jax.ShapeDtypeStruct((rows, width), bf),
            jax.ShapeDtypeStruct((width, rows), bf),
            jax.ShapeDtypeStruct((rows, span), bf),
            jax.ShapeDtypeStruct((rows, span), bf),
            jax.ShapeDtypeStruct((rows, width), jnp.float32),
            jax.ShapeDtypeStruct((rows, width), bf),
            jax.ShapeDtypeStruct((width, rows), bf),
            jax.ShapeDtypeStruct((width, LANES), jnp.float32),
        ],
        scratch_shapes=set_scratch(weights_down) + set_scratch(weights_in) + [pltpu.VMEM((LANES, width), jnp.float32)],
        compiler_params=params(),
        cost_estimate=SMALL,
        name="middle",
    )(*set_args(weights_down), *set_args(weights_in), total, *hidden, *slope, norms, cotangent)


def store_rows(place_ref, t, refs, value, cut):
    stay_ref, away_ref = refs
    count = stay_ref.shape[2]
    for x in range(2):
        a = jnp.where(place_ref[0] == 0, t, x)
        b = jnp.where(place_ref[0] == 0, x, t)
        for z in range(ZS):
            start = (z * 2 + x) * count
            piece = low(value[start : start + count])

            @pl.when(a == place_ref[1])
            def _():
                stay_ref[b, z, :, cut] = piece

            @pl.when(a != place_ref[1])
            def _():
                away_ref[b, z, :, cut] = piece


def weigh_kernel(jobs, place_ref, stats_ref, stats_got_ref, *refs):
    refs = list(refs)
    sources = [refs.pop(0) for _ in range(6 * len(jobs))]
    outs = refs.pop(0), refs.pop(0)
    *buffers, sems = refs
    copies = []
    for j, (views, start, size) in enumerate(jobs):
        flat_buf, value_buf = buffers[2 * j], buffers[2 * j + 1]
        rows = flat_buf.shape[1] // 2
        low_part, high_part = pl.ds(0, rows), pl.ds(rows, rows)
        targets = [
            flat_buf.at[:, low_part], flat_buf.at[:, high_part],
            value_buf.at[0, low_part], value_buf.at[0, high_part],
            value_buf.at[1, low_part], value_buf.at[1, high_part],
        ]
        copies.append([
            pltpu.make_async_copy(view(source, place_ref), target, sems.at[6 * j + i])
            for i, (view, source, target) in enumerate(zip(views, sources[6 * j : 6 * j + 6], targets))
        ])
    for group in copies:
        for copy in group:
            copy.start()
    for j, (_, start, size) in enumerate(jobs):
        flat_buf, value_buf = buffers[2 * j], buffers[2 * j + 1]
        for t in range(2):
            for copy in copies[j][2 + 2 * t : 4 + 2 * t] + (copies[j][:2] if t == 0 else []):
                copy.wait()
            value = dot_nn(flat_buf[...], value_buf[t])
            if stats_ref.shape[0] == value.shape[0]:
                edge = size - LANES
                store_rows(place_ref, t, outs, value[:, :edge], slice(start, start + edge))
                value = jnp.where(place_ref[0] == 0, value[:, edge:], stats_ref[...] + stats_got_ref[...])
                store_rows(place_ref, t, outs, value, slice(start + edge, start + size))
            else:
                store_rows(place_ref, t, outs, value, slice(start, start + size))


def weigh_call(place, stats, stats_got, *jobs):
    width, rows = jobs[0][0][0].shape
    cols = sum(job[2] for job in jobs)
    shape = (2, ZS, width // (2 * ZS), cols)
    bf = jnp.bfloat16
    arrays, plan, scratch, start = [], [], [], 0
    for values, views, size in jobs:
        arrays += values
        plan.append((views, start, size))
        scratch += [pltpu.VMEM((width, 2 * rows), bf), pltpu.VMEM((2, 2 * rows, size), bf)]
        start += size
    return pl.pallas_call(
        functools.partial(weigh_kernel, plan),
        in_specs=[pl.BlockSpec(memory_space=pltpu.SMEM)] + [pl.BlockSpec(memory_space=pltpu.VMEM)] * 2
        + [pl.BlockSpec(memory_space=pl.ANY)] * len(arrays),
        out_specs=[pl.BlockSpec(memory_space=pltpu.VMEM)] * 2,
        out_shape=[jax.ShapeDtypeStruct(shape, bf)] * 2,
        scratch_shapes=scratch + [pltpu.SemaphoreType.DMA((len(arrays),))],
        compiler_params=params(),
        cost_estimate=SMALL,
        name="weigh",
    )(place, stats, stats_got, *arrays)


def whole(ref, place_ref):
    return ref


def half_of(t, size):
    return lambda ref, place_ref: ref.at[:, pl.ds(t * size, size)]


def halved(flat, value, flat_got, value_got):
    size = value.shape[1] // 2
    views = [whole, whole, half_of(0, size), half_of(0, size), half_of(1, size), half_of(1, size)]
    return [flat, flat_got, value, value_got, value, value_got], views, size


def weigh(place, *args):
    none = jnp.zeros((8, LANES), jnp.float32)
    return weigh_call(place, none, none, halved(*args))


def weigh_more(place, flat, value, flat_got, value_got, flat_two, u, v, flat_two_got, u_got, v_got):
    own = lambda ref, place_ref: ref.at[place_ref[0]]
    views = [whole, whole, own, whole, own, whole]
    none = jnp.zeros((8, LANES), jnp.float32)
    return weigh_call(
        place, none, none,
        ([flat_two, flat_two_got, u, u_got, v, v_got], views, EDGE),
        halved(flat, value, flat_got, value_got),
    )


def weigh_last(place, flat, u, v, flat_got, u_got, v_got, stats, stats_got):
    return weigh_call(place, stats, stats_got, ([flat, flat_got, u, u_got, v, v_got], [whole] * 6, u.shape[1]))


def input_kernel(side_ref, mine_ref, other_ref, res_ref, um_ref, uo_ref, vm_ref, vo_ref, out_ref, mine, other, sems):
    @pl.when(pl.program_id(0) == 0)
    def _():
        load_halves(side_ref, mine_ref, other_ref, mine, other, sems)
        wait_set(mine, other, sems)

    total = res_ref[...]
    for t, (near, away) in enumerate(((um_ref, uo_ref), (vm_ref, vo_ref))):
        total = total + dot_nt(near[...], mine[t]) + dot_nt(away[...], other[t])
    out_ref[...] = low(total)


def input_back(resid, parts, weights):
    rows, width = resid.shape
    by_row = lambda n: pl.BlockSpec((BLOCK, n), lambda r: (r, 0))
    return pl.pallas_call(
        input_kernel,
        grid=(rows // BLOCK,),
        in_specs=set_specs() + [by_row(width)] + [by_row(parts[0][0].shape[1])] * 4,
        out_specs=by_row(width),
        out_shape=jax.ShapeDtypeStruct((rows, width), jnp.bfloat16),
        scratch_shapes=set_scratch(weights),
        compiler_params=params(),
        cost_estimate=SMALL,
        name="input_back",
    )(*set_args(weights), resid, *parts[0], *parts[1])


def halves(value):
    return jnp.split(value, 2, axis=-1)


def shards(
    tokens,
    segment,
    weight_qkv,
    weight_out,
    weight_in,
    weight_down,
    gain_one,
    shift_one,
    gain_two,
    shift_two,
    cotangent,
):
    rows, width = tokens.shape
    own = weight_qkv.shape[1]
    wide = weight_out.shape[0]
    half_span = weight_in.shape[1]
    bf = jnp.bfloat16

    norms = jnp.stack([gain_one, shift_one, gain_two, shift_two], axis=1)
    norms = jnp.pad(norms, ((0, 0), (0, LANES - 4)))
    set_one = jnp.concatenate([jnp.transpose(weight_qkv, (1, 0, 2)).reshape(own, -1), norms], axis=1)
    one = Flow(gather_steps(*halves(set_one)))
    one.go(2)
    weight_out, weight_in, weight_down, tokens, segment = sync(
        one, weight_out, weight_in, weight_down, tokens, segment
    )
    one.go()
    out_flat, half = weight_out.T, half_span // 2
    out_flat = jnp.pad(out_flat, ((0, 0), (0, 2 * EDGE - wide)))
    two = Flow(gather_steps(*[
        jnp.concatenate([o, w], axis=1) for o, w in zip(halves(out_flat), halves(weight_in))
    ]))
    three = Flow(gather_steps(*halves(weight_down.T)))
    two.go(2)
    three.go(2)
    numbers = lax.dynamic_slice_in_dim(segment, lax.axis_index("tensor") * rows, rows)
    numbers = numbers.reshape(-1, 1, SEQ), jnp.broadcast_to(numbers[:, None], (rows, LANES)).reshape(-1, SEQ, LANES)
    tokens, numbers = sync(one, two, three, tokens, numbers)
    one.go()
    sync(one, two)
    one.go()
    two.go()
    two.value = hold(two.value, one)
    one.go()
    one.go()
    sync(one, two)
    one.go()
    two.go()
    sync(one, two, three)
    one.go()
    two.go()
    tokens = sync(one, tokens)
    weights_one = one.go()
    kept = [attend(tokens, weights_one, numbers, 0, 0), None]
    tokens, kept[0] = sync(two, three, tokens, kept[0])
    two.go()
    tokens = sync(two, tokens)
    two.go()
    three.go()
    kept[0] = attend(tokens, weights_one, numbers, 0, 1, kept[0])
    tokens, kept[0] = sync(tokens, kept[0])
    kept[1] = attend(tokens, weights_one, numbers, 1, 0)
    tokens, kept[1] = sync(two, three, tokens, kept[1])
    two.go()
    three.go()
    tokens, kept[1] = sync(two, three, tokens, kept[1])
    two.go()
    three.go()
    first_mine, first_other, first_side = weights_one
    norms = jnp.where(first_side[0] == 0, first_other, first_mine)[:, 0, :, :, first_mine.shape[4] - LANES :]
    norms = jnp.transpose(norms, (1, 0, 2, 3)).reshape(width, LANES)[:, :8].T.astype(jnp.float32)
    kept[1] = attend(tokens, weights_one, numbers, 1, 1, kept[1])
    tokens, kept[1], norms = sync(two, three, tokens, kept[1], norms)
    three.go()
    tokens = sync(three, tokens)
    three.go()
    weights_two = two.go()
    attended = [kept[t][3] for t in range(2)]
    attended_got = [exchange(lax.dynamic_index_in_dim(value, 1 - core_side(), 0, keepdims=False)) for value in attended]
    total, tokens_flat, low_flat, *wide_out = widen(tokens, attended, weights_two, norms)
    hidden, slope = wide_out[:2], wide_out[2:]
    total, tokens_flat, low_flat, hidden, attended_got = sync(
        three, total, tokens_flat, low_flat, hidden, attended_got
    )
    three.go(2)
    weights_three = three.go()
    weights_three, away, low_flat, tokens_flat = sync(weights_three, hidden[1], low_flat, tokens_flat)
    hidden_got, low_got, tokens_got = exchange(away), exchange(low_flat), exchange(tokens_flat)
    output, second_flat, inner_mine, inner_other, grad_resid_one, grad_branch, branch_flat, stats = middle(
        total, hidden, slope, weights_three, weights_two, norms, cotangent
    )
    second_flat, hidden_got, low_got, tokens_got, inner_other, branch_flat, stats = sync(
        second_flat, hidden_got, low_got, tokens_got, inner_other, branch_flat, stats
    )
    second_got = exchange(second_flat)
    second_got, inner_other, branch_flat, stats = sync(second_got, inner_other, branch_flat, stats)
    inner_got, branch_got, stats_got = exchange(inner_other), exchange(branch_flat), exchange(stats)
    three = Flow(scatter_steps(lambda own: weigh(
        place_of(own), second_flat, hidden[0 if own else 1], second_got, hidden_got
    )))
    inner_mine, inner_got, branch_got, stats_got = sync(three, inner_mine, inner_got, branch_got, stats_got)
    three.go()
    two = Flow(scatter_steps(lambda own: weigh_more(
        place_of(own), low_flat, inner_mine if own else inner_other, low_got, inner_got,
        branch_flat, *attended, branch_got, *attended_got,
    )))
    grad_branch = sync(two, grad_branch)
    two.go()
    parts = [attend_back(grad_branch, weights_two, kept[0], 0)]
    parts[0] = sync(three, parts[0])
    three.go()
    grad_branch, kept[1], parts[0] = sync(three, grad_branch, kept[1], parts[0])
    three.go()
    parts_got = [exchange(parts[0][1])]
    parts.append(attend_back(grad_branch, weights_two, kept[1], 1))
    parts, parts_got = sync(two, three, parts, parts_got)
    parts_got.append(exchange(parts[1][1]))
    two.go()
    three.go()
    parts, parts_got = sync(two, three, parts, parts_got)
    two.go()
    three.go()
    one = Flow(scatter_steps(lambda own: weigh_last(
        place_of(own), tokens_flat, *[value[0 if own else 1] for value in parts], tokens_got, *parts_got, stats, stats_got
    )))
    grad_resid_one = sync(one, two, three, grad_resid_one)
    one.go()
    two.go()
    two.go()
    three.go(2)
    input_grad = input_back(grad_resid_one, parts, weights_one)
    if isinstance(two.value, list):
        first, second, third = two.value
        input_grad, first, third = sync(one, input_grad, first, third)
        two.value = [first, second, third]
    one.go()
    one.go()
    two.go(2)
    sync(one, two)
    one.go()
    one.go()
    one.go(2)
    sum_one = jnp.concatenate(one.go(), axis=1)
    two_left, two_right = two.go()
    sum_three = jnp.concatenate(three.go(), axis=1)
    stats = sum_one[:, 3 * wide : 3 * wide + 4].T
    sum_out = jnp.concatenate([two_left[:, :EDGE], two_right[:, :EDGE]], axis=1)[:, :wide]
    return (
        output,
        input_grad,
        jnp.transpose(sum_one[:, : 3 * wide].reshape(own, 3, -1), (1, 0, 2)),
        sum_out.T,
        jnp.concatenate([two_left[:, EDGE:], two_right[:, EDGE:]], axis=1),
        sum_three.T,
        stats[0],
        stats[1],
        stats[2],
        stats[3],
    )


def solution(mesh):
    both = P(("dp", "tensor"), None)
    split = P("dp")
    qkv_spec = P(None, "dp", "tensor")
    row_spec = P("tensor", "dp")
    in_spec = P("dp", "tensor")
    return jax.shard_map(
        shards,
        mesh=mesh,
        in_specs=(both, split, qkv_spec, row_spec, in_spec, row_spec, split, split, split, split, both),
        out_specs=(both, both, qkv_spec, row_spec, in_spec, row_spec, split, split, split, split),
        check_vma=False,
    )
```
